128 devices in a mesh: seq: 8 (over z_lo, x), tp: 16 (over y, z_hi, core).
Axes of the slice: x: 4, y: 4, z: 4 (z_hi: 2, z_lo: 2; z = z_hi * 2 + z_lo), core: 2. Of those that a mesh axis runs over, the one named last changes fastest.
Arguments:
- tokens: bfloat16 [8192, 6144], P(('seq', 'tp')), may hold values from -6 to 6
- w_x: bfloat16 [6144, 8192], P(None, 'tp'), may hold values from -0.078125 to 0.078125
- w_z: bfloat16 [6144, 8192], P(None, 'tp'), may hold values from -0.078125 to 0.078125
- w_bc: bfloat16 [6144, 1024], P(None, 'tp'), may hold values from -0.078125 to 0.078125
- w_dt: bfloat16 [6144, 128], P(None, 'tp'), may hold values from -0.078125 to 0.078125
- conv_x: bfloat16 [4, 8192], P(None, 'tp'), may hold values from -3 to 3
- conv_bc: bfloat16 [4, 1024], P(None, 'tp'), may hold values from -3 to 3
- dt_bias: float32 [128], P('tp'), may hold values from -1.5 to 0.5
- decay_rate: float32 [128], P('tp'), may hold values from 6.1035156e-05 to 0.08
- skip: float32 [128], P('tp'), may hold values from 0 to 2.5
- norm_gain: bfloat16 [8192], P('tp'), may hold values from 0.5 to 1.5
- w_out: bfloat16 [8192, 6144], P('tp'), may hold values from -0.0625 to 0.0625
Outputs:
- mixed: bfloat16 [8192, 6144], P(('seq', 'tp'))
The draws below stay inside these ranges and needn't reach their ends.
All inputs are finite; a program needn't handle non-finite values.
Results may differ from the reference program's by a relative error of at most 0.023.
Values may be sent and summed in bfloat16 or wider, within the bound.
A program may use at most 128 MiB of HBM per device.

```python
import math
import jax
import jax.numpy as jnp
from jax import lax

D = 6144
HEADS = 128
HEAD_DIM = 64
STATE = 128
GROUPS = 4
KCONV = 4
BLOCK = 256
DINNER = 8192
TOKENS = 8192
N_TP = 16


def levels(rng, extent, cuts, smallest, top_value):
    level, own = 1.0, jax.random.fold_in(rng, 6)
    for dim, parts in cuts:
        heights = jnp.exp(jax.random.uniform(jax.random.fold_in(own, dim), (parts,), jnp.float32, smallest / len(cuts), top_value / len(cuts)))
        level = level * jnp.repeat(heights, extent[dim] // parts).reshape([-1 if axis == dim else 1 for axis in range(len(extent))])
    return level


def noise(key, dims, scale, most, cuts=(), kind=jnp.bfloat16):
    drawn = scale * jax.random.normal(key, dims, jnp.float32)
    if cuts:
        drawn = drawn * levels(key, dims, cuts, -0.22, 0.18)
    return jnp.clip(drawn, -most, most).astype(kind)


def setup_inputs(seed: int = 0) -> dict:
    key_of = jax.random.split(jax.random.key(seed), 13)
    return {
        "tokens": noise(key_of[0], (TOKENS, D), 1.0, 6.0, ((0, 128),)),
        "w_x": noise(key_of[1], (D, DINNER), D ** -0.5, 0.078125, ((1, 16),)),
        "w_z": noise(key_of[2], (D, DINNER), D ** -0.5, 0.078125, ((1, 16),)),
        "w_bc": noise(key_of[3], (D, 2 * GROUPS * STATE), D ** -0.5, 0.078125, ((1, 16),)),
        "w_dt": noise(key_of[4], (D, HEADS), D ** -0.5, 0.078125, ((1, 16),)),
        "conv_x": noise(key_of[5], (KCONV, DINNER), KCONV ** -0.5, 3.0, ((1, 16),)),
        "conv_bc": noise(key_of[6], (KCONV, 2 * GROUPS * STATE), KCONV ** -0.5, 3.0, ((1, 16),)),
        "dt_bias": jnp.clip(-1.5 + 2.0 * jax.random.uniform(key_of[7], (HEADS,), jnp.float32) ** levels(key_of[7], (HEADS,), ((0, 16),), -0.2, 0.2), -1.5, 0.5),
        "decay_rate": jnp.clip(jnp.exp(math.log(0.08) - 7.178332 * jax.random.uniform(key_of[8], (HEADS,), jnp.float32) ** levels(key_of[8], (HEADS,), ((0, 16),), -0.2, 0.2)), 6.103515625e-05, 0.08),
        "skip": jnp.clip(2.5 * jax.random.uniform(key_of[9], (HEADS,), jnp.float32) ** levels(key_of[9], (HEADS,), ((0, 16),), -0.2, 0.2), 0.0, 2.5),
        "norm_gain": jnp.clip(1.0 + 0.1 * jax.random.normal(key_of[10], (DINNER,), jnp.float32), 0.5, 1.5).astype(jnp.bfloat16),
        "w_out": noise(key_of[11], (DINNER, D), DINNER ** -0.5, 0.0625, ((0, 16),)),
    }


HIGH = lax.Precision.HIGHEST

def causal_conv(values, taps):
    width = taps.shape[0]
    padded = jnp.concatenate([jnp.zeros((width - 1, values.shape[1]), values.dtype), values], axis=0)
    length = values.shape[0]
    acc = jnp.zeros((length, values.shape[1]), jnp.float32)
    for index_k in range(width):
        acc = acc + taps[index_k].astype(jnp.float32)[None, :] * padded[index_k:index_k + length].astype(jnp.float32)
    return jax.nn.silu(acc).astype(jnp.bfloat16)

def reference(tokens, w_x, w_z, w_bc, w_dt, conv_x, conv_bc, dt_bias, decay_rate, skip, norm_gain, w_out):
    length = tokens.shape[0]
    x_in = jnp.dot(tokens, w_x, preferred_element_type=jnp.float32).astype(jnp.bfloat16)
    z_gate = jnp.dot(tokens, w_z, preferred_element_type=jnp.float32).astype(jnp.bfloat16)
    bc_in = jnp.dot(tokens, w_bc, preferred_element_type=jnp.float32).astype(jnp.bfloat16)
    dt = jax.nn.softplus(jnp.dot(tokens, w_dt, preferred_element_type=jnp.float32) + dt_bias[None, :])
    x_conv = causal_conv(x_in, conv_x)
    bc_conv = causal_conv(bc_in, conv_bc)
    per_group = HEADS // GROUPS
    nblocks = length // BLOCK
    x_blocks = x_conv.astype(jnp.float32).reshape(nblocks, BLOCK, HEADS, HEAD_DIM)
    bc_split = bc_conv.astype(jnp.float32).reshape(nblocks, BLOCK, GROUPS, 2, STATE)
    b_blocks = bc_split[:, :, :, 0, :]
    c_blocks = bc_split[:, :, :, 1, :]
    dt_blocks = dt.reshape(nblocks, BLOCK, HEADS)
    causal = jnp.arange(BLOCK)[:, None] >= jnp.arange(BLOCK)[None, :]

    def one_block(state, pieces):
        x_blk, b_blk, c_blk, dt_blk = pieces
        accum = jnp.cumsum(dt_blk * decay_rate[None, :], axis=0)
        b_heads = jnp.repeat(b_blk, per_group, axis=1)
        c_heads = jnp.repeat(c_blk, per_group, axis=1)
        affinity = jnp.einsum('thn,shn->hts', c_heads, b_heads, precision=HIGH)
        expo = accum.T[:, :, None] - accum.T[:, None, :]
        decay = jnp.where(causal[None], jnp.exp(-jnp.where(causal[None], expo, 0.0)), 0.0)
        weights = affinity * decay * dt_blk.T[:, None, :]
        y_intra = jnp.einsum('hts,shp->thp', weights, x_blk, precision=HIGH)
        y_inter = jnp.exp(-accum)[:, :, None] * jnp.einsum('thn,hpn->thp', c_heads, state, precision=HIGH)
        y_blk = y_intra + y_inter + skip[None, :, None] * x_blk
        tail = jnp.exp(-(accum[-1][None, :] - accum)) * dt_blk
        contrib = jnp.einsum('shp,shn->hpn', x_blk * tail[:, :, None], b_heads, precision=HIGH)
        new_state = jnp.exp(-accum[-1])[:, None, None] * state + contrib
        return (new_state, y_blk)
    start_state = jnp.zeros((HEADS, HEAD_DIM, STATE), jnp.float32)
    final_state, y_all = lax.scan(one_block, start_state, (x_blocks, b_blocks, c_blocks, dt_blocks))
    y_flat = y_all.reshape(length, HEADS * HEAD_DIM)
    gated = y_flat * jax.nn.silu(z_gate.astype(jnp.float32))
    mean_sq = lax.optimization_barrier(jnp.mean(gated * gated, axis=1)) + 1e-05
    normed = (gated * lax.rsqrt(mean_sq)[:, None] * norm_gain.astype(jnp.float32)[None, :]).astype(jnp.bfloat16)
    slice_width = HEADS * HEAD_DIM // N_TP
    total = jnp.zeros((length, w_out.shape[1]), jnp.float32)
    for index_s in range(N_TP):
        part_prod = jnp.dot(normed[:, index_s * slice_width:(index_s + 1) * slice_width], w_out[index_s * slice_width:(index_s + 1) * slice_width], preferred_element_type=jnp.float32)
        rounded = lax.optimization_barrier(part_prod.astype(jnp.bfloat16))
        total = total + rounded.astype(jnp.float32)
    return total.astype(jnp.bfloat16)
```

```python
import functools

import jax
import jax.numpy as jnp
from jax import lax
from jax.experimental import pallas as pl
from jax.experimental.pallas import tpu as pltpu
from jax.sharding import PartitionSpec as P

HEAD_DIM = 64
STATE = 128
GROUPS = 4
BLOCK = 256
MESH = pl.DeviceIdType.MESH
F32 = jnp.float32
BF16 = jnp.bfloat16

D = 6144
ROWS = 64
SPAN = 1024
COLS = 512
SPLIT = 3584
HALF_P = SPLIT // 2
HALF_Q = 1280
WIDE = D + 128


def place():
    tp = lax.axis_index("tp")
    return lax.axis_index("seq"), tp // 4, tp // 2 % 2, tp % 2


def greet(peers):
    barrier = pltpu.get_barrier_semaphore()
    for peer in peers:
        pl.semaphore_signal(barrier, inc=1, device_id=peer, device_id_type=MESH)
    pl.semaphore_wait(barrier, len(peers))


def project_kernel(
    tok, wx, wz, wbc, wdt, x_out, z_out, small_out, buf, w, w_small, st_bc, st_dt, sends, recvs, locs
):
    s, y, h, c = place()
    up, down, far = (y + 1) % 4, (y + 3) % 4, (y + 2) % 4
    dev = lambda yy, hh, cc: (s, yy * 4 + hh * 2 + cc)
    dev_up, dev_down, dev_z, dev_sib = dev(up, h, c), dev(down, h, c), dev(y, 1 - h, c), dev(y, h, 1 - c)
    part_p, part_q = (0, SPLIT), (SPLIT, D - SPLIT)
    p_a, p_b = (0, HALF_P), (HALF_P, SPLIT - HALF_P)
    q_a, q_b = (SPLIT, HALF_Q), (SPLIT + HALF_Q, D - SPLIT - HALF_Q)
    whole = (0, D)

    def at(yy, hh, cc, cols):
        row = pl.multiple_of((yy * 4 + hh * 2 + cc) * ROWS, ROWS)
        return buf.at[pl.ds(row, ROWS), pl.ds(cols[0], cols[1])]

    started = []

    def send(k, yy, hh, cols, to, own=False):
        dst = at(yy, hh, c, cols)
        src = tok.at[:, pl.ds(cols[0], cols[1])] if own else dst
        copy = pltpu.make_async_remote_copy(
            src_ref=src, dst_ref=dst, send_sem=sends.at[k], recv_sem=recvs.at[k],
            device_id=to, device_id_type=MESH,
        )
        copy.start()
        started.append(copy)

    def arrive(k, yy, hh, cols, sib=False):
        ref = at(yy, hh, 1 - c if sib else c, cols)
        pltpu.make_async_remote_copy(
            src_ref=ref, dst_ref=ref, send_sem=sends.at[k], recv_sem=recvs.at[k],
            device_id=dev_sib, device_id_type=MESH,
        ).wait_recv()

    locals_ = [
        pltpu.make_async_copy(tok, at(y, h, c, whole), locs.at[0]),
        pltpu.make_async_copy(wbc, st_bc, locs.at[1]),
        pltpu.make_async_copy(wdt, st_dt, locs.at[2]),
        pltpu.make_async_copy(wx, w.at[:, pl.ds(0, COLS)], locs.at[3]),
        pltpu.make_async_copy(wz, w.at[:, pl.ds(COLS, COLS)], locs.at[4]),
    ]
    for copy in locals_:
        copy.start()
    greet([dev_up, dev_down, dev_z, dev_sib])
    send(0, y, h, part_p, dev_z, own=True)
    send(1, y, h, part_q, dev_up, own=True)
    send(2, y, h, part_q, dev_down, own=True)
    send(3, y, h, whole, dev_sib, own=True)
    send(4, y, h, part_q, dev_z, own=True)
    send(5, y, h, part_p, dev_up, own=True)
    send(6, y, h, part_p, dev_down, own=True)

    def project(yy, hh):
        row = pl.multiple_of((yy * 4 + hh * 2) * ROWS, 2 * ROWS)
        rows = pl.ds(row, 2 * ROWS)
        for out, base in ((x_out, 0), (z_out, COLS)):

            @pl.loop(0, COLS // 256)
            def _(j):
                col = pl.multiple_of(j * 256, 256)
                out[rows, pl.ds(col, 256)] = jnp.dot(
                    buf[rows, :], w[:, pl.ds(base + col, 256)], preferred_element_type=F32
                ).astype(BF16)

        small_out[rows, :] = jnp.dot(buf[rows, :], w_small[...], preferred_element_type=F32)

    locals_[1].wait()
    locals_[2].wait()
    w_small[...] = jnp.zeros_like(w_small)
    w_small[:, 0:64] = st_bc[...]
    w_small[:, 64:72] = st_dt[...]
    locals_[0].wait()
    locals_[3].wait()
    locals_[4].wait()
    arrive(3, y, h, whole, sib=True)
    project(y, h)
    arrive(1, down, h, part_q)
    send(7, down, h, q_a, dev_up)
    send(8, down, h, part_q, dev_z)
    send(9, down, h, part_q, dev_sib)
    arrive(2, up, h, part_q)
    send(10, up, h, q_b, dev_down)
    send(11, up, h, part_q, dev_z)
    send(12, up, h, part_q, dev_sib)
    arrive(0, y, 1 - h, part_p)
    send(13, y, 1 - h, part_p, dev_up)
    send(14, y, 1 - h, part_p, dev_down)
    send(15, y, 1 - h, part_p, dev_sib)
    arrive(7, far, h, q_a)
    send(17, far, h, q_a, dev_z)
    send(18, far, h, q_a, dev_sib)
    arrive(10, far, h, q_b)
    send(19, far, h, q_b, dev_z)
    send(20, far, h, q_b, dev_sib)
    arrive(4, y, 1 - h, part_q)
    send(16, y, 1 - h, part_q, dev_sib)
    arrive(5, down, h, part_p)
    send(21, down, h, p_a, dev_up)
    send(22, down, h, part_p, dev_sib)
    arrive(6, up, h, part_p)
    send(23, up, h, p_b, dev_down)
    send(24, up, h, part_p, dev_sib)
    arrive(15, y, 1 - h, part_p, sib=True)
    arrive(16, y, 1 - h, part_q, sib=True)
    project(y, 1 - h)
    arrive(9, down, h, part_q, sib=True)
    arrive(22, down, h, part_p, sib=True)
    project(down, h)
    arrive(13, down, 1 - h, part_p)
    send(27, down, 1 - h, p_a, dev_up)
    send(28, down, 1 - h, part_p, dev_sib)
    arrive(14, up, 1 - h, part_p)
    send(29, up, 1 - h, p_b, dev_down)
    send(30, up, 1 - h, part_p, dev_sib)
    arrive(12, up, h, part_q, sib=True)
    arrive(24, up, h, part_p, sib=True)
    project(up, h)
    arrive(8, down, 1 - h, part_q)
    send(25, down, 1 - h, part_q, dev_sib)
    arrive(11, up, 1 - h, part_q)
    send(26, up, 1 - h, part_q, dev_sib)
    arrive(25, down, 1 - h, part_q, sib=True)
    arrive(28, down, 1 - h, part_p, sib=True)
    project(down, 1 - h)
    arrive(21, far, h, p_a)
    send(33, far, h, p_a, dev_sib)
    arrive(23, far, h, p_b)
    send(34, far, h, p_b, dev_sib)
    arrive(26, up, 1 - h, part_q, sib=True)
    arrive(30, up, 1 - h, part_p, sib=True)
    project(up, 1 - h)
    arrive(17, far, 1 - h, q_a)
    send(31, far, 1 - h, q_a, dev_sib)
    arrive(19, far, 1 - h, q_b)
    send(32, far, 1 - h, q_b, dev_sib)
    arrive(18, far, h, q_a, sib=True)
    arrive(20, far, h, q_b, sib=True)
    arrive(33, far, h, p_a, sib=True)
    arrive(34, far, h, p_b, sib=True)
    project(far, h)
    arrive(27, far, 1 - h, p_a)
    send(35, far, 1 - h, p_a, dev_sib)
    arrive(29, far, 1 - h, p_b)
    send(36, far, 1 - h, p_b, dev_sib)
    arrive(31, far, 1 - h, q_a, sib=True)
    arrive(32, far, 1 - h, q_b, sib=True)
    arrive(35, far, 1 - h, p_a, sib=True)
    arrive(36, far, 1 - h, p_b, sib=True)
    project(far, 1 - h)
    for copy in started:
        copy.wait_send()


def gather_project(tokens, w_x, w_z, w_bc, w_dt):
    anywhere = pl.BlockSpec(memory_space=pl.ANY)
    vmem = pl.BlockSpec(memory_space=pltpu.VMEM)
    return pl.pallas_call(
        project_kernel,
        out_shape=(
            jax.ShapeDtypeStruct((SPAN, COLS), BF16),
            jax.ShapeDtypeStruct((SPAN, COLS), BF16),
            jax.ShapeDtypeStruct((SPAN, 128), F32),
        ),
        in_specs=[anywhere] * 5,
        out_specs=(vmem, vmem, vmem),
        scratch_shapes=[
            pltpu.VMEM((SPAN, D), BF16),
            pltpu.VMEM((D, 2 * COLS), BF16),
            pltpu.VMEM((D, 128), BF16),
            pltpu.VMEM((D, 64), BF16),
            pltpu.VMEM((D, 8), BF16),
            pltpu.SemaphoreType.DMA((37,)),
            pltpu.SemaphoreType.DMA((37,)),
            pltpu.SemaphoreType.DMA((5,)),
        ],
        compiler_params=pltpu.CompilerParams(
            collective_id=1, has_side_effects=True, vmem_limit_bytes=56 << 20
        ),
        name="gather_project",
    )(tokens, w_x, w_z, w_bc, w_dt)


def reduce_kernel(
    g, sq, w_out, out, o, sib, zq, pa, pb, qa, qb, pf, qf, zp, sends, recvs
):
    s, y, h, c = place()
    up, down, far = (y + 1) % 4, (y + 3) % 4, (y + 2) % 4
    dev = lambda yy, hh, cc: (s, yy * 4 + hh * 2 + cc)
    dev_up, dev_down, dev_z, dev_sib = dev(up, h, c), dev(down, h, c), dev(y, 1 - h, c), dev(y, h, 1 - c)
    wide_q = WIDE - SPLIT
    part_p, part_q = (0, SPLIT), (SPLIT, wide_q)
    p_a, p_b = (0, HALF_P), (HALF_P, SPLIT - HALF_P)
    q_a, q_b = (SPLIT, HALF_Q), (SPLIT + HALF_Q, wide_q - HALF_Q)
    started = []

    def at(yy, hh, cc, cols):
        row = pl.multiple_of((yy * 4 + hh * 2 + cc) * ROWS, ROWS)
        return o.at[pl.ds(row, ROWS), pl.ds(cols[0], cols[1])]

    def copy_of(k, src, dst, to):
        return pltpu.make_async_remote_copy(
            src_ref=src, dst_ref=dst, send_sem=sends.at[k], recv_sem=recvs.at[k],
            device_id=to, device_id_type=MESH,
        )

    def send(k, src, dst, to):
        copy = copy_of(k, src, dst, to)
        copy.start()
        started.append(copy)

    def arrive(k, ref):
        copy_of(k, ref, ref, dev_sib).wait_recv()

    def add(yy, hh, cols, ref):
        target = at(yy, hh, c, cols)

        @pl.loop(0, ROWS // 16)
        def _(i):
            rows = pl.ds(pl.multiple_of(i * 16, 16), 16)
            target[rows, :] = (target[rows, :].astype(F32) + ref[rows, :].astype(F32)).astype(BF16)

    def chip(yy, hh):
        return yy * 2 + hh

    def partial(yy, hh, k):
        row = pl.multiple_of((yy * 4 + hh * 2) * ROWS, 2 * ROWS)
        rows = pl.ds(row, 2 * ROWS)
        left = g[rows, :]

        @pl.loop(0, D // 512)
        def _(j):
            cols = pl.ds(pl.multiple_of(j * 512, 512), 512)
            o[rows, cols] = jnp.dot(left, w_out[:, cols], preferred_element_type=F32).astype(BF16)

        o[rows, pl.ds(D, 128)] = sq[rows, :]
        send(k, at(yy, hh, 1 - c, (0, WIDE)), sib.at[chip(yy, hh)], dev_sib)

    def joined(yy, hh, k):
        ref = sib.at[chip(yy, hh)]
        arrive(k, ref)
        add(yy, hh, (0, WIDE), ref)

    greet([dev_up, dev_down, dev_z, dev_sib])
    n = 1 - h
    partial(far, n, 0)
    partial(far, h, 1)
    joined(far, n, 0)
    send(8, at(far, n, c, p_a), pa.at[n], dev_up)
    send(9, at(far, n, c, p_b), pb.at[n], dev_down)
    send(10, at(far, n, c, part_q), zq.at[far], dev_z)
    partial(up, n, 2)
    joined(far, h, 1)
    send(11, at(far, h, c, p_a), pa.at[h], dev_up)
    send(12, at(far, h, c, p_b), pb.at[h], dev_down)
    partial(down, n, 3)
    joined(up, n, 2)
    send(13, at(up, n, c, part_q), zq.at[up], dev_z)
    partial(up, h, 4)
    joined(down, n, 3)
    send(14, at(down, n, c, part_q), zq.at[down], dev_z)
    arrive(8, pa.at[n])
    add(up, n, p_a, pa.at[n])
    send(15, at(up, n, c, part_p), pf.at[0, n], dev_up)
    arrive(9, pb.at[n])
    add(down, n, p_b, pb.at[n])
    send(16, at(down, n, c, part_p), pf.at[1, n], dev_down)
    partial(down, h, 5)
    joined(up, h, 4)
    arrive(11, pa.at[h])
    add(up, h, p_a, pa.at[h])
    send(17, at(up, h, c, part_p), pf.at[0, h], dev_up)
    partial(y, n, 6)
    joined(down, h, 5)
    arrive(12, pb.at[h])
    add(down, h, p_b, pb.at[h])
    send(18, at(down, h, c, part_p), pf.at[1, h], dev_down)
    joined(y, n, 6)
    send(19, at(y, n, c, part_q), zq.at[y], dev_z)
    partial(y, h, 7)
    arrive(10, zq.at[far])
    add(far, h, part_q, zq.at[far])
    send(20, at(far, h, c, q_a), qa, dev_up)
    send(21, at(far, h, c, q_b), qb, dev_down)
    joined(y, h, 7)
    arrive(13, zq.at[up])
    add(up, h, part_q, zq.at[up])
    arrive(20, qa)
    add(up, h, q_a, qa)
    send(22, at(up, h, c, part_q), qf.at[0], dev_up)
    arrive(14, zq.at[down])
    add(down, h, part_q, zq.at[down])
    arrive(21, qb)
    add(down, h, q_b, qb)
    send(23, at(down, h, c, part_q), qf.at[1], dev_down)
    arrive(15, pf.at[0, n])
    add(y, n, part_p, pf.at[0, n])
    arrive(16, pf.at[1, n])
    add(y, n, part_p, pf.at[1, n])
    send(24, at(y, n, c, part_p), zp, dev_z)
    arrive(17, pf.at[0, h])
    add(y, h, part_p, pf.at[0, h])
    arrive(18, pf.at[1, h])
    add(y, h, part_p, pf.at[1, h])
    arrive(19, zq.at[y])
    arrive(22, qf.at[0])
    arrive(23, qf.at[1])
    mine_q = at(y, h, c, part_q)
    mine_p = at(y, h, c, part_p)
    terms = (mine_q, zq.at[y], qf.at[0], qf.at[1])
    lane = pl.ds(D - SPLIT, 128)
    squares = sum(t[:, lane].astype(F32) for t in terms)
    scale = lax.rsqrt(squares / (COLS * 16) + 1e-05)

    @pl.loop(0, (D - SPLIT) // 128)
    def _(j):
        cols = pl.ds(pl.multiple_of(j * 128, 128), 128)
        total = sum(t[:, cols].astype(F32) for t in terms)
        out[:, pl.ds(pl.multiple_of(SPLIT + j * 128, 128), 128)] = (total * scale).astype(BF16)

    arrive(24, zp)

    @pl.loop(0, SPLIT // 128)
    def _(j):
        cols = pl.ds(pl.multiple_of(j * 128, 128), 128)
        total = mine_p[:, cols].astype(F32) + zp[:, cols].astype(F32)
        out[:, cols] = (total * scale).astype(BF16)

    for copy in started:
        copy.wait_send()


def project_reduce(g, sq, w_out):
    vmem = pl.BlockSpec(memory_space=pltpu.VMEM)
    wide_q = WIDE - SPLIT
    return pl.pallas_call(
        reduce_kernel,
        out_shape=jax.ShapeDtypeStruct((ROWS, D), BF16),
        in_specs=[vmem] * 3,
        out_specs=vmem,
        scratch_shapes=[
            pltpu.VMEM((SPAN, WIDE), BF16),
            pltpu.VMEM((8, ROWS, WIDE), BF16),
            pltpu.VMEM((4, ROWS, wide_q), BF16),
            pltpu.VMEM((2, ROWS, HALF_P), BF16),
            pltpu.VMEM((2, ROWS, SPLIT - HALF_P), BF16),
            pltpu.VMEM((ROWS, HALF_Q), BF16),
            pltpu.VMEM((ROWS, wide_q - HALF_Q), BF16),
            pltpu.VMEM((2, 2, ROWS, SPLIT), BF16),
            pltpu.VMEM((2, ROWS, wide_q), BF16),
            pltpu.VMEM((ROWS, SPLIT), BF16),
            pltpu.SemaphoreType.DMA((25,)),
            pltpu.SemaphoreType.DMA((25,)),
        ],
        compiler_params=pltpu.CompilerParams(
            collective_id=2, has_side_effects=True, vmem_limit_bytes=56 << 20
        ),
        name="project_reduce",
    )(g, sq, w_out)


def from_behind(value, axis, steps):
    count = lax.axis_size(axis)
    first, last = (max(0, -steps), min(count, count - steps))
    return lax.ppermute(value, axis, [(source, source + steps) for source in range(first, last)])


def from_partner(block, axis, stride):
    count = lax.axis_size(axis)
    route = []
    for low in range(count):
        high = low | 1 << stride
        if high != low and high < count:
            route += [(low, high), (high, low)]
    return lax.ppermute(block, axis, route)


def on_device(
    tokens, w_x, w_z, w_bc, w_dt, conv_x, conv_bc, dt_bias, decay_rate, skip, norm_gain, w_out
):
    col_x = w_x.shape[1]
    col_bc = w_bc.shape[1]
    heads_dev = w_dt.shape[1]
    taps = conv_x.shape[0]
    x_in, z_gate, small = gather_project(tokens, w_x, w_z, w_bc, w_dt)
    span_len = x_in.shape[0]
    bc_in = small[:, :col_bc].astype(jnp.bfloat16)
    dt_raw = small[:, col_bc : col_bc + heads_dev]
    conv_input = jnp.concatenate([x_in, bc_in], axis=1)
    rim_rows = from_behind(conv_input[span_len - (taps - 1) :], "seq", 1)
    padded = jnp.concatenate([rim_rows, conv_input], axis=0)
    all_taps = jnp.concatenate([conv_x, conv_bc], axis=1).astype(jnp.float32)
    conv_acc = jnp.zeros(conv_input.shape, jnp.float32)
    for index_k in range(taps):
        conv_acc = conv_acc + all_taps[index_k][None, :] * padded[
            index_k : index_k + span_len
        ].astype(jnp.float32)
    conv_out = jax.nn.silu(conv_acc).astype(jnp.bfloat16)
    x_conv = conv_out[:, :col_x]
    own_maps = conv_out[:, col_x:]
    levels = (lax.axis_size("tp") // GROUPS).bit_length() - 1
    held = own_maps
    for level in range(levels):
        partner = from_partner(held, "tp", level)
        upper = lax.axis_index("tp") // 2**level % 2
        held = jnp.where(
            upper == 1,
            jnp.concatenate([partner, held], axis=1),
            jnp.concatenate([held, partner], axis=1),
        )
    b_mat = held[:, :STATE]
    c_mat = held[:, STATE : 2 * STATE]
    dt = jax.nn.softplus(dt_raw + dt_bias[None, :])
    nblocks = span_len // BLOCK
    x_blocks = x_conv.astype(jnp.float32).reshape(nblocks, BLOCK, heads_dev, HEAD_DIM)
    b_blocks = b_mat.astype(jnp.float32).reshape(nblocks, BLOCK, STATE)
    c_blocks = c_mat.astype(jnp.float32).reshape(nblocks, BLOCK, STATE)
    dt_heads = jnp.transpose(dt.reshape(nblocks, BLOCK, heads_dev), (0, 2, 1))
    accum = jnp.cumsum(dt_heads * decay_rate[None, :, None], axis=2)
    causal = (jnp.arange(BLOCK)[:, None] >= jnp.arange(BLOCK)[None, :])[None, None, :, :]
    affinity = jnp.einsum("btn,bsn->bts", c_blocks, b_blocks, precision=lax.Precision.DEFAULT)
    expo = accum[:, :, :, None] - accum[:, :, None, :]
    decay = jnp.where(causal, jnp.exp(-jnp.where(causal, expo, 0.0)), 0.0)
    weights = affinity[:, None, :, :] * decay * dt_heads[:, :, None, :]
    y_intra = jnp.einsum("bhts,bshp->bthp", weights, x_blocks, precision=lax.Precision.DEFAULT)
    tail = jnp.exp(-(accum[:, :, -1:] - accum)) * dt_heads
    contrib = jnp.einsum("bshp,bhs,bsn->bhpn", x_blocks, tail, b_blocks, precision=lax.Precision.DEFAULT)
    block_decay = jnp.exp(-accum[:, :, -1])
    local_state = jnp.zeros((heads_dev, HEAD_DIM, STATE), jnp.float32)
    prefix_decay = jnp.ones((heads_dev,), jnp.float32)
    entry_local = []
    entry_decay = []
    for index_b in range(nblocks):
        entry_local.append(local_state)
        entry_decay.append(prefix_decay)
        local_state = block_decay[index_b][:, None, None] * local_state + contrib[index_b]
        prefix_decay = prefix_decay * block_decay[index_b]
    zero_state = jnp.zeros((heads_dev, HEAD_DIM, STATE), jnp.float32)

    def advance(count, incoming):
        return from_behind(
            (prefix_decay[:, None, None] * incoming + local_state).astype(jnp.bfloat16), "seq", 1
        ).astype(jnp.float32)

    state_in = lax.fori_loop(0, lax.axis_size("seq") - 1, advance, zero_state)
    entry_states = jnp.stack(
        [
            entry_decay[index_b][:, None, None] * state_in + entry_local[index_b]
            for index_b in range(nblocks)
        ],
        axis=0,
    )
    entry_scale = jnp.transpose(jnp.exp(-accum), (0, 2, 1))
    y_inter = entry_scale[..., None] * jnp.einsum(
        "btn,bhpn->bthp", c_blocks, entry_states, precision=lax.Precision.DEFAULT
    )
    y_all = y_intra + y_inter + skip[None, None, :, None] * x_blocks
    y_flat = y_all.reshape(span_len, col_x)
    gated = y_flat * jax.nn.silu(z_gate.astype(jnp.float32))
    squares = jnp.sum(gated * gated, axis=1, keepdims=True)
    scaled = (gated * norm_gain.astype(jnp.float32)[None, :]).astype(jnp.bfloat16)
    spread = jnp.broadcast_to(squares, (span_len, 128)).astype(jnp.bfloat16)
    return project_reduce(scaled, spread, w_out)


def solution(mesh):
    placed = (
        P(("seq", "tp"), None),
        P(None, "tp"),
        P(None, "tp"),
        P(None, "tp"),
        P(None, "tp"),
        P(None, "tp"),
        P(None, "tp"),
        P("tp"),
        P("tp"),
        P("tp"),
        P("tp"),
        P("tp", None),
    )
    return jax.shard_map(
        on_device, mesh=mesh, in_specs=placed, out_specs=P(("seq", "tp"), None), check_vma=False
    )
```

```python
import jax
import jax.numpy as jnp
from jax import lax
from jax.experimental import pallas as pl
from jax.experimental.pallas import tpu as pltpu
from jax.sharding import PartitionSpec as P

HEAD_DIM = 64
STATE = 128
BLOCK = 256
MESH = pl.DeviceIdType.MESH
F32 = jnp.float32
BF16 = jnp.bfloat16

D = 6144
ROWS = 64
SPAN = 1024
COLS = 512
SPLIT = 3584
HALF_P = SPLIT // 2
HALF_Q = 1280
WIDE = D + 128


def place():
    tp = lax.axis_index("tp")
    return lax.axis_index("seq"), tp // 4, tp // 2 % 2, tp % 2


def greet(peers):
    barrier = pltpu.get_barrier_semaphore()
    for peer in peers:
        pl.semaphore_signal(barrier, inc=1, device_id=peer, device_id_type=MESH)
    pl.semaphore_wait(barrier, len(peers))


def silu(v):
    return v / (1.0 + jnp.exp(-v))


def mixer_kernel(
    tok, wx, wz, wbc, wdt, cx, cbc, bias, rate, skip, gain, g_out, sq_out,
    buf, w, w_small, st_w, st_dt, xp, zs, small, bco, bcs, own, oth, maps, b_t, xc, dtx, xt,
    ea_x, yloc, cols, rows_a, a_x, spread, aff, entry, state, states, decays, t_out, t_in,
    sends, recvs, locs, sib_s, sib_r, z_s, z_r, halo_s, halo_r, line_s, line_r, t_s, t_r,
):
    s, y, h, c = place()
    up, down, far = (y + 1) % 4, (y + 3) % 4, (y + 2) % 4
    n = 1 - h
    line, x = s // 4, s % 4
    dev = lambda yy, hh, cc: (s, yy * 4 + hh * 2 + cc)
    span = lambda ss, hh: (ss, y * 4 + hh * 2 + c)
    dev_up, dev_down, dev_z, dev_sib = dev(up, h, c), dev(down, h, c), dev(y, n, c), dev(y, h, 1 - c)
    dev_zsib = dev(y, n, 1 - c)
    later, before = (s + 1) % 8, (s + 7) % 8
    on_line = [span(line * 4 + (x + d) % 4, h) for d in (1, 2, 3)]
    across = span((1 - line) * 4 + x, h)
    part_p, part_q = (0, SPLIT), (SPLIT, D - SPLIT)
    p_a, p_b = (0, HALF_P), (HALF_P, SPLIT - HALF_P)
    q_a, q_b = (SPLIT, HALF_Q), (SPLIT + HALF_Q, D - SPLIT - HALF_Q)
    whole = (0, D)

    def at(yy, hh, cc, cols_):
        row = pl.multiple_of((yy * 4 + hh * 2 + cc) * ROWS, ROWS)
        return buf.at[pl.ds(row, ROWS), pl.ds(cols_[0], cols_[1])]

    started = []

    def remote(src, dst, send_sem, recv_sem, to):
        return pltpu.make_async_remote_copy(
            src_ref=src, dst_ref=dst, send_sem=send_sem, recv_sem=recv_sem,
            device_id=to, device_id_type=MESH,
        )

    def push(src, dst, send_sem, recv_sem, to):
        copy = remote(src, dst, send_sem, recv_sem, to)
        copy.start()
        started.append(copy)

    def landed(ref, send_sem, recv_sem):
        remote(ref, ref, send_sem, recv_sem, dev_sib).wait_recv()

    def send(k, yy, hh, cols_, to, own=False):
        dst = at(yy, hh, c, cols_)
        src = tok.at[:, pl.ds(cols_[0], cols_[1])] if own else dst
        push(src, dst, sends.at[k], recvs.at[k], to)

    def arrive(k, yy, hh, cols_, sib=False):
        landed(at(yy, hh, 1 - c if sib else c, cols_), sends.at[k], recvs.at[k])

    tall = pl.ds(pl.multiple_of(c * 64, 64), 64)
    locals_ = [
        pltpu.make_async_copy(tok, at(y, h, c, whole), locs.at[0]),
        pltpu.make_async_copy(wbc, st_w.at[tall], locs.at[1]),
        pltpu.make_async_copy(wdt, st_dt, locs.at[2]),
        pltpu.make_async_copy(wx, w.at[:, pl.ds(0, COLS)], locs.at[3]),
        pltpu.make_async_copy(wz, w.at[:, pl.ds(COLS, COLS)], locs.at[4]),
    ]
    st_w[...] = jnp.zeros_like(st_w)
    for copy in locals_:
        copy.start()
    greet(
        [dev_up, dev_down, dev_z, dev_sib, dev_zsib, across]
        + on_line
        + [span(later, h), span(later, n), span(before, h), span(before, n)]
    )
    send(0, y, h, part_p, dev_z, own=True)
    send(1, y, h, part_q, dev_up, own=True)
    send(2, y, h, part_q, dev_down, own=True)
    send(3, y, h, whole, dev_sib, own=True)
    send(4, y, h, part_q, dev_z, own=True)
    send(5, y, h, part_p, dev_up, own=True)
    send(6, y, h, part_p, dev_down, own=True)

    units = [(y, h), (y, n), (down, h), (up, h), (down, n), (up, n), (far, h), (far, n)]

    def unit_row(k, flip=False):
        yy, hh = units[k]
        return pl.multiple_of((yy * 4 + (1 - hh if flip else hh) * 2) * ROWS, 2 * ROWS)

    def share(k, row, count):
        rows = pl.ds(row, count)
        push(bco.at[rows], bcs.at[rows], sib_s.at[k], sib_r.at[k], dev_sib)

    def merge(k):
        row = unit_row(k)
        rows = pl.ds(row, 2 * ROWS)
        landed(bcs.at[rows], sib_s.at[k], sib_r.at[k])
        own[pl.ds(pl.multiple_of(row + 16, 16), 2 * ROWS), :] = bco[rows, :] + bcs[rows, :]
        half = pl.ds(pl.multiple_of(row + 16 + c * ROWS, 16), ROWS)
        push(own.at[half], oth.at[half], z_s.at[k, 0], z_r.at[k, 0], dev_z)
        push(own.at[half], oth.at[half], z_s.at[k, 1], z_r.at[k, 1], dev_zsib)

    def merged_there(k):
        row = unit_row(k, flip=True)
        for rel, core in ((0, c), (1, 1 - c)):
            ref = oth.at[pl.ds(pl.multiple_of(row + 16 + core * ROWS, 16), ROWS)]
            landed(ref, z_s.at[k, rel], z_r.at[k, rel])

    def project(k):
        row = unit_row(k)
        rows = pl.ds(row, 2 * ROWS)
        part = jnp.dot(buf[rows, :], w_small[...], preferred_element_type=F32)
        small[rows, :] = part
        lane = lax.broadcasted_iota(jnp.int32, part.shape, 1)
        bco[rows, :] = jnp.where(lane // 64 == c, part, 0.0).astype(BF16)
        share(k, row, 2 * ROWS)
        past = pl.ds(pl.multiple_of(row + 16, 16), 2 * ROWS)
        for out, base, target in ((xp, 0, past), (zs, COLS, rows)):

            @pl.loop(0, COLS // 256)
            def _(j):
                col = pl.multiple_of(j * 256, 256)
                out[target, pl.ds(col, 256)] = jnp.dot(
                    buf[rows, :], w[:, pl.ds(base + col, 256)], preferred_element_type=F32
                ).astype(BF16)

    tap_rows = pl.ds(SPAN, 16)
    tap_own = pl.ds(SPAN + 16, 16)
    tap = jnp.concatenate([cbc[...].astype(F32), jnp.zeros((12, 64), F32)], axis=0)
    none = jnp.zeros_like(tap)
    bco[tap_rows, :] = jnp.where(
        c == 0, jnp.concatenate([tap, none], axis=1), jnp.concatenate([none, tap], axis=1)
    ).astype(BF16)
    share(8, SPAN, 16)

    lane_i = lax.broadcasted_iota(jnp.int32, (256, 3 * COLS), 1)
    deep_i = lax.broadcasted_iota(jnp.int32, (256, 3 * COLS), 0)
    spread[...] = jnp.where(
        deep_i % 128 == (lane_i // COLS + 1) * 8 + lane_i % COLS // HEAD_DIM, 1.0, 0.0
    ).astype(BF16)
    head_lane = lax.broadcasted_iota(jnp.int32, (8, COLS), 1) // HEAD_DIM
    head_sub = lax.broadcasted_iota(jnp.int32, (8, COLS), 0)
    skip_x = sum(jnp.where(head_lane[0:1] == i, skip[i], 0.0) for i in range(8))
    sub256 = lax.broadcasted_iota(jnp.int32, (8, BLOCK), 0)
    bias_r = sum(jnp.where(sub256 == i, bias[i], 0.0) for i in range(8))
    rate_r = sum(jnp.where(sub256 == i, rate[i], 0.0) for i in range(8))

    locals_[1].wait()
    locals_[2].wait()
    st_w[pl.ds(pl.multiple_of((1 - c) * 64, 64), 16), :] = st_dt[...]

    @pl.loop(0, D // 128)
    def _(j):
        part = pl.ds(pl.multiple_of(j * 128, 128), 128)
        w_small[part, :] = st_w[:, part].T

    landed(bcs.at[tap_rows], sib_s.at[8], sib_r.at[8])
    own[tap_own, :] = bco[tap_rows, :] + bcs[tap_rows, :]
    push(own.at[tap_own], oth.at[tap_own], z_s.at[8, 0], z_r.at[8, 0], dev_z)
    locals_[0].wait()
    locals_[3].wait()
    locals_[4].wait()
    arrive(3, y, h, whole, sib=True)
    project(0)
    arrive(1, down, h, part_q)
    send(7, down, h, q_a, dev_up)
    send(8, down, h, part_q, dev_z)
    send(9, down, h, part_q, dev_sib)
    arrive(2, up, h, part_q)
    send(10, up, h, q_b, dev_down)
    send(11, up, h, part_q, dev_z)
    send(12, up, h, part_q, dev_sib)
    merge(0)
    arrive(0, y, n, part_p)
    send(13, y, n, part_p, dev_up)
    send(14, y, n, part_p, dev_down)
    send(15, y, n, part_p, dev_sib)
    arrive(7, far, h, q_a)
    send(17, far, h, q_a, dev_z)
    send(18, far, h, q_a, dev_sib)
    arrive(10, far, h, q_b)
    send(19, far, h, q_b, dev_z)
    send(20, far, h, q_b, dev_sib)
    arrive(4, y, n, part_q)
    send(16, y, n, part_q, dev_sib)
    arrive(5, down, h, part_p)
    send(21, down, h, p_a, dev_up)
    send(22, down, h, part_p, dev_sib)
    arrive(6, up, h, part_p)
    send(23, up, h, p_b, dev_down)
    send(24, up, h, part_p, dev_sib)
    arrive(15, y, n, part_p, sib=True)
    arrive(16, y, n, part_q, sib=True)
    project(1)
    arrive(9, down, h, part_q, sib=True)
    arrive(22, down, h, part_p, sib=True)
    project(2)
    merge(1)
    arrive(13, down, n, part_p)
    send(27, down, n, p_a, dev_up)
    send(28, down, n, part_p, dev_sib)
    arrive(14, up, n, part_p)
    send(29, up, n, p_b, dev_down)
    send(30, up, n, part_p, dev_sib)
    arrive(12, up, h, part_q, sib=True)
    arrive(24, up, h, part_p, sib=True)
    project(3)
    merge(2)
    arrive(8, down, n, part_q)
    send(25, down, n, part_q, dev_sib)
    arrive(11, up, n, part_q)
    send(26, up, n, part_q, dev_sib)
    arrive(25, down, n, part_q, sib=True)
    arrive(28, down, n, part_p, sib=True)
    project(4)
    merge(3)
    arrive(21, far, h, p_a)
    send(33, far, h, p_a, dev_sib)
    arrive(23, far, h, p_b)
    send(34, far, h, p_b, dev_sib)
    arrive(26, up, n, part_q, sib=True)
    arrive(30, up, n, part_p, sib=True)
    project(5)
    merge(4)
    arrive(17, far, n, q_a)
    send(31, far, n, q_a, dev_sib)
    arrive(19, far, n, q_b)
    send(32, far, n, q_b, dev_sib)
    arrive(18, far, h, q_a, sib=True)
    arrive(20, far, h, q_b, sib=True)
    arrive(33, far, h, p_a, sib=True)
    arrive(34, far, h, p_b, sib=True)
    project(6)
    merge(5)
    arrive(27, far, n, p_a)
    send(35, far, n, p_a, dev_sib)
    arrive(29, far, n, p_b)
    send(36, far, n, p_b, dev_sib)
    arrive(31, far, n, q_a, sib=True)
    arrive(32, far, n, q_b, sib=True)
    arrive(35, far, n, p_a, sib=True)
    arrive(36, far, n, p_b, sib=True)
    project(7)
    merge(6)
    merge(7)

    last, first = pl.ds(SPAN, 16), pl.ds(0, 16)
    push(xp.at[last], xp.at[first], halo_s.at[0], halo_r.at[0], span(later, h))
    push(own.at[last], own.at[first], halo_s.at[1], halo_r.at[1], span(later, h))
    push(own.at[last], oth.at[first], halo_s.at[2], halo_r.at[2], span(later, n))

    causal = lax.broadcasted_iota(jnp.int32, (BLOCK, BLOCK), 0)
    summing = jnp.where(causal <= lax.broadcasted_iota(jnp.int32, (BLOCK, BLOCK), 1), 1.0, 0.0)

    @pl.loop(0, 4)
    def _(b):
        rows = pl.ds(pl.multiple_of(b * BLOCK, BLOCK), BLOCK)
        turned = small[rows, :].T
        raw = jnp.where(c == 0, turned[64:72], turned[0:8]) + bias_r
        dt = jnp.maximum(raw, 0.0) + jnp.log1p(jnp.exp(-jnp.abs(raw)))
        accum = jnp.dot(
            dt * rate_r, summing, preferred_element_type=F32, precision=lax.Precision.HIGHEST
        )
        end = accum[:, BLOCK - 1 : BLOCK]
        stack = jnp.concatenate(
            [accum, dt, jnp.exp(accum - end) * dt, jnp.exp(-accum), jnp.zeros((96, BLOCK), F32)], axis=0
        )
        cols[rows, :] = stack.T
        rows_a[b] = accum
        total = jnp.sum(jnp.where(head_sub == head_lane, end, 0.0), axis=0, keepdims=True)
        a_x[b] = jnp.broadcast_to(total, (8, COLS))

    decays[x] = a_x[0] + a_x[1] + a_x[2] + a_x[3]
    for d in (1, 2, 3):
        push(decays.at[x], decays.at[x], line_s.at[3 + d], line_r.at[3 + d], on_line[d - 1])

    taps_x = cx[...].astype(F32)
    step = 64

    def convolve(src, row, lanes, taps):
        v = src[pl.ds(row, step + 16), lanes].astype(F32)
        acc = taps[0:1] * v[13 : 13 + step]
        for k in (1, 2, 3):
            acc = acc + taps[k : k + 1] * v[13 + k : 13 + k + step]
        return silu(acc).astype(BF16)

    def conv_x(low, high):
        @pl.loop(low // step, high // step)
        def _(i):
            row = pl.multiple_of(i * step, step)
            for j in range(4):
                lanes = slice(128 * j, 128 * j + 128)
                xc[pl.ds(row, step), lanes] = convolve(xp, row, lanes, taps_x[:, lanes])

    def conv_maps(src, index, taps, low, high):
        @pl.loop(low // step, high // step)
        def _(i):
            row = pl.multiple_of(i * step, step)
            maps[index, pl.ds(row, step), :] = convolve(src, row, slice(0, 128), taps)

    conv_x(step, SPAN)
    landed(xp.at[first], halo_s.at[0], halo_r.at[0])

    @pl.when(s == 0)
    def _():
        xp[first, :] = jnp.zeros((16, COLS), BF16)

    conv_x(0, step)

    @pl.loop(0, 4)
    def _(b):
        rows = pl.ds(pl.multiple_of(b * BLOCK, BLOCK), BLOCK)
        exact = cols[rows, :]
        high = exact.astype(BF16)
        both = jnp.concatenate([high, (exact - high.astype(F32)).astype(BF16)], axis=1)
        for j in range(4):
            lanes = slice(128 * j, 128 * j + 128)
            value = xc[rows, lanes].astype(F32)
            grown = [
                jnp.dot(both, spread[:, q * COLS + 128 * j : q * COLS + 128 * j + 128], preferred_element_type=F32)
                for q in range(3)
            ]
            dtx[rows, lanes] = (value * grown[0]).astype(BF16)
            xt[rows, lanes] = (value * grown[1]).astype(BF16)
            ea_x[rows, lanes] = grown[2]

    tap_o = own[tap_own, :][0:4].astype(F32)
    conv_maps(own, h, tap_o, step, SPAN)
    landed(oth.at[tap_own], z_s.at[8, 0], z_r.at[8, 0])
    for k in range(8):
        merged_there(k)
    tap_t = oth[tap_own, :][0:4].astype(F32)
    conv_maps(oth, n, tap_t, step, SPAN)
    landed(own.at[first], halo_s.at[1], halo_r.at[1])
    landed(oth.at[first], halo_s.at[2], halo_r.at[2])

    @pl.when(s == 0)
    def _():
        own[first, :] = jnp.zeros((16, 128), BF16)
        oth[first, :] = jnp.zeros((16, 128), BF16)

    conv_maps(own, h, tap_o, 0, step)
    conv_maps(oth, n, tap_t, 0, step)

    state[...] = jnp.zeros_like(state)

    @pl.loop(0, 4)
    def _(b):
        rows = pl.ds(pl.multiple_of(b * BLOCK, BLOCK), BLOCK)
        turned = maps[0, rows, :].T
        b_t[:, rows] = turned
        entry[b] = state[...]
        state[...] = jnp.exp(-a_x[b][0:1]) * state[...] + jnp.dot(
            turned, xt[rows, :], preferred_element_type=F32
        )

    states[x] = state[...].astype(BF16)
    for d in (1, 2, 3):
        push(states.at[x], states.at[x], line_s.at[d - 1], line_r.at[d - 1], on_line[d - 1])

    pair_lane = lax.broadcasted_iota(jnp.int32, (128, 128), 1)

    @pl.loop(0, 4)
    def _(b):
        start = pl.multiple_of(b * BLOCK, BLOCK)
        rows = pl.ds(start, BLOCK)
        aff[...] = jnp.dot(maps[1, rows, :], b_t[:, rows], preferred_element_type=F32)
        accum = rows_a[b]
        for t in (0, 1):
            reach = 128 * (t + 1)
            here = pl.ds(pl.multiple_of(start + 128 * t, 128), 128)
            near = pl.ds(start, reach)
            keep = (
                lax.broadcasted_iota(jnp.int32, (128, reach), 0) + 128 * t
                >= lax.broadcasted_iota(jnp.int32, (128, reach), 1)
            )
            column = cols[here, :]
            for j in range(4):
                lanes = slice(128 * j, 128 * j + 128)
                weights = [
                    jnp.where(
                        keep,
                        aff[128 * t : 128 * t + 128, 0:reach]
                        * jnp.exp(accum[i : i + 1, 0:reach] - column[:, i : i + 1]),
                        0.0,
                    ).astype(BF16)
                    for i in (2 * j, 2 * j + 1)
                ]
                both = jnp.dot(
                    jnp.concatenate(weights, axis=0), dtx[near, lanes], preferred_element_type=F32
                )
                yloc[here, lanes] = (
                    jnp.where(pair_lane < HEAD_DIM, both[0:128], both[128:256])
                    + skip_x[:, lanes] * xc[here, lanes].astype(F32)
                )

    for d in (1, 2, 3):
        index = (x + 4 - d) % 4
        landed(decays.at[index], line_s.at[3 + d], line_r.at[3 + d])
        landed(states.at[index], line_s.at[d - 1], line_r.at[d - 1])
    total = jnp.zeros((STATE, COLS), F32)
    for j in range(4):
        total = jnp.exp(-decays[j][0:1]) * total + states[j].astype(F32)
    t_out[...] = total.astype(BF16)
    push(t_out, t_in, t_s.at[0], t_r.at[0], across)
    total = jnp.zeros((STATE, COLS), F32)
    passed = jnp.zeros((1, COLS), F32)
    for j in range(4):
        taken = jnp.where(j < x, 1.0, 0.0)
        through = jnp.where(j < x, jnp.exp(-decays[j][0:1]), 1.0)
        total = through * total + taken * states[j].astype(F32)
        passed = passed + taken * decays[j][0:1]
    landed(t_in, t_s.at[0], t_r.at[0])
    state[...] = total + jnp.where(line == 1, jnp.exp(-passed), 0.0) * t_in[...].astype(F32)

    @pl.loop(0, 4)
    def _(b):
        rows = pl.ds(pl.multiple_of(b * BLOCK, BLOCK), BLOCK)
        ahead = sum(jnp.where(i < b, 1.0, 0.0) * a_x[i][0:1] for i in range(3))
        squares = jnp.zeros((BLOCK, 128), F32)
        for j in range(4):
            lanes = slice(128 * j, 128 * j + 128)
            entering = entry[b, :, lanes] + jnp.exp(-ahead[:, lanes]) * state[:, lanes]
            far_y = jnp.dot(maps[1, rows, :], entering.astype(BF16), preferred_element_type=F32)
            value = yloc[rows, lanes] + far_y * ea_x[rows, lanes]
            value = value * silu(zs[rows, lanes].astype(F32))
            squares = squares + value * value
            g_out[rows, lanes] = (value * gain[:, lanes].astype(F32)).astype(BF16)
        sq_out[rows, :] = jnp.broadcast_to(
            jnp.sum(squares, axis=1, keepdims=True), (BLOCK, 128)
        ).astype(BF16)

    for copy in started:
        copy.wait_send()


def mix(tokens, w_x, w_z, w_bc, w_dt, conv_x, conv_bc, dt_bias, decay_rate, skip, norm_gain):
    anywhere = pl.BlockSpec(memory_space=pl.ANY)
    vmem = pl.BlockSpec(memory_space=pltpu.VMEM)
    smem = pl.BlockSpec(memory_space=pltpu.SMEM)
    dma = pltpu.SemaphoreType.DMA
    return pl.pallas_call(
        mixer_kernel,
        out_shape=(
            jax.ShapeDtypeStruct((SPAN, COLS), BF16),
            jax.ShapeDtypeStruct((SPAN, 128), BF16),
        ),
        in_specs=[anywhere] * 5 + [vmem, vmem, smem, smem, smem, vmem],
        out_specs=(vmem, vmem),
        scratch_shapes=[
            pltpu.VMEM((SPAN, D), BF16),
            pltpu.VMEM((D, 2 * COLS), BF16),
            pltpu.VMEM((D, 128), BF16),
            pltpu.VMEM((128, D), BF16),
            pltpu.VMEM((16, D), BF16),
            pltpu.VMEM((SPAN + 16, COLS), BF16),
            pltpu.VMEM((SPAN, COLS), BF16),
            pltpu.VMEM((SPAN, 128), F32),
            pltpu.VMEM((SPAN + 16, 128), BF16),
            pltpu.VMEM((SPAN + 16, 128), BF16),
            pltpu.VMEM((SPAN + 32, 128), BF16),
            pltpu.VMEM((SPAN + 32, 128), BF16),
            pltpu.VMEM((2, SPAN, 128), BF16),
            pltpu.VMEM((STATE, SPAN), BF16),
            pltpu.VMEM((SPAN, COLS), BF16),
            pltpu.VMEM((SPAN, COLS), BF16),
            pltpu.VMEM((SPAN, COLS), BF16),
            pltpu.VMEM((SPAN, COLS), F32),
            pltpu.VMEM((SPAN, COLS), F32),
            pltpu.VMEM((SPAN, 128), F32),
            pltpu.VMEM((4, 8, BLOCK), F32),
            pltpu.VMEM((4, 8, COLS), F32),
            pltpu.VMEM((256, 3 * COLS), BF16),
            pltpu.VMEM((BLOCK, BLOCK), F32),
            pltpu.VMEM((4, STATE, COLS), F32),
            pltpu.VMEM((STATE, COLS), F32),
            pltpu.VMEM((4, STATE, COLS), BF16),
            pltpu.VMEM((4, 8, COLS), F32),
            pltpu.VMEM((STATE, COLS), BF16),
            pltpu.VMEM((STATE, COLS), BF16),
            dma((37,)), dma((37,)), dma((5,)), dma((9,)), dma((9,)), dma((9, 2)), dma((9, 2)),
            dma((3,)), dma((3,)), dma((7,)), dma((7,)), dma((1,)), dma((1,)),
        ],
        compiler_params=pltpu.CompilerParams(
            collective_id=1, has_side_effects=True, vmem_limit_bytes=58 << 20
        ),
        name="mix",
    )(
        tokens, w_x, w_z, w_bc.T, jnp.pad(w_dt.T, ((0, 8), (0, 0))), conv_x, conv_bc, dt_bias,
        decay_rate, skip, norm_gain.reshape(1, COLS),
    )


def reduce_kernel(
    g, sq, w_out, out, o, sib, zq, pa, pb, qa, qb, pf, qf, zp, sends, recvs
):
    s, y, h, c = place()
    up, down, far = (y + 1) % 4, (y + 3) % 4, (y + 2) % 4
    dev = lambda yy, hh, cc: (s, yy * 4 + hh * 2 + cc)
    dev_up, dev_down, dev_z, dev_sib = dev(up, h, c), dev(down, h, c), dev(y, 1 - h, c), dev(y, h, 1 - c)
    wide_q = WIDE - SPLIT
    part_p, part_q = (0, SPLIT), (SPLIT, wide_q)
    p_a, p_b = (0, HALF_P), (HALF_P, SPLIT - HALF_P)
    q_a, q_b = (SPLIT, HALF_Q), (SPLIT + HALF_Q, wide_q - HALF_Q)
    started = []

    def at(yy, hh, cc, cols):
        row = pl.multiple_of((yy * 4 + hh * 2 + cc) * ROWS, ROWS)
        return o.at[pl.ds(row, ROWS), pl.ds(cols[0], cols[1])]

    def copy_of(k, src, dst, to):
        return pltpu.make_async_remote_copy(
            src_ref=src, dst_ref=dst, send_sem=sends.at[k], recv_sem=recvs.at[k],
            device_id=to, device_id_type=MESH,
        )

    def send(k, src, dst, to):
        copy = copy_of(k, src, dst, to)
        copy.start()
        started.append(copy)

    def arrive(k, ref):
        copy_of(k, ref, ref, dev_sib).wait_recv()

    def add(yy, hh, cols, ref):
        target = at(yy, hh, c, cols)

        @pl.loop(0, ROWS // 16)
        def _(i):
            rows = pl.ds(pl.multiple_of(i * 16, 16), 16)
            target[rows, :] = (target[rows, :].astype(F32) + ref[rows, :].astype(F32)).astype(BF16)

    def chip(yy, hh):
        return yy * 2 + hh

    def partial(yy, hh, k):
        row = pl.multiple_of((yy * 4 + hh * 2) * ROWS, 2 * ROWS)
        rows = pl.ds(row, 2 * ROWS)
        left = g[rows, :]

        @pl.loop(0, D // 512)
        def _(j):
            cols = pl.ds(pl.multiple_of(j * 512, 512), 512)
            o[rows, cols] = jnp.dot(left, w_out[:, cols], preferred_element_type=F32).astype(BF16)

        o[rows, pl.ds(D, 128)] = sq[rows, :]
        send(k, at(yy, hh, 1 - c, (0, WIDE)), sib.at[chip(yy, hh)], dev_sib)

    def joined(yy, hh, k):
        ref = sib.at[chip(yy, hh)]
        arrive(k, ref)
        add(yy, hh, (0, WIDE), ref)

    greet([dev_up, dev_down, dev_z, dev_sib])
    n = 1 - h
    partial(far, n, 0)
    partial(far, h, 1)
    joined(far, n, 0)
    send(8, at(far, n, c, p_a), pa.at[n], dev_up)
    send(9, at(far, n, c, p_b), pb.at[n], dev_down)
    send(10, at(far, n, c, part_q), zq.at[far], dev_z)
    partial(up, n, 2)
    joined(far, h, 1)
    send(11, at(far, h, c, p_a), pa.at[h], dev_up)
    send(12, at(far, h, c, p_b), pb.at[h], dev_down)
    partial(down, n, 3)
    joined(up, n, 2)
    send(13, at(up, n, c, part_q), zq.at[up], dev_z)
    partial(up, h, 4)
    joined(down, n, 3)
    send(14, at(down, n, c, part_q), zq.at[down], dev_z)
    arrive(8, pa.at[n])
    add(up, n, p_a, pa.at[n])
    send(15, at(up, n, c, part_p), pf.at[0, n], dev_up)
    arrive(9, pb.at[n])
    add(down, n, p_b, pb.at[n])
    send(16, at(down, n, c, part_p), pf.at[1, n], dev_down)
    partial(down, h, 5)
    joined(up, h, 4)
    arrive(11, pa.at[h])
    add(up, h, p_a, pa.at[h])
    send(17, at(up, h, c, part_p), pf.at[0, h], dev_up)
    partial(y, n, 6)
    joined(down, h, 5)
    arrive(12, pb.at[h])
    add(down, h, p_b, pb.at[h])
    send(18, at(down, h, c, part_p), pf.at[1, h], dev_down)
    joined(y, n, 6)
    send(19, at(y, n, c, part_q), zq.at[y], dev_z)
    partial(y, h, 7)
    arrive(10, zq.at[far])
    add(far, h, part_q, zq.at[far])
    send(20, at(far, h, c, q_a), qa, dev_up)
    send(21, at(far, h, c, q_b), qb, dev_down)
    joined(y, h, 7)
    arrive(13, zq.at[up])
    add(up, h, part_q, zq.at[up])
    arrive(20, qa)
    add(up, h, q_a, qa)
    send(22, at(up, h, c, part_q), qf.at[0], dev_up)
    arrive(14, zq.at[down])
    add(down, h, part_q, zq.at[down])
    arrive(21, qb)
    add(down, h, q_b, qb)
    send(23, at(down, h, c, part_q), qf.at[1], dev_down)
    arrive(15, pf.at[0, n])
    add(y, n, part_p, pf.at[0, n])
    arrive(16, pf.at[1, n])
    add(y, n, part_p, pf.at[1, n])
    send(24, at(y, n, c, part_p), zp, dev_z)
    arrive(17, pf.at[0, h])
    add(y, h, part_p, pf.at[0, h])
    arrive(18, pf.at[1, h])
    add(y, h, part_p, pf.at[1, h])
    arrive(19, zq.at[y])
    arrive(22, qf.at[0])
    arrive(23, qf.at[1])
    mine_q = at(y, h, c, part_q)
    mine_p = at(y, h, c, part_p)
    terms = (mine_q, zq.at[y], qf.at[0], qf.at[1])
    lane = pl.ds(D - SPLIT, 128)
    squares = sum(t[:, lane].astype(F32) for t in terms)
    scale = lax.rsqrt(squares / (COLS * 16) + 1e-05)

    @pl.loop(0, (D - SPLIT) // 128)
    def _(j):
        cols = pl.ds(pl.multiple_of(j * 128, 128), 128)
        total = sum(t[:, cols].astype(F32) for t in terms)
        out[:, pl.ds(pl.multiple_of(SPLIT + j * 128, 128), 128)] = (total * scale).astype(BF16)

    arrive(24, zp)

    @pl.loop(0, SPLIT // 128)
    def _(j):
        cols = pl.ds(pl.multiple_of(j * 128, 128), 128)
        total = mine_p[:, cols].astype(F32) + zp[:, cols].astype(F32)
        out[:, cols] = (total * scale).astype(BF16)

    for copy in started:
        copy.wait_send()


def project_reduce(g, sq, w_out):
    vmem = pl.BlockSpec(memory_space=pltpu.VMEM)
    wide_q = WIDE - SPLIT
    return pl.pallas_call(
        reduce_kernel,
        out_shape=jax.ShapeDtypeStruct((ROWS, D), BF16),
        in_specs=[vmem] * 3,
        out_specs=vmem,
        scratch_shapes=[
            pltpu.VMEM((SPAN, WIDE), BF16),
            pltpu.VMEM((8, ROWS, WIDE), BF16),
            pltpu.VMEM((4, ROWS, wide_q), BF16),
            pltpu.VMEM((2, ROWS, HALF_P), BF16),
            pltpu.VMEM((2, ROWS, SPLIT - HALF_P), BF16),
            pltpu.VMEM((ROWS, HALF_Q), BF16),
            pltpu.VMEM((ROWS, wide_q - HALF_Q), BF16),
            pltpu.VMEM((2, 2, ROWS, SPLIT), BF16),
            pltpu.VMEM((2, ROWS, wide_q), BF16),
            pltpu.VMEM((ROWS, SPLIT), BF16),
            pltpu.SemaphoreType.DMA((25,)),
            pltpu.SemaphoreType.DMA((25,)),
        ],
        compiler_params=pltpu.CompilerParams(
            collective_id=2, has_side_effects=True, vmem_limit_bytes=56 << 20
        ),
        name="project_reduce",
    )(g, sq, w_out)


def on_device(
    tokens, w_x, w_z, w_bc, w_dt, conv_x, conv_bc, dt_bias, decay_rate, skip, norm_gain, w_out
):
    gated, squares = mix(
        tokens, w_x, w_z, w_bc, w_dt, conv_x, conv_bc, dt_bias, decay_rate, skip, norm_gain
    )
    return project_reduce(gated, squares, w_out)


def solution(mesh):
    placed = (
        P(("seq", "tp"), None),
        P(None, "tp"),
        P(None, "tp"),
        P(None, "tp"),
        P(None, "tp"),
        P(None, "tp"),
        P(None, "tp"),
        P("tp"),
        P("tp"),
        P("tp"),
        P("tp"),
        P("tp", None),
    )
    return jax.shard_map(
        on_device, mesh=mesh, in_specs=placed, out_specs=P(("seq", "tp"), None), check_vma=False
    )
```

```python
import jax
import jax.numpy as jnp
from jax import lax
from jax.experimental import pallas as pl
from jax.experimental.pallas import tpu as pltpu
from jax.sharding import PartitionSpec as P

HEAD_DIM = 64
STATE = 128
BLOCK = 256
MESH = pl.DeviceIdType.MESH
F32 = jnp.float32
BF16 = jnp.bfloat16

D = 6144
ROWS = 64
SPAN = 1024
COLS = 512
SPLIT = 3584
HALF_P = SPLIT // 2
HALF_Q = 1280
WIDE = D + 128


def place():
    tp = lax.axis_index("tp")
    return lax.axis_index("seq"), tp // 4, tp // 2 % 2, tp % 2


def greet(peers):
    barrier = pltpu.get_barrier_semaphore()
    for peer in peers:
        pl.semaphore_signal(barrier, inc=1, device_id=peer, device_id_type=MESH)
    pl.semaphore_wait(barrier, len(peers))


def silu(v):
    return v / (1.0 + jnp.exp(-v))


def mixer_kernel(
    tok, wx, wz, wbc, wdt, cx, cbc, bias, rate, skip, gain, g_out, sq_out,
    buf, partials, w, w_small, st_w, st_dt, xp, zs, small, bco, bcs, own, oth, maps, b_t, xc, dtx, xt,
    ea_x, yloc, cols, rows_a, a_x, spread, aff, entry, state, states, decays, t_out, t_in,
    sends, recvs, locs, sib_s, sib_r, z_s, z_r, halo_s, halo_r, line_s, line_r, t_s, t_r,
):
    s, y, h, c = place()
    up, down, far = (y + 1) % 4, (y + 3) % 4, (y + 2) % 4
    n = 1 - h
    line, x = s // 4, s % 4
    dev = lambda yy, hh, cc: (s, yy * 4 + hh * 2 + cc)
    span = lambda ss, hh: (ss, y * 4 + hh * 2 + c)
    dev_up, dev_down, dev_z, dev_sib = dev(up, h, c), dev(down, h, c), dev(y, n, c), dev(y, h, 1 - c)
    dev_zsib = dev(y, n, 1 - c)
    later, before = (s + 1) % 8, (s + 7) % 8
    on_line = [span(line * 4 + (x + d) % 4, h) for d in (1, 2, 3)]
    across = span((1 - line) * 4 + x, h)
    part_p, part_q = (0, SPLIT), (SPLIT, D - SPLIT)
    p_a, p_b = (0, HALF_P), (HALF_P, SPLIT - HALF_P)
    q_a, q_b = (SPLIT, HALF_Q), (SPLIT + HALF_Q, D - SPLIT - HALF_Q)
    whole = (0, D)

    def at(yy, hh, cc, cols_):
        row = pl.multiple_of((yy * 4 + hh * 2 + cc) * ROWS, ROWS)
        return buf.at[pl.ds(row, ROWS), pl.ds(cols_[0], cols_[1])]

    started = []

    def remote(src, dst, send_sem, recv_sem, to):
        return pltpu.make_async_remote_copy(
            src_ref=src, dst_ref=dst, send_sem=send_sem, recv_sem=recv_sem,
            device_id=to, device_id_type=MESH,
        )

    def push(src, dst, send_sem, recv_sem, to):
        copy = remote(src, dst, send_sem, recv_sem, to)
        copy.start()
        started.append(copy)
        return copy

    def sent(*copies):
        for copy in copies:
            copy.wait_send()
            started[:] = [other for other in started if other is not copy]

    def landed(ref, send_sem, recv_sem):
        remote(ref, ref, send_sem, recv_sem, dev_sib).wait_recv()

    def send(k, yy, hh, cols_, to, own=False):
        dst = at(yy, hh, c, cols_)
        src = tok.at[:, pl.ds(cols_[0], cols_[1])] if own else dst
        return push(src, dst, sends.at[k], recvs.at[k], to)

    def arrive(k, yy, hh, cols_, sib=False):
        landed(at(yy, hh, 1 - c if sib else c, cols_), sends.at[k], recvs.at[k])

    tall = pl.ds(pl.multiple_of(c * 64, 64), 64)
    locals_ = [
        pltpu.make_async_copy(tok, at(y, h, c, whole), locs.at[0]),
        pltpu.make_async_copy(wbc, st_w.at[tall], locs.at[1]),
        pltpu.make_async_copy(wdt, st_dt, locs.at[2]),
        pltpu.make_async_copy(wx, w.at[:, pl.ds(0, COLS)], locs.at[3]),
        pltpu.make_async_copy(wz, w.at[:, pl.ds(COLS, COLS)], locs.at[4]),
    ]
    st_w[...] = jnp.zeros_like(st_w)
    for copy in locals_:
        copy.start()
    greet(
        [dev_up, dev_down, dev_z, dev_sib, dev_zsib, across]
        + on_line
        + [span(later, h), span(later, n), span(before, h), span(before, n)]
    )
    send(0, y, h, part_p, dev_z, own=True)
    send(1, y, h, part_q, dev_up, own=True)
    send(2, y, h, part_q, dev_down, own=True)
    send(3, y, h, whole, dev_sib, own=True)

    units = [(y, h), (y, n), (down, h), (up, h), (down, n), (up, n), (far, h), (far, n)]

    def unit_row(k, flip=False):
        yy, hh = units[k]
        return pl.multiple_of((yy * 4 + (1 - hh if flip else hh) * 2) * ROWS, 2 * ROWS)

    def share(k, row, count):
        rows = pl.ds(row, count)
        push(bco.at[rows], bcs.at[rows], sib_s.at[k], sib_r.at[k], dev_sib)

    def merge(k):
        row = unit_row(k)
        rows = pl.ds(row, 2 * ROWS)
        landed(bcs.at[rows], sib_s.at[k], sib_r.at[k])
        own[pl.ds(pl.multiple_of(row + 16, 16), 2 * ROWS), :] = bco[rows, :] + bcs[rows, :]
        half = pl.ds(pl.multiple_of(row + 16 + c * ROWS, 16), ROWS)
        push(own.at[half], oth.at[half], z_s.at[k, 0], z_r.at[k, 0], dev_z)
        push(own.at[half], oth.at[half], z_s.at[k, 1], z_r.at[k, 1], dev_zsib)

    def merged_there(k):
        row = unit_row(k, flip=True)
        for rel, core in ((0, c), (1, 1 - c)):
            ref = oth.at[pl.ds(pl.multiple_of(row + 16 + core * ROWS, 16), ROWS)]
            landed(ref, z_s.at[k, rel], z_r.at[k, rel])

    def project(k, cols_=(0, D), keep=None, add=None):
        row = unit_row(k)
        rows = pl.ds(row, 2 * ROWS)
        inner = pl.ds(cols_[0], cols_[1])
        part = jnp.dot(buf[rows, inner], w_small[inner, :], preferred_element_type=F32)
        if add is not None:
            part = part + partials[add, :, 2 * COLS : 2 * COLS + 128]
        if keep is not None:
            partials[keep, :, 2 * COLS : 2 * COLS + 128] = part
        else:
            small[rows, :] = part
            lane = lax.broadcasted_iota(jnp.int32, part.shape, 1)
            bco[rows, :] = jnp.where(lane // 64 == c, part, 0.0).astype(BF16)
            share(k, row, 2 * ROWS)
        past = pl.ds(pl.multiple_of(row + 16, 16), 2 * ROWS)
        for out, base, target in ((xp, 0, past), (zs, COLS, rows)):

            lanes = pl.ds(base, COLS)
            part = jnp.dot(buf[rows, inner], w[inner, lanes], preferred_element_type=F32)
            if add is not None:
                part = part + partials[add, :, lanes]
            if keep is not None:
                partials[keep, :, lanes] = part
            else:
                out[target, :] = part.astype(BF16)

    tap_rows = pl.ds(SPAN, 16)
    tap_own = pl.ds(SPAN + 16, 16)
    tap = jnp.concatenate([cbc[...].astype(F32), jnp.zeros((12, 64), F32)], axis=0)
    none = jnp.zeros_like(tap)
    bco[tap_rows, :] = jnp.where(
        c == 0, jnp.concatenate([tap, none], axis=1), jnp.concatenate([none, tap], axis=1)
    ).astype(BF16)
    share(8, SPAN, 16)

    lane_i = lax.broadcasted_iota(jnp.int32, (256, 3 * COLS), 1)
    deep_i = lax.broadcasted_iota(jnp.int32, (256, 3 * COLS), 0)
    spread[...] = jnp.where(
        deep_i % 128 == (lane_i // COLS + 1) * 8 + lane_i % COLS // HEAD_DIM, 1.0, 0.0
    ).astype(BF16)
    head_lane = lax.broadcasted_iota(jnp.int32, (8, COLS), 1) // HEAD_DIM
    head_sub = lax.broadcasted_iota(jnp.int32, (8, COLS), 0)
    skip_x = sum(jnp.where(head_lane[0:1] == i, skip[i], 0.0) for i in range(8))
    sub256 = lax.broadcasted_iota(jnp.int32, (8, BLOCK), 0)
    bias_r = sum(jnp.where(sub256 == i, bias[i], 0.0) for i in range(8))
    rate_r = sum(jnp.where(sub256 == i, rate[i], 0.0) for i in range(8))

    locals_[1].wait()
    locals_[2].wait()
    st_w[pl.ds(pl.multiple_of((1 - c) * 64, 64), 16), :] = (
        jnp.concatenate([st_dt[...].astype(F32), jnp.zeros((8, D), F32)], axis=0).astype(BF16)
    )

    @pl.loop(0, D // 128)
    def _(j):
        part = pl.ds(pl.multiple_of(j * 128, 128), 128)
        w_small[part, :] = st_w[:, part].T

    landed(bcs.at[tap_rows], sib_s.at[8], sib_r.at[8])
    own[tap_own, :] = bco[tap_rows, :] + bcs[tap_rows, :]
    push(own.at[tap_own], oth.at[tap_own], z_s.at[8, 0], z_r.at[8, 0], dev_z)
    locals_[0].wait()
    locals_[3].wait()
    locals_[4].wait()
    arrive(3, y, h, whole, sib=True)
    project(0)
    send(5, y, h, part_p, dev_up, own=True)
    send(6, y, h, part_p, dev_down, own=True)
    send(4, y, h, part_q, dev_z, own=True)
    arrive(1, down, h, part_q)
    send(7, down, h, q_a, dev_up)
    send(8, down, h, part_q, dev_z)
    send(9, down, h, part_q, dev_sib)
    arrive(2, up, h, part_q)
    send(10, up, h, q_b, dev_down)
    send(11, up, h, part_q, dev_z)
    send(12, up, h, part_q, dev_sib)
    merge(0)
    arrive(0, y, n, part_p)
    send(13, y, n, part_p, dev_up)
    send(14, y, n, part_p, dev_down)
    send(15, y, n, part_p, dev_sib)
    arrive(4, y, n, part_q)
    send(16, y, n, part_q, dev_sib)
    arrive(5, down, h, part_p)
    send(21, down, h, p_a, dev_up)
    send(22, down, h, part_p, dev_sib)
    arrive(6, up, h, part_p)
    send(23, up, h, p_b, dev_down)
    send(24, up, h, part_p, dev_sib)
    arrive(15, y, n, part_p, sib=True)
    arrive(16, y, n, part_q, sib=True)
    project(1)
    arrive(7, far, h, q_a)
    send(17, far, h, q_a, dev_z)
    send(18, far, h, q_a, dev_sib)
    arrive(10, far, h, q_b)
    send(19, far, h, q_b, dev_z)
    send(20, far, h, q_b, dev_sib)
    arrive(9, down, h, part_q, sib=True)
    arrive(22, down, h, part_p, sib=True)
    project(2)
    merge(1)
    arrive(8, down, n, part_q)
    send(25, down, n, part_q, dev_sib)
    arrive(12, up, h, part_q, sib=True)
    arrive(24, up, h, part_p, sib=True)
    project(3)
    arrive(18, far, h, q_a, sib=True)
    arrive(20, far, h, q_b, sib=True)
    project(6, part_q, keep=0)
    merge(2)
    arrive(13, down, n, part_p)
    send(27, down, n, p_a, dev_up)
    send(28, down, n, part_p, dev_sib)
    arrive(14, up, n, part_p)
    send(29, up, n, p_b, dev_down)
    send(30, up, n, part_p, dev_sib)
    merge(3)
    arrive(11, up, n, part_q)
    send(26, up, n, part_q, dev_sib)
    arrive(21, far, h, p_a)
    send(33, far, h, p_a, dev_sib)
    arrive(23, far, h, p_b)
    send(34, far, h, p_b, dev_sib)
    arrive(25, down, n, part_q, sib=True)
    arrive(28, down, n, part_p, sib=True)
    project(4)
    arrive(26, up, n, part_q, sib=True)
    arrive(30, up, n, part_p, sib=True)
    project(5)
    merge(4)
    arrive(33, far, h, p_a, sib=True)
    arrive(34, far, h, p_b, sib=True)
    project(6, part_p, add=0)
    merge(5)
    arrive(17, far, n, q_a)
    send(31, far, n, q_a, dev_sib)
    arrive(19, far, n, q_b)
    send(32, far, n, q_b, dev_sib)
    arrive(27, far, n, p_a)
    send(35, far, n, p_a, dev_sib)
    arrive(29, far, n, p_b)
    send(36, far, n, p_b, dev_sib)
    arrive(31, far, n, q_a, sib=True)
    arrive(32, far, n, q_b, sib=True)
    project(7, part_q, keep=1)
    merge(6)
    arrive(35, far, n, p_a, sib=True)
    arrive(36, far, n, p_b, sib=True)
    project(7, part_p, add=1)
    merge(7)

    last, first = pl.ds(SPAN, 16), pl.ds(0, 16)
    push(xp.at[last], xp.at[first], halo_s.at[0], halo_r.at[0], span(later, h))
    push(own.at[last], own.at[first], halo_s.at[1], halo_r.at[1], span(later, h))
    push(own.at[last], oth.at[first], halo_s.at[2], halo_r.at[2], span(later, n))

    causal = lax.broadcasted_iota(jnp.int32, (BLOCK, BLOCK), 0)
    summing = jnp.where(causal <= lax.broadcasted_iota(jnp.int32, (BLOCK, BLOCK), 1), 1.0, 0.0)

    @pl.loop(0, 4)
    def _(b):
        rows = pl.ds(pl.multiple_of(b * BLOCK, BLOCK), BLOCK)
        turned = small[rows, :].T
        raw = jnp.where(c == 0, turned[64:72], turned[0:8]) + bias_r
        dt = jnp.maximum(raw, 0.0) + jnp.log1p(jnp.exp(-jnp.abs(raw)))
        accum = jnp.dot(
            dt * rate_r, summing, preferred_element_type=F32, precision=lax.Precision.HIGHEST
        )
        end = accum[:, BLOCK - 1 : BLOCK]
        stack = jnp.concatenate(
            [accum, dt, jnp.exp(accum - end) * dt, jnp.exp(-accum), jnp.zeros((96, BLOCK), F32)], axis=0
        )
        cols[rows, :] = stack.T
        rows_a[b] = accum
        total = jnp.sum(jnp.where(head_sub == head_lane, end, 0.0), axis=0, keepdims=True)
        a_x[b] = jnp.broadcast_to(total, (8, COLS))

    decays[x] = a_x[0] + a_x[1] + a_x[2] + a_x[3]
    for d in (1, 2, 3):
        push(decays.at[x], decays.at[x], line_s.at[5 + d], line_r.at[5 + d], on_line[d - 1])

    taps_x = cx[...].astype(F32)
    step = 64

    def convolve(src, row, lanes, taps):
        v = src[pl.ds(row, step + 16), lanes].astype(F32)
        acc = taps[0:1] * v[13 : 13 + step]
        for k in (1, 2, 3):
            acc = acc + taps[k : k + 1] * v[13 + k : 13 + k + step]
        return silu(acc).astype(BF16)

    def conv_x(low, high):
        @pl.loop(low // step, high // step)
        def _(i):
            row = pl.multiple_of(i * step, step)
            for j in range(4):
                lanes = slice(128 * j, 128 * j + 128)
                xc[pl.ds(row, step), lanes] = convolve(xp, row, lanes, taps_x[:, lanes])

    def conv_maps(src, index, taps, low, high):
        @pl.loop(low // step, high // step)
        def _(i):
            row = pl.multiple_of(i * step, step)
            maps[index, pl.ds(row, step), :] = convolve(src, row, slice(0, 128), taps)

    conv_x(step, SPAN)
    landed(xp.at[first], halo_s.at[0], halo_r.at[0])

    @pl.when(s == 0)
    def _():
        xp[first, :] = jnp.zeros((16, COLS), BF16)

    conv_x(0, step)

    @pl.loop(0, 4)
    def _(b):
        rows = pl.ds(pl.multiple_of(b * BLOCK, BLOCK), BLOCK)
        exact = cols[rows, :]
        high = exact.astype(BF16)
        both = jnp.concatenate([high, (exact - high.astype(F32)).astype(BF16)], axis=1)
        for j in range(4):
            lanes = slice(128 * j, 128 * j + 128)
            value = xc[rows, lanes].astype(F32)
            grown = [
                jnp.dot(both, spread[:, q * COLS + 128 * j : q * COLS + 128 * j + 128], preferred_element_type=F32)
                for q in range(3)
            ]
            dtx[rows, lanes] = (value * grown[0]).astype(BF16)
            xt[rows, lanes] = (value * grown[1]).astype(BF16)
            ea_x[rows, lanes] = grown[2]

    tap_o = own[tap_own, :][0:4].astype(F32)
    conv_maps(own, h, tap_o, step, SPAN)
    landed(oth.at[tap_own], z_s.at[8, 0], z_r.at[8, 0])
    for k in range(8):
        merged_there(k)
    tap_t = oth[tap_own, :][0:4].astype(F32)
    conv_maps(oth, n, tap_t, step, SPAN)
    landed(own.at[first], halo_s.at[1], halo_r.at[1])
    landed(oth.at[first], halo_s.at[2], halo_r.at[2])

    @pl.when(s == 0)
    def _():
        own[first, :] = jnp.zeros((16, 128), BF16)
        oth[first, :] = jnp.zeros((16, 128), BF16)

    conv_maps(own, h, tap_o, 0, step)
    conv_maps(oth, n, tap_t, 0, step)

    state[...] = jnp.zeros_like(state)

    @pl.loop(0, 4)
    def _(b):
        rows = pl.ds(pl.multiple_of(b * BLOCK, BLOCK), BLOCK)
        turned = maps[0, rows, :].T
        b_t[:, rows] = turned
        entry[b] = state[...]
        state[...] = jnp.exp(-a_x[b][0:1]) * state[...] + jnp.dot(
            turned, xt[rows, :], preferred_element_type=F32
        )

    states[x] = state[...].astype(BF16)
    halves = [pl.ds(0, COLS // 2), pl.ds(COLS // 2, COLS // 2)]
    for part, lanes in enumerate(halves):
        for d in (1, 3, 2):
            ref = states.at[x, :, lanes]
            push(ref, ref, line_s.at[part * 3 + d - 1], line_r.at[part * 3 + d - 1], on_line[d - 1])

    pair_lane = lax.broadcasted_iota(jnp.int32, (128, 128), 1)

    @pl.loop(0, 4)
    def _(b):
        start = pl.multiple_of(b * BLOCK, BLOCK)
        rows = pl.ds(start, BLOCK)
        aff[...] = jnp.dot(maps[1, rows, :], b_t[:, rows], preferred_element_type=F32)
        accum = rows_a[b]
        for t in (0, 1):
            reach = 128 * (t + 1)
            here = pl.ds(pl.multiple_of(start + 128 * t, 128), 128)
            near = pl.ds(start, reach)
            keep = (
                lax.broadcasted_iota(jnp.int32, (128, reach), 0) + 128 * t
                >= lax.broadcasted_iota(jnp.int32, (128, reach), 1)
            )
            column = cols[here, :]
            for j in range(4):
                lanes = slice(128 * j, 128 * j + 128)
                weights = [
                    jnp.where(
                        keep,
                        aff[128 * t : 128 * t + 128, 0:reach]
                        * jnp.exp(accum[i : i + 1, 0:reach] - column[:, i : i + 1]),
                        0.0,
                    ).astype(BF16)
                    for i in (2 * j, 2 * j + 1)
                ]
                both = jnp.dot(
                    jnp.concatenate(weights, axis=0), dtx[near, lanes], preferred_element_type=F32
                )
                yloc[here, lanes] = (
                    jnp.where(pair_lane < HEAD_DIM, both[0:128], both[128:256])
                    + skip_x[:, lanes] * xc[here, lanes].astype(F32)
                )

    for d in (1, 2, 3):
        index = (x + 4 - d) % 4
        landed(decays.at[index], line_s.at[5 + d], line_r.at[5 + d])
    for part, lanes in enumerate(halves):
        for d in (1, 3, 2):
            landed(
                states.at[(x + 4 - d) % 4, :, lanes], line_s.at[part * 3 + d - 1], line_r.at[part * 3 + d - 1]
            )
        total = jnp.zeros((STATE, COLS // 2), F32)
        for j in range(4):
            total = jnp.exp(-decays[j, 0:1, lanes]) * total + states[j, :, lanes].astype(F32)
        t_out[:, lanes] = total.astype(BF16)
        push(t_out.at[:, lanes], t_in.at[:, lanes], t_s.at[part], t_r.at[part], across)
    for part, lanes in enumerate(halves):
        total = jnp.zeros((STATE, COLS // 2), F32)
        passed = jnp.zeros((1, COLS // 2), F32)
        for j in range(4):
            taken = jnp.where(j < x, 1.0, 0.0)
            through = jnp.where(j < x, jnp.exp(-decays[j, 0:1, lanes]), 1.0)
            total = through * total + taken * states[j, :, lanes].astype(F32)
            passed = passed + taken * decays[j, 0:1, lanes]
        landed(t_in.at[:, lanes], t_s.at[part], t_r.at[part])
        state[:, lanes] = total + jnp.where(line == 1, jnp.exp(-passed), 0.0) * t_in[:, lanes].astype(F32)

    gain_r = gain[...].astype(F32).reshape(1, COLS)

    @pl.loop(0, 4)
    def _(b):
        rows = pl.ds(pl.multiple_of(b * BLOCK, BLOCK), BLOCK)
        ahead = sum(jnp.where(i < b, 1.0, 0.0) * a_x[i][0:1] for i in range(3))
        squares = jnp.zeros((BLOCK, 128), F32)
        for j in range(4):
            lanes = slice(128 * j, 128 * j + 128)
            entering = entry[b, :, lanes] + jnp.exp(-ahead[:, lanes]) * state[:, lanes]
            far_y = jnp.dot(maps[1, rows, :], entering.astype(BF16), preferred_element_type=F32)
            value = yloc[rows, lanes] + far_y * ea_x[rows, lanes]
            value = value * silu(zs[rows, lanes].astype(F32))
            squares = squares + value * value
            g_out[rows, lanes] = (value * gain_r[:, lanes]).astype(BF16)
        sq_out[rows, :] = jnp.broadcast_to(
            jnp.sum(squares, axis=1, keepdims=True), (BLOCK, 128)
        ).astype(BF16)

    for copy in started:
        copy.wait_send()


def mix(tokens, w_x, w_z, w_bc, w_dt, conv_x, conv_bc, dt_bias, decay_rate, skip, norm_gain):
    anywhere = pl.BlockSpec(memory_space=pl.ANY)
    vmem = pl.BlockSpec(memory_space=pltpu.VMEM)
    smem = pl.BlockSpec(memory_space=pltpu.SMEM)
    dma = pltpu.SemaphoreType.DMA
    return pl.pallas_call(
        mixer_kernel,
        out_shape=(
            jax.ShapeDtypeStruct((SPAN, COLS), BF16),
            jax.ShapeDtypeStruct((SPAN, 128), BF16),
        ),
        in_specs=[anywhere] * 5 + [vmem, vmem, smem, smem, smem, vmem],
        out_specs=(vmem, vmem),
        scratch_shapes=[
            pltpu.VMEM((SPAN, D), BF16),
            pltpu.VMEM((2, 2 * ROWS, 2 * COLS + 128), F32),
            pltpu.VMEM((D, 2 * COLS), BF16),
            pltpu.VMEM((D, 128), BF16),
            pltpu.VMEM((128, D), BF16),
            pltpu.VMEM((8, D), BF16),
            pltpu.VMEM((SPAN + 16, COLS), BF16),
            pltpu.VMEM((SPAN, COLS), BF16),
            pltpu.VMEM((SPAN, 128), F32),
            pltpu.VMEM((SPAN + 16, 128), BF16),
            pltpu.VMEM((SPAN + 16, 128), BF16),
            pltpu.VMEM((SPAN + 32, 128), BF16),
            pltpu.VMEM((SPAN + 32, 128), BF16),
            pltpu.VMEM((2, SPAN, 128), BF16),
            pltpu.VMEM((STATE, SPAN), BF16),
            pltpu.VMEM((SPAN, COLS), BF16),
            pltpu.VMEM((SPAN, COLS), BF16),
            pltpu.VMEM((SPAN, COLS), BF16),
            pltpu.VMEM((SPAN, COLS), F32),
            pltpu.VMEM((SPAN, COLS), F32),
            pltpu.VMEM((SPAN, 128), F32),
            pltpu.VMEM((4, 8, BLOCK), F32),
            pltpu.VMEM((4, 8, COLS), F32),
            pltpu.VMEM((256, 3 * COLS), BF16),
            pltpu.VMEM((BLOCK, BLOCK), F32),
            pltpu.VMEM((4, STATE, COLS), F32),
            pltpu.VMEM((STATE, COLS), F32),
            pltpu.VMEM((4, STATE, COLS), BF16),
            pltpu.VMEM((4, 8, COLS), F32),
            pltpu.VMEM((STATE, COLS), BF16),
            pltpu.VMEM((STATE, COLS), BF16),
            dma((37,)), dma((37,)), dma((5,)), dma((9,)), dma((9,)), dma((9, 2)), dma((9, 2)),
            dma((3,)), dma((3,)), dma((9,)), dma((9,)), dma((2,)), dma((2,)),
        ],
        compiler_params=pltpu.CompilerParams(
            collective_id=1, has_side_effects=True, vmem_limit_bytes=58 << 20
        ),
        name="mix",
    )(
        tokens, w_x, w_z, w_bc.T, w_dt.T, conv_x, conv_bc, dt_bias,
        decay_rate, skip, norm_gain,
    )


def reduce_kernel(
    g, sq, w_out, out, o, sib, zq, pa, pb, qa, qb, pf, qf, zp, sends, recvs
):
    s, y, h, c = place()
    up, down, far = (y + 1) % 4, (y + 3) % 4, (y + 2) % 4
    dev = lambda yy, hh, cc: (s, yy * 4 + hh * 2 + cc)
    dev_up, dev_down, dev_z, dev_sib = dev(up, h, c), dev(down, h, c), dev(y, 1 - h, c), dev(y, h, 1 - c)
    wide_q = WIDE - SPLIT
    part_p, part_q = (0, SPLIT), (SPLIT, wide_q)
    p_a, p_b = (0, HALF_P), (HALF_P, SPLIT - HALF_P)
    q_a, q_b = (SPLIT, HALF_Q), (SPLIT + HALF_Q, wide_q - HALF_Q)
    started = []

    def at(yy, hh, cc, cols):
        row = pl.multiple_of((yy * 4 + hh * 2 + cc) * ROWS, ROWS)
        return o.at[pl.ds(row, ROWS), pl.ds(cols[0], cols[1])]

    def copy_of(k, src, dst, to):
        return pltpu.make_async_remote_copy(
            src_ref=src, dst_ref=dst, send_sem=sends.at[k], recv_sem=recvs.at[k],
            device_id=to, device_id_type=MESH,
        )

    def send(k, src, dst, to):
        copy = copy_of(k, src, dst, to)
        copy.start()
        started.append(copy)
        return copy

    def arrive(k, ref):
        copy_of(k, ref, ref, dev_sib).wait_recv()

    def add(yy, hh, cols, ref):
        target = at(yy, hh, c, cols)

        @pl.loop(0, ROWS // 16)
        def _(i):
            rows = pl.ds(pl.multiple_of(i * 16, 16), 16)
            target[rows, :] = (target[rows, :].astype(F32) + ref[rows, :].astype(F32)).astype(BF16)

    def chip(yy, hh):
        return yy * 2 + hh

    def partial(yy, hh, k):
        row = pl.multiple_of((yy * 4 + hh * 2) * ROWS, 2 * ROWS)
        rows = pl.ds(row, 2 * ROWS)
        left = g[rows, :]

        for j in range(D // 1536):
            cols = pl.ds(j * 1536, 1536)
            o[rows, cols] = jnp.dot(left, w_out[:, cols], preferred_element_type=F32).astype(BF16)

        o[rows, pl.ds(D, 128)] = sq[rows, :]
        send(k, at(yy, hh, 1 - c, (0, WIDE)), sib.at[chip(yy, hh)], dev_sib)

    def joined(yy, hh, k):
        ref = sib.at[chip(yy, hh)]
        arrive(k, ref)
        add(yy, hh, (0, WIDE), ref)

    def in_q(cols):
        return pl.ds(cols[0] - SPLIT, cols[1])

    def in_p(cols):
        return pl.ds(cols[0], cols[1])

    greet([dev_up, dev_down, dev_z, dev_sib])
    n = 1 - h
    partial(far, n, 0)
    partial(up, n, 2)
    joined(far, n, 0)
    send(8, at(far, n, c, p_a), pa.at[n], dev_up)
    send(9, at(far, n, c, p_b), pb.at[n], dev_down)
    send(10, at(far, n, c, part_q), zq.at[far], dev_z)
    partial(down, n, 3)
    joined(up, n, 2)
    send(11, at(up, n, c, p_b), pf.at[0, n, :, in_p(p_b)], dev_up)
    send(13, at(up, n, c, part_q), zq.at[up], dev_z)
    partial(far, h, 1)
    joined(down, n, 3)
    send(12, at(down, n, c, p_a), pf.at[1, n, :, in_p(p_a)], dev_down)
    send(14, at(down, n, c, part_q), zq.at[down], dev_z)
    partial(up, h, 4)
    joined(far, h, 1)
    arrive(8, pa.at[n])
    add(up, n, p_a, pa.at[n])
    send(15, at(up, n, c, p_a), pf.at[0, n, :, in_p(p_a)], dev_up)
    arrive(9, pb.at[n])
    add(down, n, p_b, pb.at[n])
    send(16, at(down, n, c, p_b), pf.at[1, n, :, in_p(p_b)], dev_down)
    send(17, at(far, h, c, p_a), pa.at[h], dev_up)
    send(18, at(far, h, c, p_b), pb.at[h], dev_down)
    partial(down, h, 5)
    joined(up, h, 4)
    send(19, at(up, h, c, p_b), pf.at[0, h, :, in_p(p_b)], dev_up)
    partial(y, n, 6)
    joined(down, h, 5)
    send(20, at(down, h, c, p_a), pf.at[1, h, :, in_p(p_a)], dev_down)
    partial(y, h, 7)
    joined(y, n, 6)
    send(21, at(y, n, c, part_q), zq.at[y], dev_z)
    arrive(10, zq.at[far])
    add(far, h, part_q, zq.at[far])
    joined(y, h, 7)
    arrive(11, pf.at[0, n, :, in_p(p_b)])
    arrive(15, pf.at[0, n, :, in_p(p_a)])
    add(y, n, part_p, pf.at[0, n])
    arrive(12, pf.at[1, n, :, in_p(p_a)])
    arrive(16, pf.at[1, n, :, in_p(p_b)])
    add(y, n, part_p, pf.at[1, n])
    send(24, at(y, n, c, part_p), zp, dev_z)
    arrive(17, pa.at[h])
    add(up, h, p_a, pa.at[h])
    send(22, at(up, h, c, p_a), pf.at[0, h, :, in_p(p_a)], dev_up)
    arrive(18, pb.at[h])
    add(down, h, p_b, pb.at[h])
    send(23, at(down, h, c, p_b), pf.at[1, h, :, in_p(p_b)], dev_down)
    send(25, at(far, h, c, q_a), qa, dev_up)
    send(26, at(far, h, c, q_b), qb, dev_down)
    arrive(13, zq.at[up])
    add(up, h, part_q, zq.at[up])
    send(27, at(up, h, c, q_b), qf.at[0, :, in_q(q_b)], dev_up)
    arrive(14, zq.at[down])
    add(down, h, part_q, zq.at[down])
    send(28, at(down, h, c, q_a), qf.at[1, :, in_q(q_a)], dev_down)
    arrive(19, pf.at[0, h, :, in_p(p_b)])
    arrive(22, pf.at[0, h, :, in_p(p_a)])
    add(y, h, part_p, pf.at[0, h])
    arrive(20, pf.at[1, h, :, in_p(p_a)])
    arrive(23, pf.at[1, h, :, in_p(p_b)])
    add(y, h, part_p, pf.at[1, h])
    arrive(25, qa)
    add(up, h, q_a, qa)
    send(29, at(up, h, c, q_a), qf.at[0, :, in_q(q_a)], dev_up)
    arrive(26, qb)
    add(down, h, q_b, qb)
    send(30, at(down, h, c, q_b), qf.at[1, :, in_q(q_b)], dev_down)
    arrive(21, zq.at[y])
    arrive(27, qf.at[0, :, in_q(q_b)])
    arrive(28, qf.at[1, :, in_q(q_a)])
    arrive(29, qf.at[0, :, in_q(q_a)])
    arrive(30, qf.at[1, :, in_q(q_b)])
    mine_q = at(y, h, c, part_q)
    mine_p = at(y, h, c, part_p)
    terms = (mine_q, zq.at[y], qf.at[0], qf.at[1])
    lane = pl.ds(D - SPLIT, 128)
    squares = sum(t[:, lane].astype(F32) for t in terms)
    scale = lax.rsqrt(squares / (COLS * 16) + 1e-05)

    @pl.loop(0, (D - SPLIT) // 128)
    def _(j):
        cols = pl.ds(pl.multiple_of(j * 128, 128), 128)
        total = sum(t[:, cols].astype(F32) for t in terms)
        out[:, pl.ds(pl.multiple_of(SPLIT + j * 128, 128), 128)] = (total * scale).astype(BF16)

    arrive(24, zp)

    @pl.loop(0, SPLIT // 128)
    def _(j):
        cols = pl.ds(pl.multiple_of(j * 128, 128), 128)
        total = mine_p[:, cols].astype(F32) + zp[:, cols].astype(F32)
        out[:, cols] = (total * scale).astype(BF16)

    for copy in started:
        copy.wait_send()


def project_reduce(g, sq, w_out):
    vmem = pl.BlockSpec(memory_space=pltpu.VMEM)
    wide_q = WIDE - SPLIT
    return pl.pallas_call(
        reduce_kernel,
        out_shape=jax.ShapeDtypeStruct((ROWS, D), BF16),
        in_specs=[vmem] * 3,
        out_specs=vmem,
        scratch_shapes=[
            pltpu.VMEM((SPAN, WIDE), BF16),
            pltpu.VMEM((8, ROWS, WIDE), BF16),
            pltpu.VMEM((4, ROWS, wide_q), BF16),
            pltpu.VMEM((2, ROWS, HALF_P), BF16),
            pltpu.VMEM((2, ROWS, SPLIT - HALF_P), BF16),
            pltpu.VMEM((ROWS, HALF_Q), BF16),
            pltpu.VMEM((ROWS, wide_q - HALF_Q), BF16),
            pltpu.VMEM((2, 2, ROWS, SPLIT), BF16),
            pltpu.VMEM((2, ROWS, wide_q), BF16),
            pltpu.VMEM((ROWS, SPLIT), BF16),
            pltpu.SemaphoreType.DMA((31,)),
            pltpu.SemaphoreType.DMA((31,)),
        ],
        compiler_params=pltpu.CompilerParams(
            collective_id=2, has_side_effects=True, vmem_limit_bytes=56 << 20
        ),
        name="project_reduce",
    )(g, sq, w_out)


def on_device(
    tokens, w_x, w_z, w_bc, w_dt, conv_x, conv_bc, dt_bias, decay_rate, skip, norm_gain, w_out
):
    gated, squares = mix(
        tokens, w_x, w_z, w_bc, w_dt, conv_x, conv_bc, dt_bias, decay_rate, skip, norm_gain
    )
    return project_reduce(gated, squares, w_out)


def solution(mesh):
    placed = (
        P(("seq", "tp"), None),
        P(None, "tp"),
        P(None, "tp"),
        P(None, "tp"),
        P(None, "tp"),
        P(None, "tp"),
        P(None, "tp"),
        P("tp"),
        P("tp"),
        P("tp"),
        P("tp"),
        P("tp", None),
    )
    return jax.shard_map(
        on_device, mesh=mesh, in_specs=placed, out_specs=P(("seq", "tp"), None), check_vma=False
    )
```

```python
import jax
import jax.numpy as jnp
from jax import lax
from jax.experimental import pallas as pl
from jax.experimental.pallas import tpu as pltpu
from jax.sharding import PartitionSpec as P

HEAD_DIM = 64
STATE = 128
BLOCK = 256
MESH = pl.DeviceIdType.MESH
F32 = jnp.float32
BF16 = jnp.bfloat16

D = 6144
ROWS = 64
SPAN = 1024
COLS = 512
SPLIT = 3584
HALF_P = SPLIT // 2
HALF_Q = 1280
WIDE = D + 128


def place():
    tp = lax.axis_index("tp")
    return lax.axis_index("seq"), tp // 4, tp // 2 % 2, tp % 2


def greet(peers):
    barrier = pltpu.get_barrier_semaphore()
    for peer in peers:
        pl.semaphore_signal(barrier, inc=1, device_id=peer, device_id_type=MESH)
    pl.semaphore_wait(barrier, len(peers))


def silu(v):
    return v / (1.0 + jnp.exp(-v))


def mixer_kernel(
    tok, wx, wz, wbc, wdt, cx, cbc, bias, rate, skip, gain, w_out, out,
    buf, partials, w, w_small, st_w, st_dt, xp, zs, small, bco, bcs, own, oth, maps, b_t, xc, dtx, xt,
    yloc, cols, rows_a, a_x, spread, aff, entry, state, states, decays, t_out, t_in,
    sends, recvs, locs, sib_s, sib_r, z_s, z_r, halo_s, halo_r, line_s, line_r, t_s, t_r,
    g, w_o, *reduce_refs,
):
    s, y, h, c = place()
    up, down, far = (y + 1) % 4, (y + 3) % 4, (y + 2) % 4
    n = 1 - h
    line, x = s // 4, s % 4
    dev = lambda yy, hh, cc: (s, yy * 4 + hh * 2 + cc)
    span = lambda ss, hh: (ss, y * 4 + hh * 2 + c)
    dev_up, dev_down, dev_z, dev_sib = dev(up, h, c), dev(down, h, c), dev(y, n, c), dev(y, h, 1 - c)
    dev_zsib = dev(y, n, 1 - c)
    later, before = (s + 1) % 8, (s + 7) % 8
    on_line = [span(line * 4 + (x + d) % 4, h) for d in (1, 2, 3)]
    across = span((1 - line) * 4 + x, h)
    part_p, part_q = (0, SPLIT), (SPLIT, D - SPLIT)
    p_a, p_b = (0, HALF_P), (HALF_P, SPLIT - HALF_P)
    q_a, q_b = (SPLIT, HALF_Q), (SPLIT + HALF_Q, D - SPLIT - HALF_Q)
    whole = (0, D)

    def at(yy, hh, cc, cols_):
        row = pl.multiple_of((yy * 4 + hh * 2 + cc) * ROWS, ROWS)
        return buf.at[pl.ds(row, ROWS), pl.ds(cols_[0], cols_[1])]

    started = []

    def remote(src, dst, send_sem, recv_sem, to):
        return pltpu.make_async_remote_copy(
            src_ref=src, dst_ref=dst, send_sem=send_sem, recv_sem=recv_sem,
            device_id=to, device_id_type=MESH,
        )

    def push(src, dst, send_sem, recv_sem, to):
        copy = remote(src, dst, send_sem, recv_sem, to)
        copy.start()
        started.append(copy)
        return copy

    def sent(*copies):
        for copy in copies:
            copy.wait_send()
            started[:] = [other for other in started if other is not copy]

    def landed(ref, send_sem, recv_sem):
        remote(ref, ref, send_sem, recv_sem, dev_sib).wait_recv()

    def send(k, yy, hh, cols_, to, own=False):
        dst = at(yy, hh, c, cols_)
        src = tok.at[:, pl.ds(cols_[0], cols_[1])] if own else dst
        return push(src, dst, sends.at[k], recvs.at[k], to)

    def arrive(k, yy, hh, cols_, sib=False):
        landed(at(yy, hh, 1 - c if sib else c, cols_), sends.at[k], recvs.at[k])

    tall = pl.ds(pl.multiple_of(c * 64, 64), 64)
    locals_ = [
        pltpu.make_async_copy(tok, at(y, h, c, whole), locs.at[0]),
        pltpu.make_async_copy(wbc, st_w.at[tall], locs.at[1]),
        pltpu.make_async_copy(wdt, st_dt, locs.at[2]),
        pltpu.make_async_copy(wx, w.at[:, pl.ds(0, COLS)], locs.at[3]),
        pltpu.make_async_copy(wz, w.at[:, pl.ds(COLS, COLS)], locs.at[4]),
        pltpu.make_async_copy(w_out, w_o, locs.at[5]),
    ]
    st_w[...] = jnp.zeros_like(st_w)
    for copy in locals_:
        copy.start()
    greet(
        [dev_up, dev_down, dev_z, dev_sib, dev_zsib, across]
        + on_line
        + [span(later, h), span(later, n), span(before, h), span(before, n)]
    )
    send(0, y, h, part_p, dev_z, own=True)
    send(1, y, h, part_q, dev_up, own=True)
    send(2, y, h, part_q, dev_down, own=True)
    send(3, y, h, whole, dev_sib, own=True)
    send(5, y, h, part_p, dev_up, own=True)
    send(6, y, h, part_p, dev_down, own=True)
    send(4, y, h, part_q, dev_z, own=True)

    units = [(y, h), (y, n), (down, h), (up, h), (down, n), (up, n), (far, h), (far, n)]

    def unit_row(k, flip=False):
        yy, hh = units[k]
        return pl.multiple_of((yy * 4 + (1 - hh if flip else hh) * 2) * ROWS, 2 * ROWS)

    def share(k, row, count):
        rows = pl.ds(row, count)
        push(bco.at[rows], bcs.at[rows], sib_s.at[k], sib_r.at[k], dev_sib)

    def merge(k):
        row = unit_row(k)
        rows = pl.ds(row, 2 * ROWS)
        landed(bcs.at[rows], sib_s.at[k], sib_r.at[k])
        own[pl.ds(pl.multiple_of(row + 16, 16), 2 * ROWS), :] = bco[rows, :] + bcs[rows, :]
        half = pl.ds(pl.multiple_of(row + 16 + c * ROWS, 16), ROWS)
        push(own.at[half], oth.at[half], z_s.at[k, 0], z_r.at[k, 0], dev_z)
        push(own.at[half], oth.at[half], z_s.at[k, 1], z_r.at[k, 1], dev_zsib)

    def merged_there(k):
        row = unit_row(k, flip=True)
        for rel, core in ((0, c), (1, 1 - c)):
            ref = oth.at[pl.ds(pl.multiple_of(row + 16 + core * ROWS, 16), ROWS)]
            landed(ref, z_s.at[k, rel], z_r.at[k, rel])

    def project(k, cols_=(0, D), keep=None, add=None):
        row = unit_row(k)
        rows = pl.ds(row, 2 * ROWS)
        inner = pl.ds(cols_[0], cols_[1])
        part = jnp.dot(buf[rows, inner], w_small[inner, :], preferred_element_type=F32)
        if add is not None:
            part = part + partials[add, :, 2 * COLS : 2 * COLS + 128]
        if keep is not None:
            partials[keep, :, 2 * COLS : 2 * COLS + 128] = part
        else:
            small[rows, :] = part
            lane = lax.broadcasted_iota(jnp.int32, part.shape, 1)
            bco[rows, :] = jnp.where(lane // 64 == c, part, 0.0).astype(BF16)
            share(k, row, 2 * ROWS)
        past = pl.ds(pl.multiple_of(row + 16, 16), 2 * ROWS)
        for out, base, target in ((xp, 0, past), (zs, COLS, rows)):

            lanes = pl.ds(base, COLS)
            part = jnp.dot(buf[rows, inner], w[inner, lanes], preferred_element_type=F32)
            if add is not None:
                part = part + partials[add, :, lanes]
            if keep is not None:
                partials[keep, :, lanes] = part
            else:
                out[target, :] = part.astype(BF16)

    tap_rows = pl.ds(SPAN, 16)
    tap_own = pl.ds(SPAN + 16, 16)
    tap = jnp.concatenate([cbc[...].astype(F32), jnp.zeros((12, 64), F32)], axis=0)
    none = jnp.zeros_like(tap)
    bco[tap_rows, :] = jnp.where(
        c == 0, jnp.concatenate([tap, none], axis=1), jnp.concatenate([none, tap], axis=1)
    ).astype(BF16)
    share(8, SPAN, 16)

    lane_i = lax.broadcasted_iota(jnp.int32, (256, 3 * COLS), 1)
    deep_i = lax.broadcasted_iota(jnp.int32, (256, 3 * COLS), 0)
    spread[...] = jnp.where(
        deep_i % 128 == (lane_i // COLS + 1) * 8 + lane_i % COLS // HEAD_DIM, 1.0, 0.0
    ).astype(BF16)
    head_lane = lax.broadcasted_iota(jnp.int32, (8, COLS), 1) // HEAD_DIM
    head_sub = lax.broadcasted_iota(jnp.int32, (8, COLS), 0)
    skip_x = sum(jnp.where(head_lane[0:1] == i, skip[i], 0.0) for i in range(8))
    sub256 = lax.broadcasted_iota(jnp.int32, (8, BLOCK), 0)
    bias_r = sum(jnp.where(sub256 == i, bias[i], 0.0) for i in range(8))
    rate_r = sum(jnp.where(sub256 == i, rate[i], 0.0) for i in range(8))

    locals_[1].wait()
    locals_[2].wait()
    st_w[pl.ds(pl.multiple_of((1 - c) * 64, 64), 16), :] = (
        jnp.concatenate([st_dt[...].astype(F32), jnp.zeros((8, D), F32)], axis=0).astype(BF16)
    )

    @pl.loop(0, D // 128)
    def _(j):
        part = pl.ds(pl.multiple_of(j * 128, 128), 128)
        w_small[part, :] = st_w[:, part].T

    landed(bcs.at[tap_rows], sib_s.at[8], sib_r.at[8])
    own[tap_own, :] = bco[tap_rows, :] + bcs[tap_rows, :]
    push(own.at[tap_own], oth.at[tap_own], z_s.at[8, 0], z_r.at[8, 0], dev_z)
    locals_[0].wait()
    locals_[3].wait()
    locals_[4].wait()
    arrive(3, y, h, whole, sib=True)
    project(0)
    arrive(1, down, h, part_q)
    send(8, down, h, part_q, dev_z)
    send(9, down, h, part_q, dev_sib)
    arrive(2, up, h, part_q)
    send(11, up, h, part_q, dev_z)
    send(12, up, h, part_q, dev_sib)
    merge(0)
    arrive(0, y, n, part_p)
    send(13, y, n, part_p, dev_up)
    send(14, y, n, part_p, dev_down)
    send(7, down, h, q_a, dev_up)
    send(10, up, h, q_b, dev_down)
    send(15, y, n, part_p, dev_sib)
    arrive(4, y, n, part_q)
    send(16, y, n, part_q, dev_sib)
    arrive(5, down, h, part_p)
    send(21, down, h, p_a, dev_up)
    send(22, down, h, part_p, dev_sib)
    arrive(6, up, h, part_p)
    send(23, up, h, p_b, dev_down)
    send(24, up, h, part_p, dev_sib)
    arrive(15, y, n, part_p, sib=True)
    arrive(16, y, n, part_q, sib=True)
    project(1)
    arrive(7, far, h, q_a)
    send(17, far, h, q_a, dev_z)
    send(18, far, h, q_a, dev_sib)
    arrive(10, far, h, q_b)
    send(19, far, h, q_b, dev_z)
    send(20, far, h, q_b, dev_sib)
    arrive(9, down, h, part_q, sib=True)
    arrive(22, down, h, part_p, sib=True)
    project(2)
    merge(1)
    arrive(8, down, n, part_q)
    send(25, down, n, part_q, dev_sib)
    arrive(12, up, h, part_q, sib=True)
    arrive(24, up, h, part_p, sib=True)
    project(3)
    arrive(18, far, h, q_a, sib=True)
    arrive(20, far, h, q_b, sib=True)
    project(6, part_q, keep=0)
    merge(2)
    arrive(13, down, n, part_p)
    send(27, down, n, p_a, dev_up)
    send(28, down, n, part_p, dev_sib)
    arrive(14, up, n, part_p)
    send(29, up, n, p_b, dev_down)
    send(30, up, n, part_p, dev_sib)
    merge(3)
    arrive(11, up, n, part_q)
    send(26, up, n, part_q, dev_sib)
    arrive(21, far, h, p_a)
    send(33, far, h, p_a, dev_sib)
    arrive(23, far, h, p_b)
    send(34, far, h, p_b, dev_sib)
    arrive(25, down, n, part_q, sib=True)
    arrive(28, down, n, part_p, sib=True)
    project(4)
    arrive(26, up, n, part_q, sib=True)
    arrive(30, up, n, part_p, sib=True)
    project(5)
    merge(4)
    arrive(33, far, h, p_a, sib=True)
    arrive(34, far, h, p_b, sib=True)
    project(6, part_p, add=0)
    merge(5)
    arrive(17, far, n, q_a)
    send(31, far, n, q_a, dev_sib)
    arrive(19, far, n, q_b)
    send(32, far, n, q_b, dev_sib)
    arrive(27, far, n, p_a)
    send(35, far, n, p_a, dev_sib)
    arrive(29, far, n, p_b)
    send(36, far, n, p_b, dev_sib)
    arrive(31, far, n, q_a, sib=True)
    arrive(32, far, n, q_b, sib=True)
    project(7, part_q, keep=1)
    merge(6)
    arrive(35, far, n, p_a, sib=True)
    arrive(36, far, n, p_b, sib=True)
    project(7, part_p, add=1)
    merge(7)

    last, first = pl.ds(SPAN, 16), pl.ds(0, 16)
    push(xp.at[last], xp.at[first], halo_s.at[0], halo_r.at[0], span(later, h))
    push(own.at[last], own.at[first], halo_s.at[1], halo_r.at[1], span(later, h))
    push(own.at[last], oth.at[first], halo_s.at[2], halo_r.at[2], span(later, n))

    causal = lax.broadcasted_iota(jnp.int32, (BLOCK, BLOCK), 0)
    summing = jnp.where(causal <= lax.broadcasted_iota(jnp.int32, (BLOCK, BLOCK), 1), 1.0, 0.0)

    @pl.loop(0, 4)
    def _(b):
        rows = pl.ds(pl.multiple_of(b * BLOCK, BLOCK), BLOCK)
        turned = small[rows, :].T
        raw = jnp.where(c == 0, turned[64:72], turned[0:8]) + bias_r
        dt = jnp.maximum(raw, 0.0) + jnp.log1p(jnp.exp(-jnp.abs(raw)))
        accum = jnp.dot(
            dt * rate_r, summing, preferred_element_type=F32, precision=lax.Precision.HIGHEST
        )
        end = accum[:, BLOCK - 1 : BLOCK]
        stack = jnp.concatenate(
            [accum, dt, jnp.exp(accum - end) * dt, jnp.exp(-accum), jnp.zeros((96, BLOCK), F32)], axis=0
        )
        cols[rows, :] = stack.T
        rows_a[b] = accum
        total = jnp.sum(jnp.where(head_sub == head_lane, end, 0.0), axis=0, keepdims=True)
        a_x[b] = jnp.broadcast_to(total, (8, COLS))

    decays[x] = a_x[0] + a_x[1] + a_x[2] + a_x[3]
    for d in (1, 2, 3):
        push(decays.at[x], decays.at[x], line_s.at[5 + d], line_r.at[5 + d], on_line[d - 1])

    taps_x = cx[...].astype(F32)
    step = 64

    def convolve(src, row, lanes, taps):
        v = src[pl.ds(row, step + 16), lanes].astype(F32)
        acc = taps[0:1] * v[13 : 13 + step]
        for k in (1, 2, 3):
            acc = acc + taps[k : k + 1] * v[13 + k : 13 + k + step]
        return silu(acc).astype(BF16)

    def split(exact):
        high = exact.astype(BF16)
        return jnp.concatenate([high, (exact - high.astype(F32)).astype(BF16)], axis=1)

    def conv_x(low, high):
        @pl.loop(low // step, high // step)
        def _(i):
            row = pl.multiple_of(i * step, step)
            for j in range(4):
                lanes = slice(128 * j, 128 * j + 128)
                xc[pl.ds(row, step), lanes] = convolve(xp, row, lanes, taps_x[:, lanes])

    def conv_maps(src, index, taps, low, high):
        @pl.loop(low // step, high // step)
        def _(i):
            row = pl.multiple_of(i * step, step)
            maps[index, pl.ds(row, step), :] = convolve(src, row, slice(0, 128), taps)

    conv_x(step, SPAN)
    landed(xp.at[first], halo_s.at[0], halo_r.at[0])

    @pl.when(s == 0)
    def _():
        xp[first, :] = jnp.zeros((16, COLS), BF16)

    conv_x(0, step)

    @pl.loop(0, 4)
    def _(b):
        rows = pl.ds(pl.multiple_of(b * BLOCK, BLOCK), BLOCK)
        both = split(cols[rows, :])
        for j in range(4):
            lanes = slice(128 * j, 128 * j + 128)
            value = xc[rows, lanes].astype(F32)
            grown = [
                jnp.dot(both, spread[:, q * COLS + 128 * j : q * COLS + 128 * j + 128], preferred_element_type=F32)
                for q in range(2)
            ]
            dtx[rows, lanes] = (value * grown[0]).astype(BF16)
            xt[rows, lanes] = (value * grown[1]).astype(BF16)

    tap_o = own[tap_own, :][0:4].astype(F32)
    conv_maps(own, h, tap_o, step, SPAN)
    landed(oth.at[tap_own], z_s.at[8, 0], z_r.at[8, 0])
    for k in range(8):
        merged_there(k)
    tap_t = oth[tap_own, :][0:4].astype(F32)
    conv_maps(oth, n, tap_t, step, SPAN)
    landed(own.at[first], halo_s.at[1], halo_r.at[1])
    landed(oth.at[first], halo_s.at[2], halo_r.at[2])

    @pl.when(s == 0)
    def _():
        own[first, :] = jnp.zeros((16, 128), BF16)
        oth[first, :] = jnp.zeros((16, 128), BF16)

    conv_maps(own, h, tap_o, 0, step)
    conv_maps(oth, n, tap_t, 0, step)

    state[...] = jnp.zeros_like(state)

    @pl.loop(0, 4)
    def _(b):
        rows = pl.ds(pl.multiple_of(b * BLOCK, BLOCK), BLOCK)
        turned = maps[0, rows, :].T
        b_t[:, rows] = turned
        entry[b] = state[...]
        state[...] = jnp.exp(-a_x[b][0:1]) * state[...] + jnp.dot(
            turned, xt[rows, :], preferred_element_type=F32
        )

    states[x] = state[...].astype(BF16)
    halves = [pl.ds(0, COLS // 2), pl.ds(COLS // 2, COLS // 2)]
    for part, lanes in enumerate(halves):
        for d in (1, 3, 2):
            ref = states.at[x, :, lanes]
            push(ref, ref, line_s.at[part * 3 + d - 1], line_r.at[part * 3 + d - 1], on_line[d - 1])

    pair_lane = lax.broadcasted_iota(jnp.int32, (128, 128), 1)

    @pl.loop(0, 4)
    def _(b):
        start = pl.multiple_of(b * BLOCK, BLOCK)
        rows = pl.ds(start, BLOCK)
        aff[...] = jnp.dot(maps[1, rows, :], b_t[:, rows], preferred_element_type=F32)
        accum = rows_a[b]
        for t in (0, 1):
            reach = 128 * (t + 1)
            here = pl.ds(pl.multiple_of(start + 128 * t, 128), 128)
            near = pl.ds(start, reach)
            keep = (
                lax.broadcasted_iota(jnp.int32, (128, reach), 0) + 128 * t
                >= lax.broadcasted_iota(jnp.int32, (128, reach), 1)
            )
            column = cols[here, :]
            for j in range(4):
                lanes = slice(128 * j, 128 * j + 128)
                weights = [
                    jnp.where(
                        keep,
                        aff[128 * t : 128 * t + 128, 0:reach]
                        * jnp.exp(accum[i : i + 1, 0:reach] - column[:, i : i + 1]),
                        0.0,
                    ).astype(BF16)
                    for i in (2 * j, 2 * j + 1)
                ]
                both = jnp.dot(
                    jnp.concatenate(weights, axis=0), dtx[near, lanes], preferred_element_type=F32
                )
                yloc[here, lanes] = (
                    jnp.where(pair_lane < HEAD_DIM, both[0:128], both[128:256])
                    + skip_x[:, lanes] * xc[here, lanes].astype(F32)
                )

    sent(*list(started))

    for d in (1, 2, 3):
        index = (x + 4 - d) % 4
        landed(decays.at[index], line_s.at[5 + d], line_r.at[5 + d])
    for part, lanes in enumerate(halves):
        for d in (1, 3, 2):
            landed(
                states.at[(x + 4 - d) % 4, :, lanes], line_s.at[part * 3 + d - 1], line_r.at[part * 3 + d - 1]
            )
        total = jnp.zeros((STATE, COLS // 2), F32)
        for j in range(4):
            total = jnp.exp(-decays[j, 0:1, lanes]) * total + states[j, :, lanes].astype(F32)
        t_out[:, lanes] = total.astype(BF16)
        push(t_out.at[:, lanes], t_in.at[:, lanes], t_s.at[part], t_r.at[part], across)
    for part, lanes in enumerate(halves):
        total = jnp.zeros((STATE, COLS // 2), F32)
        passed = jnp.zeros((1, COLS // 2), F32)
        for j in range(4):
            taken = jnp.where(j < x, 1.0, 0.0)
            through = jnp.where(j < x, jnp.exp(-decays[j, 0:1, lanes]), 1.0)
            total = through * total + taken * states[j, :, lanes].astype(F32)
            passed = passed + taken * decays[j, 0:1, lanes]
        landed(t_in.at[:, lanes], t_s.at[part], t_r.at[part])
        state[:, lanes] = total + jnp.where(line == 1, jnp.exp(-passed), 0.0) * t_in[:, lanes].astype(F32)

    sent(*list(started))
    gain_r = gain[...].astype(F32).reshape(1, COLS)

    @pl.loop(0, 4)
    def _(b):
        rows = pl.ds(pl.multiple_of(b * BLOCK, BLOCK), BLOCK)
        ahead = sum(jnp.where(i < b, 1.0, 0.0) * a_x[i][0:1] for i in range(3))
        squares = jnp.zeros((BLOCK, 128), F32)
        both = split(cols[rows, :])
        for j in range(4):
            lanes = slice(128 * j, 128 * j + 128)
            entering = entry[b, :, lanes] + jnp.exp(-ahead[:, lanes]) * state[:, lanes]
            far_y = jnp.dot(maps[1, rows, :], entering.astype(BF16), preferred_element_type=F32)
            shrink = jnp.dot(
                both, spread[:, 2 * COLS + 128 * j : 2 * COLS + 128 * j + 128], preferred_element_type=F32
            )
            value = yloc[rows, lanes] + far_y * shrink
            value = value * silu(zs[rows, lanes].astype(F32))
            squares = squares + value * value
            g[rows, lanes] = (value * gain_r[:, lanes]).astype(BF16)
        buf[rows, pl.ds(D, 128)] = jnp.broadcast_to(
            jnp.sum(squares, axis=1, keepdims=True), (BLOCK, 128)
        ).astype(BF16)

    locals_[5].wait()
    reduce_stage(g, w_o, out, buf, *reduce_refs)


def reduce_stage(
    g, w_out, out, o, sib, zq, pa, pb, qa, qb, pf, qf, zp, sends, recvs
):
    s, y, h, c = place()
    up, down, far = (y + 1) % 4, (y + 3) % 4, (y + 2) % 4
    dev = lambda yy, hh, cc: (s, yy * 4 + hh * 2 + cc)
    dev_up, dev_down, dev_z, dev_sib = dev(up, h, c), dev(down, h, c), dev(y, 1 - h, c), dev(y, h, 1 - c)
    wide_q = WIDE - SPLIT
    part_p, part_q = (0, SPLIT), (SPLIT, wide_q)
    p_a, p_b = (0, HALF_P), (HALF_P, SPLIT - HALF_P)
    q_a, q_b = (SPLIT, HALF_Q), (SPLIT + HALF_Q, wide_q - HALF_Q)
    started = []

    def at(yy, hh, cc, cols):
        row = pl.multiple_of((yy * 4 + hh * 2 + cc) * ROWS, ROWS)
        return o.at[pl.ds(row, ROWS), pl.ds(cols[0], cols[1])]

    def copy_of(k, src, dst, to):
        return pltpu.make_async_remote_copy(
            src_ref=src, dst_ref=dst, send_sem=sends.at[k], recv_sem=recvs.at[k],
            device_id=to, device_id_type=MESH,
        )

    def send(k, src, dst, to):
        copy = copy_of(k, src, dst, to)
        copy.start()
        started.append(copy)
        return copy

    def arrive(k, ref):
        copy_of(k, ref, ref, dev_sib).wait_recv()

    def add(yy, hh, cols, ref):
        target = at(yy, hh, c, cols)

        @pl.loop(0, ROWS // 16)
        def _(i):
            rows = pl.ds(pl.multiple_of(i * 16, 16), 16)
            target[rows, :] = (target[rows, :].astype(F32) + ref[rows, :].astype(F32)).astype(BF16)

    def chip(yy, hh):
        return yy * 2 + hh

    def partial(yy, hh, k):
        row = pl.multiple_of((yy * 4 + hh * 2) * ROWS, 2 * ROWS)
        rows = pl.ds(row, 2 * ROWS)
        left = g[rows, :]

        for j in range(D // 1536):
            cols = pl.ds(j * 1536, 1536)
            o[rows, cols] = jnp.dot(left, w_out[:, cols], preferred_element_type=F32).astype(BF16)

        send(k, at(yy, hh, 1 - c, (0, WIDE)), sib.at[chip(yy, hh)], dev_sib)

    def joined(yy, hh, k):
        ref = sib.at[chip(yy, hh)]
        arrive(k, ref)
        add(yy, hh, (0, WIDE), ref)

    def in_q(cols):
        return pl.ds(cols[0] - SPLIT, cols[1])

    def in_p(cols):
        return pl.ds(cols[0], cols[1])

    n = 1 - h
    partial(far, n, 0)
    partial(up, n, 2)
    joined(far, n, 0)
    send(8, at(far, n, c, p_a), pa.at[n], dev_up)
    send(9, at(far, n, c, p_b), pb.at[n], dev_down)
    send(10, at(far, n, c, part_q), zq.at[far], dev_z)
    partial(down, n, 3)
    joined(up, n, 2)
    send(11, at(up, n, c, p_b), pf.at[0, n, :, in_p(p_b)], dev_up)
    send(13, at(up, n, c, part_q), zq.at[up], dev_z)
    partial(far, h, 1)
    joined(down, n, 3)
    send(12, at(down, n, c, p_a), pf.at[1, n, :, in_p(p_a)], dev_down)
    send(14, at(down, n, c, part_q), zq.at[down], dev_z)
    partial(up, h, 4)
    joined(far, h, 1)
    arrive(8, pa.at[n])
    add(up, n, p_a, pa.at[n])
    send(15, at(up, n, c, p_a), pf.at[0, n, :, in_p(p_a)], dev_up)
    arrive(9, pb.at[n])
    add(down, n, p_b, pb.at[n])
    send(16, at(down, n, c, p_b), pf.at[1, n, :, in_p(p_b)], dev_down)
    send(17, at(far, h, c, p_a), pa.at[h], dev_up)
    send(18, at(far, h, c, p_b), pb.at[h], dev_down)
    partial(down, h, 5)
    joined(up, h, 4)
    send(19, at(up, h, c, p_b), pf.at[0, h, :, in_p(p_b)], dev_up)
    partial(y, n, 6)
    joined(down, h, 5)
    send(20, at(down, h, c, p_a), pf.at[1, h, :, in_p(p_a)], dev_down)
    partial(y, h, 7)
    joined(y, n, 6)
    send(21, at(y, n, c, part_q), zq.at[y], dev_z)
    arrive(10, zq.at[far])
    add(far, h, part_q, zq.at[far])
    joined(y, h, 7)
    arrive(11, pf.at[0, n, :, in_p(p_b)])
    arrive(15, pf.at[0, n, :, in_p(p_a)])
    add(y, n, part_p, pf.at[0, n])
    arrive(12, pf.at[1, n, :, in_p(p_a)])
    arrive(16, pf.at[1, n, :, in_p(p_b)])
    add(y, n, part_p, pf.at[1, n])
    send(24, at(y, n, c, part_p), zp, dev_z)
    arrive(17, pa.at[h])
    add(up, h, p_a, pa.at[h])
    send(22, at(up, h, c, p_a), pf.at[0, h, :, in_p(p_a)], dev_up)
    arrive(18, pb.at[h])
    add(down, h, p_b, pb.at[h])
    send(23, at(down, h, c, p_b), pf.at[1, h, :, in_p(p_b)], dev_down)
    send(25, at(far, h, c, q_a), qa, dev_up)
    send(26, at(far, h, c, q_b), qb, dev_down)
    arrive(13, zq.at[up])
    add(up, h, part_q, zq.at[up])
    send(27, at(up, h, c, q_b), qf.at[0, :, in_q(q_b)], dev_up)
    arrive(14, zq.at[down])
    add(down, h, part_q, zq.at[down])
    send(28, at(down, h, c, q_a), qf.at[1, :, in_q(q_a)], dev_down)
    arrive(19, pf.at[0, h, :, in_p(p_b)])
    arrive(22, pf.at[0, h, :, in_p(p_a)])
    add(y, h, part_p, pf.at[0, h])
    arrive(20, pf.at[1, h, :, in_p(p_a)])
    arrive(23, pf.at[1, h, :, in_p(p_b)])
    add(y, h, part_p, pf.at[1, h])
    arrive(25, qa)
    add(up, h, q_a, qa)
    send(29, at(up, h, c, q_a), qf.at[0, :, in_q(q_a)], dev_up)
    arrive(26, qb)
    add(down, h, q_b, qb)
    send(30, at(down, h, c, q_b), qf.at[1, :, in_q(q_b)], dev_down)
    arrive(21, zq.at[y])
    arrive(27, qf.at[0, :, in_q(q_b)])
    arrive(28, qf.at[1, :, in_q(q_a)])
    arrive(29, qf.at[0, :, in_q(q_a)])
    arrive(30, qf.at[1, :, in_q(q_b)])
    mine_q = at(y, h, c, part_q)
    mine_p = at(y, h, c, part_p)
    terms = (mine_q, zq.at[y], qf.at[0], qf.at[1])
    lane = pl.ds(D - SPLIT, 128)
    squares = sum(t[:, lane].astype(F32) for t in terms)
    scale = lax.rsqrt(squares / (COLS * 16) + 1e-05)

    @pl.loop(0, (D - SPLIT) // 128)
    def _(j):
        cols = pl.ds(pl.multiple_of(j * 128, 128), 128)
        total = sum(t[:, cols].astype(F32) for t in terms)
        out[:, pl.ds(pl.multiple_of(SPLIT + j * 128, 128), 128)] = (total * scale).astype(BF16)

    arrive(24, zp)

    @pl.loop(0, SPLIT // 128)
    def _(j):
        cols = pl.ds(pl.multiple_of(j * 128, 128), 128)
        total = mine_p[:, cols].astype(F32) + zp[:, cols].astype(F32)
        out[:, cols] = (total * scale).astype(BF16)

    for copy in started:
        copy.wait_send()


def mix(tokens, w_x, w_z, w_bc, w_dt, conv_x, conv_bc, dt_bias, decay_rate, skip, norm_gain, w_out):
    anywhere = pl.BlockSpec(memory_space=pl.ANY)
    vmem = pl.BlockSpec(memory_space=pltpu.VMEM)
    smem = pl.BlockSpec(memory_space=pltpu.SMEM)
    wide_q = WIDE - SPLIT
    dma = pltpu.SemaphoreType.DMA
    return pl.pallas_call(
        mixer_kernel,
        out_shape=jax.ShapeDtypeStruct((ROWS, D), BF16),
        in_specs=[anywhere] * 5 + [vmem, vmem, smem, smem, smem, vmem, anywhere],
        out_specs=vmem,
        scratch_shapes=[
            pltpu.VMEM((SPAN, WIDE), BF16),
            pltpu.VMEM((2, 2 * ROWS, 2 * COLS + 128), F32),
            pltpu.VMEM((D, 2 * COLS), BF16),
            pltpu.VMEM((D, 128), BF16),
            pltpu.VMEM((128, D), BF16),
            pltpu.VMEM((8, D), BF16),
            pltpu.VMEM((SPAN + 16, COLS), BF16),
            pltpu.VMEM((SPAN, COLS), BF16),
            pltpu.VMEM((SPAN, 128), F32),
            pltpu.VMEM((SPAN + 16, 128), BF16),
            pltpu.VMEM((SPAN + 16, 128), BF16),
            pltpu.VMEM((SPAN + 32, 128), BF16),
            pltpu.VMEM((SPAN + 32, 128), BF16),
            pltpu.VMEM((2, SPAN, 128), BF16),
            pltpu.VMEM((STATE, SPAN), BF16),
            pltpu.VMEM((SPAN, COLS), BF16),
            pltpu.VMEM((SPAN, COLS), BF16),
            pltpu.VMEM((SPAN, COLS), BF16),
            pltpu.VMEM((SPAN, COLS), F32),
            pltpu.VMEM((SPAN, 128), F32),
            pltpu.VMEM((4, 8, BLOCK), F32),
            pltpu.VMEM((4, 8, COLS), F32),
            pltpu.VMEM((256, 3 * COLS), BF16),
            pltpu.VMEM((BLOCK, BLOCK), F32),
            pltpu.VMEM((4, STATE, COLS), F32),
            pltpu.VMEM((STATE, COLS), F32),
            pltpu.VMEM((4, STATE, COLS), BF16),
            pltpu.VMEM((4, 8, COLS), F32),
            pltpu.VMEM((STATE, COLS), BF16),
            pltpu.VMEM((STATE, COLS), BF16),
            dma((37,)), dma((37,)), dma((6,)), dma((9,)), dma((9,)), dma((9, 2)), dma((9, 2)),
            dma((3,)), dma((3,)), dma((9,)), dma((9,)), dma((2,)), dma((2,)),
            pltpu.VMEM((SPAN, COLS), BF16),
            pltpu.VMEM((COLS, D), BF16),
            pltpu.VMEM((8, ROWS, WIDE), BF16),
            pltpu.VMEM((4, ROWS, wide_q), BF16),
            pltpu.VMEM((2, ROWS, HALF_P), BF16),
            pltpu.VMEM((2, ROWS, SPLIT - HALF_P), BF16),
            pltpu.VMEM((ROWS, HALF_Q), BF16),
            pltpu.VMEM((ROWS, wide_q - HALF_Q), BF16),
            pltpu.VMEM((2, 2, ROWS, SPLIT), BF16),
            pltpu.VMEM((2, ROWS, wide_q), BF16),
            pltpu.VMEM((ROWS, SPLIT), BF16),
            pltpu.SemaphoreType.DMA((31,)),
            pltpu.SemaphoreType.DMA((31,)),
        ],
        compiler_params=pltpu.CompilerParams(
            collective_id=1, has_side_effects=True, vmem_limit_bytes=63 << 20
        ),
        name="mix",
    )(
        tokens, w_x, w_z, w_bc.T, w_dt.T, conv_x, conv_bc, dt_bias,
        decay_rate, skip, norm_gain, w_out,
    )


def on_device(
    tokens, w_x, w_z, w_bc, w_dt, conv_x, conv_bc, dt_bias, decay_rate, skip, norm_gain, w_out
):
    return mix(
        tokens, w_x, w_z, w_bc, w_dt, conv_x, conv_bc, dt_bias, decay_rate, skip, norm_gain, w_out
    )


def solution(mesh):
    placed = (
        P(("seq", "tp"), None),
        P(None, "tp"),
        P(None, "tp"),
        P(None, "tp"),
        P(None, "tp"),
        P(None, "tp"),
        P(None, "tp"),
        P("tp"),
        P("tp"),
        P("tp"),
        P("tp"),
        P("tp", None),
    )
    return jax.shard_map(
        on_device, mesh=mesh, in_specs=placed, out_specs=P(("seq", "tp"), None), check_vma=False
    )
```

```python
import jax
import jax.numpy as jnp
from jax import lax
from jax.experimental import pallas as pl
from jax.experimental.pallas import tpu as pltpu
from jax.sharding import PartitionSpec as P

HEAD_DIM = 64
STATE = 128
BLOCK = 256
MESH = pl.DeviceIdType.MESH
F32 = jnp.float32
BF16 = jnp.bfloat16

D = 6144
ROWS = 64
SPAN = 1024
COLS = 512
SPLIT = 3584
HALF_P = SPLIT // 2
HALF_Q = 1280
WIDE = D + 128


def place():
    tp = lax.axis_index("tp")
    return lax.axis_index("seq"), tp // 4, tp // 2 % 2, tp % 2


def greet(peers):
    barrier = pltpu.get_barrier_semaphore()
    for peer in peers:
        pl.semaphore_signal(barrier, inc=1, device_id=peer, device_id_type=MESH)
    pl.semaphore_wait(barrier, len(peers))


def silu(v):
    return v / (1.0 + jnp.exp(-v))


def mixer_kernel(
    tok, wx, wz, wbc, wdt, cx, cbc, bias, rate, skip, gain, w_out, out,
    buf, partials, w, w_small, st_w, st_dt, xp, zs, small, bco, bcs, mp, direct, halo_in, maps, b_t, xc, dtx, xt,
    yloc, cols, rows_a, a_x, aff, entry, state, states, decays, t_out, t_in,
    sends, recvs, locs, sib_s, sib_r, z_s, z_r, halo_s, halo_r, line_s, line_r, t_s, t_r,
    g, w_o, *reduce_refs,
):
    s, y, h, c = place()
    up, down, far = (y + 1) % 4, (y + 3) % 4, (y + 2) % 4
    n = 1 - h
    line, x = s // 4, s % 4
    dev = lambda yy, hh, cc: (s, yy * 4 + hh * 2 + cc)
    span = lambda ss, hh, cc: (ss, y * 4 + hh * 2 + cc)
    dev_up, dev_down, dev_z, dev_sib = dev(up, h, c), dev(down, h, c), dev(y, n, c), dev(y, h, 1 - c)
    dev_zsib = dev(y, n, 1 - c)
    later, before = (s + 1) % 8, (s + 7) % 8
    on_line = [span(line * 4 + (x + d) % 4, h, c) for d in (1, 2, 3)]
    across = span((1 - line) * 4 + x, h, c)
    part_p, part_q = (0, SPLIT), (SPLIT, D - SPLIT)
    p_a, p_b = (0, HALF_P), (HALF_P, SPLIT - HALF_P)
    q_a, q_b = (SPLIT, HALF_Q), (SPLIT + HALF_Q, D - SPLIT - HALF_Q)
    whole = (0, D)

    def at(yy, hh, cc, cols_):
        row = pl.multiple_of((yy * 4 + hh * 2 + cc) * ROWS, ROWS)
        return buf.at[pl.ds(row, ROWS), pl.ds(cols_[0], cols_[1])]

    started = []

    def remote(src, dst, send_sem, recv_sem, to):
        return pltpu.make_async_remote_copy(
            src_ref=src, dst_ref=dst, send_sem=send_sem, recv_sem=recv_sem,
            device_id=to, device_id_type=MESH,
        )

    def push(src, dst, send_sem, recv_sem, to):
        copy = remote(src, dst, send_sem, recv_sem, to)
        copy.start()
        started.append(copy)
        return copy

    def sent(*copies):
        for copy in copies:
            copy.wait_send()
            started[:] = [other for other in started if other is not copy]

    def landed(ref, send_sem, recv_sem):
        remote(ref, ref, send_sem, recv_sem, dev_sib).wait_recv()

    def send(k, yy, hh, cols_, to, own=False):
        dst = at(yy, hh, c, cols_)
        src = tok.at[:, pl.ds(cols_[0], cols_[1])] if own else dst
        return push(src, dst, sends.at[k], recvs.at[k], to)

    def arrive(k, yy, hh, cols_, sib=False):
        landed(at(yy, hh, 1 - c if sib else c, cols_), sends.at[k], recvs.at[k])

    tall = pl.ds(pl.multiple_of(c * 64, 64), 64)
    locals_ = [
        pltpu.make_async_copy(tok, at(y, h, c, whole), locs.at[0]),
        pltpu.make_async_copy(wbc, st_w.at[tall], locs.at[1]),
        pltpu.make_async_copy(wdt, st_dt, locs.at[2]),
        pltpu.make_async_copy(wx, w.at[:, pl.ds(0, COLS)], locs.at[3]),
        pltpu.make_async_copy(wz, w.at[:, pl.ds(COLS, COLS)], locs.at[4]),
        pltpu.make_async_copy(w_out, w_o, locs.at[5]),
    ]
    st_w[...] = jnp.zeros_like(st_w)
    for copy in locals_:
        copy.start()
    greet(
        [dev_up, dev_down, dev_z, dev_sib, dev_zsib, across]
        + on_line
        + [span(later, hh, cc) for hh in (h, n) for cc in (c, 1 - c)]
        + [span(before, hh, cc) for hh in (h, n) for cc in (c, 1 - c)]
    )
    send(0, y, h, part_p, dev_z, own=True)
    send(1, y, h, part_q, dev_up, own=True)
    send(2, y, h, part_q, dev_down, own=True)
    send(3, y, h, whole, dev_sib, own=True)
    send(5, y, h, part_p, dev_up, own=True)
    send(6, y, h, part_p, dev_down, own=True)
    send(4, y, h, part_q, dev_z, own=True)

    units = [(y, h), (y, n), (down, h), (up, h), (down, n), (up, n), (far, h), (far, n)]

    def unit_row(k, flip=False):
        yy, hh = units[k]
        return pl.multiple_of((yy * 4 + (1 - hh if flip else hh) * 2) * ROWS, 2 * ROWS)

    def share(k, row, count):
        rows = pl.ds(row, count)
        push(bco.at[rows], bcs.at[rows], sib_s.at[k], sib_r.at[k], dev_sib)

    def merge(k):
        row = unit_row(k)
        rows = pl.ds(row, 2 * ROWS)
        landed(bcs.at[rows], sib_s.at[k], sib_r.at[k])
        mp[h, pl.ds(pl.multiple_of(row + 16, 16), 2 * ROWS), :] = bco[rows, :] + bcs[rows, :]
        half = pl.ds(pl.multiple_of(row + 16 + c * ROWS, 16), ROWS)
        push(mp.at[h, half], mp.at[h, half], z_s.at[k, 0], z_r.at[k, 0], dev_z)
        push(mp.at[h, half], mp.at[h, half], z_s.at[k, 1], z_r.at[k, 1], dev_zsib)

    def merged_there(k):
        row = unit_row(k, flip=True)
        for rel, core in ((0, c), (1, 1 - c)):
            ref = mp.at[n, pl.ds(pl.multiple_of(row + 16 + core * ROWS, 16), ROWS)]
            landed(ref, z_s.at[k, rel], z_r.at[k, rel])

    def project_small(k, cols_=(0, D), keep=None, add=None):
        row = unit_row(k)
        rows, inner = pl.ds(row, 2 * ROWS), pl.ds(cols_[0], cols_[1])
        part = jnp.dot(buf[rows, inner], w_small[inner, :], preferred_element_type=F32)
        if add is not None:
            part = part + partials[add, :, 2 * COLS : 2 * COLS + 128]
        if keep is not None:
            partials[keep, :, 2 * COLS : 2 * COLS + 128] = part
        else:
            small[rows, :] = part
            lane = lax.broadcasted_iota(jnp.int32, part.shape, 1)
            bco[rows, :] = jnp.where(lane // 64 == c, part, 0.0).astype(BF16)

    def project_wide(k, which, cols_=(0, D), keep=None, add=None):
        row = unit_row(k)
        rows, inner = pl.ds(row, 2 * ROWS), pl.ds(cols_[0], cols_[1])
        lanes = pl.ds(which * COLS, COLS)
        part = jnp.dot(buf[rows, inner], w[inner, lanes], preferred_element_type=F32)
        if add is not None:
            part = part + partials[add, :, lanes]
        if keep is not None:
            partials[keep, :, lanes] = part
        elif which == 0:
            xp[pl.ds(pl.multiple_of(row + 16, 16), 2 * ROWS), :] = part.astype(BF16)
        else:
            zs[rows, :] = part.astype(BF16)

    def project(k, cols_=(0, D), keep=None, add=None):
        project_small(k, cols_, keep, add)
        if keep is None:
            share(k, unit_row(k), 2 * ROWS)
        project_wide(k, 0, cols_, keep, add)
        project_wide(k, 1, cols_, keep, add)

    tap_rows = pl.ds(SPAN, 16)
    tap_own = pl.ds(SPAN + 16, 16)
    tap = jnp.concatenate([cbc[...].astype(F32), jnp.zeros((12, 64), F32)], axis=0)
    none = jnp.zeros_like(tap)
    bco[tap_rows, :] = jnp.where(
        c == 0, jnp.concatenate([tap, none], axis=1), jnp.concatenate([none, tap], axis=1)
    ).astype(BF16)
    share(8, SPAN, 16)

    head_lane = lax.broadcasted_iota(jnp.int32, (8, COLS), 1) // HEAD_DIM
    head_sub = lax.broadcasted_iota(jnp.int32, (8, COLS), 0)
    skip_x = sum(jnp.where(head_lane[0:1] == i, skip[i], 0.0) for i in range(8))
    sub256 = lax.broadcasted_iota(jnp.int32, (8, BLOCK), 0)
    bias_r = sum(jnp.where(sub256 == i, bias[i], 0.0) for i in range(8))
    rate_r = sum(jnp.where(sub256 == i, rate[i], 0.0) for i in range(8))

    deep = lax.broadcasted_iota(jnp.int32, (BLOCK, BLOCK), 0)
    summing = jnp.where(deep <= lax.broadcasted_iota(jnp.int32, (BLOCK, BLOCK), 1), 1.0, 0.0)

    def steps(b):
        rows = pl.ds(pl.multiple_of(b * BLOCK, BLOCK), BLOCK)
        turned = small[rows, :].T
        raw = jnp.where(c == 0, turned[64:72], turned[0:8]) + bias_r
        dt = jnp.maximum(raw, 0.0) + jnp.log1p(jnp.exp(-jnp.abs(raw)))
        accum = jnp.dot(
            dt * rate_r, summing, preferred_element_type=F32, precision=lax.Precision.HIGHEST
        )
        end = accum[:, BLOCK - 1 : BLOCK]
        stack = jnp.concatenate(
            [accum, dt, jnp.exp(accum - end) * dt, jnp.exp(-accum), jnp.zeros((96, BLOCK), F32)], axis=0
        )
        cols[rows, :] = stack.T
        rows_a[b] = accum
        total = jnp.sum(jnp.where(head_sub == head_lane, end, 0.0), axis=0, keepdims=True)
        a_x[b] = jnp.broadcast_to(total, (8, COLS))

    def convolve(src, row, lanes, taps, count):
        v = src[pl.ds(row, count + 16), lanes].astype(F32)
        acc = taps[0:1] * v[13 : 13 + count]
        for k in (1, 2, 3):
            acc = acc + taps[k : k + 1] * v[13 + k : 13 + k + count]
        return silu(acc).astype(BF16)

    def over_lanes(column, q, j):
        lane = lax.broadcasted_iota(jnp.int32, (column.shape[0], 128), 1)
        low = q * 8 + 2 * j
        return jnp.where(lane < HEAD_DIM, column[:, low : low + 1], column[:, low + 1 : low + 2])

    taps_x = cx[...].astype(F32)
    head_rows, body_rows = 16, 80

    def conv_x(row, count):
        rows = pl.ds(row, count)
        column = cols[rows, :]
        for j in range(4):
            lanes = slice(128 * j, 128 * j + 128)
            done = convolve(xp, row, lanes, taps_x[:, lanes], count)
            xc[rows, lanes] = done
            value = done.astype(F32)
            dtx[rows, lanes] = (value * over_lanes(column, 1, j)).astype(BF16)
            xt[rows, lanes] = (value * over_lanes(column, 2, j)).astype(BF16)

    def conv_map(index, row, count):
        taps = mp[index, tap_own, :][0:4].astype(F32)
        maps[index, pl.ds(row, count), :] = convolve(mp.at[index], row, slice(0, 128), taps, count)

    def bodies(b, one):
        @pl.loop(0, 3)
        def _(i):
            one(pl.multiple_of(b * BLOCK + 16 + i * body_rows, 16), body_rows)

    def heads(one, low=0, high=4):
        @pl.loop(low, high)
        def _(b):
            one(pl.multiple_of(b * BLOCK, BLOCK), head_rows)

    locals_[1].wait()
    locals_[2].wait()
    st_w[pl.ds(pl.multiple_of((1 - c) * 64, 64), 16), :] = (
        jnp.concatenate([st_dt[...].astype(F32), jnp.zeros((8, D), F32)], axis=0).astype(BF16)
    )

    @pl.loop(0, D // 128)
    def _(j):
        part = pl.ds(pl.multiple_of(j * 128, 128), 128)
        w_small[part, :] = st_w[:, part].T

    landed(bcs.at[tap_rows], sib_s.at[8], sib_r.at[8])
    mp[h, tap_own, :] = bco[tap_rows, :] + bcs[tap_rows, :]
    push(mp.at[h, tap_own], mp.at[h, tap_own], z_s.at[8, 0], z_r.at[8, 0], dev_z)
    locals_[0].wait()
    locals_[3].wait()
    locals_[4].wait()
    arrive(3, y, h, whole, sib=True)
    project(0)
    arrive(1, down, h, part_q)
    send(8, down, h, part_q, dev_z)
    send(9, down, h, part_q, dev_sib)
    arrive(2, up, h, part_q)
    send(11, up, h, part_q, dev_z)
    send(12, up, h, part_q, dev_sib)
    arrive(0, y, n, part_p)
    send(13, y, n, part_p, dev_up)
    send(14, y, n, part_p, dev_down)
    send(7, down, h, q_a, dev_up)
    send(10, up, h, q_b, dev_down)
    send(15, y, n, part_p, dev_sib)
    merge(0)
    arrive(9, down, h, part_q, sib=True)
    project(2, part_q, keep=2)
    arrive(12, up, h, part_q, sib=True)
    project(3, part_q, keep=3)
    arrive(15, y, n, part_p, sib=True)
    project(1, part_p, keep=0)
    arrive(4, y, n, part_q)
    send(16, y, n, part_q, dev_sib)
    arrive(5, down, h, part_p)
    send(21, down, h, p_a, dev_up)
    send(22, down, h, part_p, dev_sib)
    arrive(6, up, h, part_p)
    send(23, up, h, p_b, dev_down)
    send(24, up, h, part_p, dev_sib)
    arrive(16, y, n, part_q, sib=True)
    project(1, part_q, add=0)
    arrive(22, down, h, part_p, sib=True)
    project(2, part_p, add=2)
    arrive(24, up, h, part_p, sib=True)
    project(3, part_p, add=3)
    merge(1)
    steps(y)
    bodies(y, conv_x)
    merge(2)
    merge(3)
    arrive(8, down, n, part_q)
    send(25, down, n, part_q, dev_sib)
    arrive(13, down, n, part_p)
    send(27, down, n, p_a, dev_up)
    send(28, down, n, part_p, dev_sib)
    arrive(14, up, n, part_p)
    send(29, up, n, p_b, dev_down)
    send(30, up, n, part_p, dev_sib)
    arrive(25, down, n, part_q, sib=True)
    arrive(28, down, n, part_p, sib=True)
    project(4)
    arrive(7, far, h, q_a)
    send(17, far, h, q_a, dev_z)
    send(18, far, h, q_a, dev_sib)
    arrive(10, far, h, q_b)
    send(19, far, h, q_b, dev_z)
    send(20, far, h, q_b, dev_sib)
    arrive(30, up, n, part_p, sib=True)
    project(5, part_p, keep=0)
    arrive(11, up, n, part_q)
    send(26, up, n, part_q, dev_sib)
    merge(4)
    arrive(18, far, h, q_a, sib=True)
    arrive(20, far, h, q_b, sib=True)
    project(6, part_q, keep=1)
    arrive(21, far, h, p_a)
    send(33, far, h, p_a, dev_sib)
    arrive(23, far, h, p_b)
    send(34, far, h, p_b, dev_sib)
    arrive(26, up, n, part_q, sib=True)
    project(5, part_q, add=0)
    steps(down)
    bodies(down, conv_x)
    merge(5)
    arrive(17, far, n, q_a)
    send(31, far, n, q_a, dev_sib)
    arrive(33, far, h, p_a, sib=True)
    arrive(34, far, h, p_b, sib=True)
    project(6, part_p, add=1)
    arrive(19, far, n, q_b)
    send(32, far, n, q_b, dev_sib)
    steps(up)
    bodies(up, conv_x)
    merge(6)
    arrive(31, far, n, q_a, sib=True)
    arrive(32, far, n, q_b, sib=True)
    project(7, part_q, keep=1)
    arrive(27, far, n, p_a)
    send(35, far, n, p_a, dev_sib)
    arrive(29, far, n, p_b)
    send(36, far, n, p_b, dev_sib)
    landed(mp.at[n, tap_own], z_s.at[8, 0], z_r.at[8, 0])
    for k in range(6):
        merged_there(k)
    for b in (y, up, down):
        bodies(b, lambda row, count: conv_map(0, row, count))
    arrive(35, far, n, p_a, sib=True)
    arrive(36, far, n, p_b, sib=True)

    project_small(7, part_p, add=1)
    unit = pl.ds(unit_row(7), 2 * ROWS)
    push(bco.at[unit], bcs.at[unit], sib_s.at[7], sib_r.at[7], dev_sib)
    push(bco.at[unit], direct.at[0], z_s.at[7, 0], z_r.at[7, 0], dev_z)
    push(bco.at[unit], direct.at[1], z_s.at[7, 1], z_r.at[7, 1], dev_zsib)
    ending = pl.ds(SPAN - 16, 16)
    for k, (hh, cc) in enumerate(((h, c), (h, 1 - c), (n, c), (n, 1 - c))):
        push(bco.at[ending], halo_in.at[k], halo_s.at[1 + k], halo_r.at[1 + k], span(later, hh, cc))
    project_wide(7, 0, part_p, add=1)
    last, first = pl.ds(SPAN, 16), pl.ds(0, 16)
    push(xp.at[last], xp.at[first], halo_s.at[0], halo_r.at[0], span(later, h, c))
    steps(far)
    decays[x] = a_x[0] + a_x[1] + a_x[2] + a_x[3]
    for d in (1, 2, 3):
        push(decays.at[x], decays.at[x], line_s.at[11 + d], line_r.at[11 + d], on_line[d - 1])
    bodies(far, conv_x)
    heads(conv_x, 1, 4)
    merged_there(6)
    landed(bcs.at[unit], sib_s.at[7], sib_r.at[7])
    mp[h, pl.ds(pl.multiple_of(unit_row(7) + 16, 16), 2 * ROWS), :] = bco[unit, :] + bcs[unit, :]
    landed(direct.at[0], z_s.at[7, 0], z_r.at[7, 0])
    landed(direct.at[1], z_s.at[7, 1], z_r.at[7, 1])
    mp[n, pl.ds(pl.multiple_of(unit_row(7, flip=True) + 16, 16), 2 * ROWS), :] = direct[0] + direct[1]
    landed(xp.at[first], halo_s.at[0], halo_r.at[0])
    for k in range(4):
        landed(halo_in.at[k], halo_s.at[1 + k], halo_r.at[1 + k])
    begun = s > 0
    xp[first, :] = jnp.where(begun, xp[first, :].astype(F32), 0.0).astype(BF16)
    mp[h, first, :] = jnp.where(begun, halo_in[0].astype(F32) + halo_in[1].astype(F32), 0.0).astype(BF16)
    mp[n, first, :] = jnp.where(begun, halo_in[2].astype(F32) + halo_in[3].astype(F32), 0.0).astype(BF16)
    bodies(far, lambda row, count: conv_map(0, row, count))
    heads(conv_x, 0, 1)
    heads(lambda row, count: conv_map(0, row, count))

    state[...] = jnp.zeros_like(state)

    @pl.loop(0, 4)
    def _(b):
        rows = pl.ds(pl.multiple_of(b * BLOCK, BLOCK), BLOCK)
        turned = maps[0, rows, :].T
        b_t[:, rows] = turned
        entry[b] = state[...]
        state[...] = jnp.exp(-a_x[b][0:1]) * state[...] + jnp.dot(
            turned, xt[rows, :], preferred_element_type=F32
        )

    earlier = list(started)
    states[x] = state[...].astype(BF16)
    quarters = [pl.ds(128 * q, 128) for q in range(4)]
    for part, lanes in enumerate(quarters):
        for d in (1, 3, 2):
            ref = states.at[x, :, lanes]
            push(ref, ref, line_s.at[part * 3 + d - 1], line_r.at[part * 3 + d - 1], on_line[d - 1])

    project_wide(7, 1, part_p, add=1)
    for b in (y, up, down, far):
        bodies(b, lambda row, count: conv_map(1, row, count))
    heads(lambda row, count: conv_map(1, row, count))
    pair_lane = lax.broadcasted_iota(jnp.int32, (128, 128), 1)

    @pl.loop(0, 4)
    def _(b):
        start = pl.multiple_of(b * BLOCK, BLOCK)
        rows = pl.ds(start, BLOCK)
        aff[...] = jnp.dot(maps[1, rows, :], b_t[:, rows], preferred_element_type=F32)
        accum = rows_a[b]
        for t in (0, 1):
            reach = 128 * (t + 1)
            here = pl.ds(pl.multiple_of(start + 128 * t, 128), 128)
            near = pl.ds(start, reach)
            keep = (
                lax.broadcasted_iota(jnp.int32, (128, reach), 0) + 128 * t
                >= lax.broadcasted_iota(jnp.int32, (128, reach), 1)
            )
            column = cols[here, :]
            for j in range(4):
                lanes = slice(128 * j, 128 * j + 128)
                weights = [
                    jnp.where(
                        keep,
                        aff[128 * t : 128 * t + 128, 0:reach]
                        * jnp.exp(accum[i : i + 1, 0:reach] - column[:, i : i + 1]),
                        0.0,
                    ).astype(BF16)
                    for i in (2 * j, 2 * j + 1)
                ]
                both = jnp.dot(
                    jnp.concatenate(weights, axis=0), dtx[near, lanes], preferred_element_type=F32
                )
                yloc[here, lanes] = (
                    jnp.where(pair_lane < HEAD_DIM, both[0:128], both[128:256])
                    + skip_x[:, lanes] * xc[here, lanes].astype(F32)
                )

    for d in (1, 2, 3):
        index = (x + 4 - d) % 4
        landed(decays.at[index], line_s.at[11 + d], line_r.at[11 + d])
    for part, lanes in enumerate(quarters):
        for d in (1, 3, 2):
            landed(
                states.at[(x + 4 - d) % 4, :, lanes], line_s.at[part * 3 + d - 1], line_r.at[part * 3 + d - 1]
            )
        total = jnp.zeros((STATE, 128), F32)
        for j in range(4):
            total = jnp.exp(-decays[j, 0:1, lanes]) * total + states[j, :, lanes].astype(F32)
        t_out[:, lanes] = total.astype(BF16)
        push(t_out.at[:, lanes], t_in.at[:, lanes], t_s.at[part], t_r.at[part], across)
    sent(*earlier)
    for part, lanes in enumerate(quarters):
        total = jnp.zeros((STATE, 128), F32)
        passed = jnp.zeros((1, 128), F32)
        for j in range(4):
            taken = jnp.where(j < x, 1.0, 0.0)
            through = jnp.where(j < x, jnp.exp(-decays[j, 0:1, lanes]), 1.0)
            total = through * total + taken * states[j, :, lanes].astype(F32)
            passed = passed + taken * decays[j, 0:1, lanes]
        landed(t_in.at[:, lanes], t_s.at[part], t_r.at[part])
        state[:, lanes] = total + jnp.where(line == 1, jnp.exp(-passed), 0.0) * t_in[:, lanes].astype(F32)

    sent(*list(started))
    gain_r = gain[...].astype(F32).reshape(1, COLS)

    def gate(b, half):
        rows = pl.ds(pl.multiple_of(b * BLOCK + half * 128, 128), 128)
        ahead = sum(jnp.where(i < b, 1.0, 0.0) * a_x[i][0:1] for i in range(3))
        squares = jnp.zeros((128, 128), F32)
        column = cols[rows, :]
        for j in range(4):
            lanes = slice(128 * j, 128 * j + 128)
            entering = entry[b, :, lanes] + jnp.exp(-ahead[:, lanes]) * state[:, lanes]
            far_y = jnp.dot(maps[1, rows, :], entering.astype(BF16), preferred_element_type=F32)
            value = yloc[rows, lanes] + far_y * over_lanes(column, 3, j)
            value = value * silu(zs[rows, lanes].astype(F32))
            squares = squares + value * value
            g[rows, lanes] = (value * gain_r[:, lanes]).astype(BF16)
        buf[rows, pl.ds(D, 128)] = jnp.broadcast_to(
            jnp.sum(squares, axis=1, keepdims=True), (128, 128)
        ).astype(BF16)

    locals_[5].wait()
    reduce_stage(gate, g, w_o, out, buf, *reduce_refs)


def reduce_stage(
    gate, g, w_out, out, o, sib, zq, pa, pb, qa, qb, pf, qf, zp, sends, recvs
):
    s, y, h, c = place()
    up, down, far = (y + 1) % 4, (y + 3) % 4, (y + 2) % 4
    dev = lambda yy, hh, cc: (s, yy * 4 + hh * 2 + cc)
    dev_up, dev_down, dev_z, dev_sib = dev(up, h, c), dev(down, h, c), dev(y, 1 - h, c), dev(y, h, 1 - c)
    wide_q = WIDE - SPLIT
    part_p, part_q = (0, SPLIT), (SPLIT, wide_q)
    p_a, p_b = (0, HALF_P), (HALF_P, SPLIT - HALF_P)
    q_a, q_b = (SPLIT, HALF_Q), (SPLIT + HALF_Q, wide_q - HALF_Q)
    started = []

    def at(yy, hh, cc, cols):
        row = pl.multiple_of((yy * 4 + hh * 2 + cc) * ROWS, ROWS)
        return o.at[pl.ds(row, ROWS), pl.ds(cols[0], cols[1])]

    def copy_of(k, src, dst, to):
        return pltpu.make_async_remote_copy(
            src_ref=src, dst_ref=dst, send_sem=sends.at[k], recv_sem=recvs.at[k],
            device_id=to, device_id_type=MESH,
        )

    def send(k, src, dst, to):
        copy = copy_of(k, src, dst, to)
        copy.start()
        started.append(copy)
        return copy

    def arrive(k, ref):
        copy_of(k, ref, ref, dev_sib).wait_recv()

    def add(yy, hh, cols, ref):
        target = at(yy, hh, c, cols)

        @pl.loop(0, ROWS // 16)
        def _(i):
            rows = pl.ds(pl.multiple_of(i * 16, 16), 16)
            target[rows, :] = (target[rows, :].astype(F32) + ref[rows, :].astype(F32)).astype(BF16)

    def chip(yy, hh):
        return yy * 2 + hh

    def partial(yy, hh, k, cols=(0, WIDE)):
        row = pl.multiple_of((yy * 4 + hh * 2) * ROWS, 2 * ROWS)
        rows = pl.ds(row, 2 * ROWS)
        left = g[rows, :]
        low, high = cols[0], min(D, cols[0] + cols[1])
        pieces = -(-(high - low) // 1792)
        width = (high - low) // pieces
        for j in range(pieces):
            part = pl.ds(low + j * width, width)
            o[rows, part] = jnp.dot(left, w_out[:, part], preferred_element_type=F32).astype(BF16)
        send(k, at(yy, hh, 1 - c, cols), sib.at[chip(yy, hh), :, pl.ds(cols[0], cols[1])], dev_sib)

    def joined(yy, hh, k, cols=(0, WIDE)):
        ref = sib.at[chip(yy, hh), :, pl.ds(cols[0], cols[1])]
        arrive(k, ref)
        add(yy, hh, cols, ref)

    def in_q(cols):
        return pl.ds(cols[0] - SPLIT, cols[1])

    def in_p(cols):
        return pl.ds(cols[0], cols[1])

    n = 1 - h
    gate(far, n)
    partial(far, n, 0, p_a)
    partial(far, n, 32, p_b)
    partial(far, n, 31, part_q)
    gate(up, n)
    joined(far, n, 0, p_a)
    send(8, at(far, n, c, p_a), pa.at[n], dev_up)
    joined(far, n, 32, p_b)
    send(9, at(far, n, c, p_b), pb.at[n], dev_down)
    partial(up, n, 2)
    gate(down, n)
    joined(far, n, 31, part_q)
    send(10, at(far, n, c, part_q), zq.at[far], dev_z)
    partial(down, n, 3)
    joined(up, n, 2)
    send(11, at(up, n, c, p_b), pf.at[0, n, :, in_p(p_b)], dev_up)
    send(13, at(up, n, c, part_q), zq.at[up], dev_z)
    gate(far, h)
    partial(far, h, 1)
    joined(down, n, 3)
    send(12, at(down, n, c, p_a), pf.at[1, n, :, in_p(p_a)], dev_down)
    send(14, at(down, n, c, part_q), zq.at[down], dev_z)
    gate(up, h)
    partial(up, h, 4)
    joined(far, h, 1)
    arrive(8, pa.at[n])
    add(up, n, p_a, pa.at[n])
    send(15, at(up, n, c, p_a), pf.at[0, n, :, in_p(p_a)], dev_up)
    arrive(9, pb.at[n])
    add(down, n, p_b, pb.at[n])
    send(16, at(down, n, c, p_b), pf.at[1, n, :, in_p(p_b)], dev_down)
    send(17, at(far, h, c, p_a), pa.at[h], dev_up)
    send(18, at(far, h, c, p_b), pb.at[h], dev_down)
    gate(down, h)
    partial(down, h, 5)
    joined(up, h, 4)
    send(19, at(up, h, c, p_b), pf.at[0, h, :, in_p(p_b)], dev_up)
    gate(y, n)
    partial(y, n, 6)
    joined(down, h, 5)
    send(20, at(down, h, c, p_a), pf.at[1, h, :, in_p(p_a)], dev_down)
    gate(y, h)
    partial(y, h, 7)
    joined(y, n, 6)
    send(21, at(y, n, c, part_q), zq.at[y], dev_z)
    arrive(10, zq.at[far])
    add(far, h, part_q, zq.at[far])
    joined(y, h, 7)
    arrive(11, pf.at[0, n, :, in_p(p_b)])
    arrive(15, pf.at[0, n, :, in_p(p_a)])
    add(y, n, part_p, pf.at[0, n])
    arrive(12, pf.at[1, n, :, in_p(p_a)])
    arrive(16, pf.at[1, n, :, in_p(p_b)])
    add(y, n, part_p, pf.at[1, n])
    send(24, at(y, n, c, part_p), zp, dev_z)
    arrive(17, pa.at[h])
    add(up, h, p_a, pa.at[h])
    send(22, at(up, h, c, p_a), pf.at[0, h, :, in_p(p_a)], dev_up)
    arrive(18, pb.at[h])
    add(down, h, p_b, pb.at[h])
    send(23, at(down, h, c, p_b), pf.at[1, h, :, in_p(p_b)], dev_down)
    send(25, at(far, h, c, q_a), qa, dev_up)
    send(26, at(far, h, c, q_b), qb, dev_down)
    arrive(13, zq.at[up])
    add(up, h, part_q, zq.at[up])
    send(27, at(up, h, c, q_b), qf.at[0, :, in_q(q_b)], dev_up)
    arrive(14, zq.at[down])
    add(down, h, part_q, zq.at[down])
    send(28, at(down, h, c, q_a), qf.at[1, :, in_q(q_a)], dev_down)
    arrive(19, pf.at[0, h, :, in_p(p_b)])
    arrive(22, pf.at[0, h, :, in_p(p_a)])
    add(y, h, part_p, pf.at[0, h])
    arrive(20, pf.at[1, h, :, in_p(p_a)])
    arrive(23, pf.at[1, h, :, in_p(p_b)])
    add(y, h, part_p, pf.at[1, h])
    arrive(25, qa)
    add(up, h, q_a, qa)
    send(29, at(up, h, c, q_a), qf.at[0, :, in_q(q_a)], dev_up)
    arrive(26, qb)
    add(down, h, q_b, qb)
    send(30, at(down, h, c, q_b), qf.at[1, :, in_q(q_b)], dev_down)
    arrive(21, zq.at[y])
    arrive(27, qf.at[0, :, in_q(q_b)])
    arrive(28, qf.at[1, :, in_q(q_a)])
    arrive(29, qf.at[0, :, in_q(q_a)])
    arrive(30, qf.at[1, :, in_q(q_b)])
    mine_q = at(y, h, c, part_q)
    mine_p = at(y, h, c, part_p)
    terms = (mine_q, zq.at[y], qf.at[0], qf.at[1])
    lane = pl.ds(D - SPLIT, 128)
    squares = sum(t[:, lane].astype(F32) for t in terms)
    scale = lax.rsqrt(squares / (COLS * 16) + 1e-05)

    @pl.loop(0, (D - SPLIT) // 128)
    def _(j):
        cols = pl.ds(pl.multiple_of(j * 128, 128), 128)
        total = sum(t[:, cols].astype(F32) for t in terms)
        out[:, pl.ds(pl.multiple_of(SPLIT + j * 128, 128), 128)] = (total * scale).astype(BF16)

    arrive(24, zp)

    @pl.loop(0, SPLIT // 128)
    def _(j):
        cols = pl.ds(pl.multiple_of(j * 128, 128), 128)
        total = mine_p[:, cols].astype(F32) + zp[:, cols].astype(F32)
        out[:, cols] = (total * scale).astype(BF16)

    for copy in started:
        copy.wait_send()


def mix(tokens, w_x, w_z, w_bc, w_dt, conv_x, conv_bc, dt_bias, decay_rate, skip, norm_gain, w_out):
    anywhere = pl.BlockSpec(memory_space=pl.ANY)
    vmem = pl.BlockSpec(memory_space=pltpu.VMEM)
    smem = pl.BlockSpec(memory_space=pltpu.SMEM)
    wide_q = WIDE - SPLIT
    dma = pltpu.SemaphoreType.DMA
    return pl.pallas_call(
        mixer_kernel,
        out_shape=jax.ShapeDtypeStruct((ROWS, D), BF16),
        in_specs=[anywhere] * 5 + [vmem, vmem, smem, smem, smem, vmem, anywhere],
        out_specs=vmem,
        scratch_shapes=[
            pltpu.VMEM((SPAN, WIDE), BF16),
            pltpu.VMEM((4, 2 * ROWS, 2 * COLS + 128), F32),
            pltpu.VMEM((D, 2 * COLS), BF16),
            pltpu.VMEM((D, 128), BF16),
            pltpu.VMEM((128, D), BF16),
            pltpu.VMEM((8, D), BF16),
            pltpu.VMEM((SPAN + 16, COLS), BF16),
            pltpu.VMEM((SPAN, COLS), BF16),
            pltpu.VMEM((SPAN, 128), F32),
            pltpu.VMEM((SPAN + 16, 128), BF16),
            pltpu.VMEM((SPAN + 16, 128), BF16),
            pltpu.VMEM((2, SPAN + 32, 128), BF16),
            pltpu.VMEM((2, 2 * ROWS, 128), BF16),
            pltpu.VMEM((4, 16, 128), BF16),
            pltpu.VMEM((2, SPAN, 128), BF16),
            pltpu.VMEM((STATE, SPAN), BF16),
            pltpu.VMEM((SPAN, COLS), BF16),
            pltpu.VMEM((SPAN, COLS), BF16),
            pltpu.VMEM((SPAN, COLS), BF16),
            pltpu.VMEM((SPAN, COLS), F32),
            pltpu.VMEM((SPAN, 128), F32),
            pltpu.VMEM((4, 8, BLOCK), F32),
            pltpu.VMEM((4, 8, COLS), F32),
            pltpu.VMEM((BLOCK, BLOCK), F32),
            pltpu.VMEM((4, STATE, COLS), F32),
            pltpu.VMEM((STATE, COLS), F32),
            pltpu.VMEM((4, STATE, COLS), BF16),
            pltpu.VMEM((4, 8, COLS), F32),
            pltpu.VMEM((STATE, COLS), BF16),
            pltpu.VMEM((STATE, COLS), BF16),
            dma((37,)), dma((37,)), dma((6,)), dma((9,)), dma((9,)), dma((9, 2)), dma((9, 2)),
            dma((5,)), dma((5,)), dma((15,)), dma((15,)), dma((4,)), dma((4,)),
            pltpu.VMEM((SPAN, COLS), BF16),
            pltpu.VMEM((COLS, D), BF16),
            pltpu.VMEM((8, ROWS, WIDE), BF16),
            pltpu.VMEM((4, ROWS, wide_q), BF16),
            pltpu.VMEM((2, ROWS, HALF_P), BF16),
            pltpu.VMEM((2, ROWS, SPLIT - HALF_P), BF16),
            pltpu.VMEM((ROWS, HALF_Q), BF16),
            pltpu.VMEM((ROWS, wide_q - HALF_Q), BF16),
            pltpu.VMEM((2, 2, ROWS, SPLIT), BF16),
            pltpu.VMEM((2, ROWS, wide_q), BF16),
            pltpu.VMEM((ROWS, SPLIT), BF16),
            pltpu.SemaphoreType.DMA((33,)),
            pltpu.SemaphoreType.DMA((33,)),
        ],
        compiler_params=pltpu.CompilerParams(
            collective_id=1, has_side_effects=True, vmem_limit_bytes=63 << 20
        ),
        name="mix",
    )(
        tokens, w_x, w_z, w_bc.T, w_dt.T, conv_x, conv_bc, dt_bias,
        decay_rate, skip, norm_gain, w_out,
    )


def on_device(
    tokens, w_x, w_z, w_bc, w_dt, conv_x, conv_bc, dt_bias, decay_rate, skip, norm_gain, w_out
):
    return mix(
        tokens, w_x, w_z, w_bc, w_dt, conv_x, conv_bc, dt_bias, decay_rate, skip, norm_gain, w_out
    )


def solution(mesh):
    placed = (
        P(("seq", "tp"), None),
        P(None, "tp"),
        P(None, "tp"),
        P(None, "tp"),
        P(None, "tp"),
        P(None, "tp"),
        P(None, "tp"),
        P("tp"),
        P("tp"),
        P("tp"),
        P("tp"),
        P("tp", None),
    )
    return jax.shard_map(
        on_device, mesh=mesh, in_specs=placed, out_specs=P(("seq", "tp"), None), check_vma=False
    )
```

```python
import jax
import jax.numpy as jnp
from jax import lax
from jax.experimental import pallas as pl
from jax.experimental.pallas import tpu as pltpu
from jax.sharding import PartitionSpec as P

HEAD_DIM = 64
STATE = 128
BLOCK = 256
MESH = pl.DeviceIdType.MESH
F32 = jnp.float32
BF16 = jnp.bfloat16

D = 6144
ROWS = 64
SPAN = 1024
COLS = 512
SPLIT = 3584
HALF_P = SPLIT // 2
HALF_Q = 1280
WIDE = D + 128
SPLIT_IN = 3840
HALF_P_IN = SPLIT_IN // 2
HALF_Q_IN = (D - SPLIT_IN) // 2


def place():
    tp = lax.axis_index("tp")
    return lax.axis_index("seq"), tp // 4, tp // 2 % 2, tp % 2


def greet(peers):
    barrier = pltpu.get_barrier_semaphore()
    for peer in peers:
        pl.semaphore_signal(barrier, inc=1, device_id=peer, device_id_type=MESH)
    pl.semaphore_wait(barrier, len(peers))


def silu(v):
    return v / (1.0 + jnp.exp(-v))


def mixer_kernel(
    tok, wx, wz, wbc, wdt, cx, cbc, bias, rate, skip, gain, w_out, out,
    buf, partials, w, w_small, st_w, st_dt, xp, zs, small, bco, bcs, mp, direct, halo_in, maps, b_t, xc, dtx, xt,
    yloc, cols, rows_a, a_x, aff, entry, state, states, decays, t_out, t_in,
    sends, recvs, locs, sib_s, sib_r, z_s, z_r, halo_s, halo_r, line_s, line_r, t_s, t_r,
    g, w_o, *reduce_refs,
):
    s, y, h, c = place()
    up, down, far = (y + 1) % 4, (y + 3) % 4, (y + 2) % 4
    n = 1 - h
    line, x = s // 4, s % 4
    dev = lambda yy, hh, cc: (s, yy * 4 + hh * 2 + cc)
    span = lambda ss, hh, cc: (ss, y * 4 + hh * 2 + cc)
    dev_up, dev_down, dev_z, dev_sib = dev(up, h, c), dev(down, h, c), dev(y, n, c), dev(y, h, 1 - c)
    dev_zsib = dev(y, n, 1 - c)
    later, before = (s + 1) % 8, (s + 7) % 8
    on_line = [span(line * 4 + (x + d) % 4, h, c) for d in (1, 2, 3)]
    across = span((1 - line) * 4 + x, h, c)
    part_p, part_q = (0, SPLIT_IN), (SPLIT_IN, D - SPLIT_IN)
    p_a, p_b = (0, HALF_P_IN), (HALF_P_IN, HALF_P_IN)
    q_a, q_b = (SPLIT_IN, HALF_Q_IN), (SPLIT_IN + HALF_Q_IN, HALF_Q_IN)
    whole = (0, D)
    p_one, p_two, p_rest = (0, 1280), (2560, 1280), (1280, 1280)
    rest_a, rest_b = (1280, 640), (1920, 640)

    def at(yy, hh, cc, cols_):
        row = pl.multiple_of((yy * 4 + hh * 2 + cc) * ROWS, ROWS)
        return buf.at[pl.ds(row, ROWS), pl.ds(cols_[0], cols_[1])]

    started = []

    def remote(src, dst, send_sem, recv_sem, to):
        return pltpu.make_async_remote_copy(
            src_ref=src, dst_ref=dst, send_sem=send_sem, recv_sem=recv_sem,
            device_id=to, device_id_type=MESH,
        )

    def push(src, dst, send_sem, recv_sem, to):
        copy = remote(src, dst, send_sem, recv_sem, to)
        copy.start()
        started.append(copy)
        return copy

    def sent(*copies):
        for copy in copies:
            copy.wait_send()
            started[:] = [other for other in started if other is not copy]

    def landed(ref, send_sem, recv_sem):
        remote(ref, ref, send_sem, recv_sem, dev_sib).wait_recv()

    def send(k, yy, hh, cols_, to, own=False):
        dst = at(yy, hh, c, cols_)
        src = tok.at[:, pl.ds(cols_[0], cols_[1])] if own else dst
        return push(src, dst, sends.at[k], recvs.at[k], to)

    def arrive(k, yy, hh, cols_, sib=False):
        landed(at(yy, hh, 1 - c if sib else c, cols_), sends.at[k], recvs.at[k])

    tall = pl.ds(pl.multiple_of(c * 64, 64), 64)
    locals_ = [
        pltpu.make_async_copy(tok, at(y, h, c, whole), locs.at[0]),
        pltpu.make_async_copy(wbc, st_w.at[tall], locs.at[1]),
        pltpu.make_async_copy(wdt, st_dt, locs.at[2]),
        pltpu.make_async_copy(wx, w.at[:, pl.ds(0, COLS)], locs.at[3]),
        pltpu.make_async_copy(wz, w.at[:, pl.ds(COLS, COLS)], locs.at[4]),
        pltpu.make_async_copy(w_out, w_o, locs.at[5]),
    ]
    st_w[...] = jnp.zeros_like(st_w)
    for copy in locals_:
        copy.start()
    greet(
        [dev_up, dev_down, dev_z, dev_sib, dev_zsib, across]
        + on_line
        + [span(later, hh, cc) for hh in (h, n) for cc in (c, 1 - c)]
        + [span(before, hh, cc) for hh in (h, n) for cc in (c, 1 - c)]
    )
    send(0, y, h, part_p, dev_z, own=True)
    send(1, y, h, part_q, dev_up, own=True)
    send(2, y, h, part_q, dev_down, own=True)
    send(3, y, h, whole, dev_sib, own=True)
    send(5, y, h, part_p, dev_up, own=True)
    send(6, y, h, part_p, dev_down, own=True)
    send(4, y, h, part_q, dev_z, own=True)

    units = [(y, h), (y, n), (down, h), (up, h), (down, n), (up, n), (far, h), (far, n)]

    def unit_row(k, flip=False):
        yy, hh = units[k]
        return pl.multiple_of((yy * 4 + (1 - hh if flip else hh) * 2) * ROWS, 2 * ROWS)

    def share(k, row, count):
        rows = pl.ds(row, count)
        push(bco.at[rows], bcs.at[rows], sib_s.at[k], sib_r.at[k], dev_sib)

    def merge(k):
        row = unit_row(k)
        rows = pl.ds(row, 2 * ROWS)
        landed(bcs.at[rows], sib_s.at[k], sib_r.at[k])
        mp[h, pl.ds(pl.multiple_of(row + 16, 16), 2 * ROWS), :] = bco[rows, :] + bcs[rows, :]
        half = pl.ds(pl.multiple_of(row + 16 + c * ROWS, 16), ROWS)
        push(mp.at[h, half], mp.at[h, half], z_s.at[k, 0], z_r.at[k, 0], dev_z)
        push(mp.at[h, half], mp.at[h, half], z_s.at[k, 1], z_r.at[k, 1], dev_zsib)

    def merged_there(k):
        row = unit_row(k, flip=True)
        for rel, core in ((0, c), (1, 1 - c)):
            ref = mp.at[n, pl.ds(pl.multiple_of(row + 16 + core * ROWS, 16), ROWS)]
            landed(ref, z_s.at[k, rel], z_r.at[k, rel])

    def project_small(k, cols_=(0, D), keep=None, add=None):
        row = unit_row(k)
        rows, inner = pl.ds(row, 2 * ROWS), pl.ds(cols_[0], cols_[1])
        part = jnp.dot(buf[rows, inner], w_small[inner, :], preferred_element_type=F32)
        if add is not None:
            part = part + partials[add, :, 2 * COLS : 2 * COLS + 128]
        if keep is not None:
            partials[keep, :, 2 * COLS : 2 * COLS + 128] = part
        else:
            small[rows, :] = part
            lane = lax.broadcasted_iota(jnp.int32, part.shape, 1)
            bco[rows, :] = jnp.where(lane // 64 == c, part, 0.0).astype(BF16)

    def project_wide(k, which, cols_=(0, D), keep=None, add=None):
        row = unit_row(k)
        rows, inner = pl.ds(row, 2 * ROWS), pl.ds(cols_[0], cols_[1])
        lanes = pl.ds(which * COLS, COLS)
        part = jnp.dot(buf[rows, inner], w[inner, lanes], preferred_element_type=F32)
        if add is not None:
            part = part + partials[add, :, lanes]
        if keep is not None:
            partials[keep, :, lanes] = part
        elif which == 0:
            xp[pl.ds(pl.multiple_of(row + 16, 16), 2 * ROWS), :] = part.astype(BF16)
        else:
            zs[rows, :] = part.astype(BF16)

    def project(k, cols_=(0, D), keep=None, add=None):
        project_small(k, cols_, keep, add)
        if keep is None:
            share(k, unit_row(k), 2 * ROWS)
        project_wide(k, 0, cols_, keep, add)
        project_wide(k, 1, cols_, keep, add)

    tap_rows = pl.ds(SPAN, 16)
    tap_own = pl.ds(SPAN + 16, 16)
    tap = jnp.concatenate([cbc[...].astype(F32), jnp.zeros((12, 64), F32)], axis=0)
    none = jnp.zeros_like(tap)
    bco[tap_rows, :] = jnp.where(
        c == 0, jnp.concatenate([tap, none], axis=1), jnp.concatenate([none, tap], axis=1)
    ).astype(BF16)
    share(8, SPAN, 16)

    head_lane = lax.broadcasted_iota(jnp.int32, (8, COLS), 1) // HEAD_DIM
    head_sub = lax.broadcasted_iota(jnp.int32, (8, COLS), 0)
    skip_x = sum(jnp.where(head_lane[0:1] == i, skip[i], 0.0) for i in range(8))
    sub256 = lax.broadcasted_iota(jnp.int32, (8, BLOCK), 0)
    bias_r = sum(jnp.where(sub256 == i, bias[i], 0.0) for i in range(8))
    rate_r = sum(jnp.where(sub256 == i, rate[i], 0.0) for i in range(8))

    deep = lax.broadcasted_iota(jnp.int32, (BLOCK, BLOCK), 0)
    summing = jnp.where(deep <= lax.broadcasted_iota(jnp.int32, (BLOCK, BLOCK), 1), 1.0, 0.0)

    def steps(b):
        rows = pl.ds(pl.multiple_of(b * BLOCK, BLOCK), BLOCK)
        turned = small[rows, :].T
        raw = jnp.where(c == 0, turned[64:72], turned[0:8]) + bias_r
        dt = jnp.maximum(raw, 0.0) + jnp.log1p(jnp.exp(-jnp.abs(raw)))
        accum = jnp.dot(
            dt * rate_r, summing, preferred_element_type=F32, precision=lax.Precision.HIGHEST
        )
        end = accum[:, BLOCK - 1 : BLOCK]
        stack = jnp.concatenate(
            [accum, dt, jnp.exp(accum - end) * dt, jnp.exp(-accum), jnp.zeros((96, BLOCK), F32)], axis=0
        )
        cols[rows, :] = stack.T
        rows_a[b] = accum
        total = jnp.sum(jnp.where(head_sub == head_lane, end, 0.0), axis=0, keepdims=True)
        a_x[b] = jnp.broadcast_to(total, (8, COLS))

    def convolve(src, row, lanes, taps, count):
        v = src[pl.ds(row, count + 16), lanes].astype(F32)
        acc = taps[0:1] * v[13 : 13 + count]
        for k in (1, 2, 3):
            acc = acc + taps[k : k + 1] * v[13 + k : 13 + k + count]
        return silu(acc).astype(BF16)

    def over_lanes(column, q, j):
        lane = lax.broadcasted_iota(jnp.int32, (column.shape[0], 128), 1)
        low = q * 8 + 2 * j
        return jnp.where(lane < HEAD_DIM, column[:, low : low + 1], column[:, low + 1 : low + 2])

    taps_x = cx[...].astype(F32)
    head_rows, body_rows = 16, 80

    def conv_x(row, count):
        rows = pl.ds(row, count)
        column = cols[rows, :]
        for j in range(4):
            lanes = slice(128 * j, 128 * j + 128)
            done = convolve(xp, row, lanes, taps_x[:, lanes], count)
            xc[rows, lanes] = done
            value = done.astype(F32)
            dtx[rows, lanes] = (value * over_lanes(column, 1, j)).astype(BF16)
            xt[rows, lanes] = (value * over_lanes(column, 2, j)).astype(BF16)

    def conv_map(index, row, count):
        taps = mp[index, tap_own, :][0:4].astype(F32)
        maps[index, pl.ds(row, count), :] = convolve(mp.at[index], row, slice(0, 128), taps, count)

    def bodies(b, one):
        @pl.loop(0, 3)
        def _(i):
            one(pl.multiple_of(b * BLOCK + 16 + i * body_rows, 16), body_rows)

    def heads(one, low=0, high=4):
        @pl.loop(low, high)
        def _(b):
            one(pl.multiple_of(b * BLOCK, BLOCK), head_rows)

    locals_[1].wait()
    locals_[2].wait()
    st_w[pl.ds(pl.multiple_of((1 - c) * 64, 64), 16), :] = (
        jnp.concatenate([st_dt[...].astype(F32), jnp.zeros((8, D), F32)], axis=0).astype(BF16)
    )

    @pl.loop(0, D // 128)
    def _(j):
        part = pl.ds(pl.multiple_of(j * 128, 128), 128)
        w_small[part, :] = st_w[:, part].T

    landed(bcs.at[tap_rows], sib_s.at[8], sib_r.at[8])
    mp[h, tap_own, :] = bco[tap_rows, :] + bcs[tap_rows, :]
    push(mp.at[h, tap_own], mp.at[h, tap_own], z_s.at[8, 0], z_r.at[8, 0], dev_z)
    locals_[0].wait()
    locals_[3].wait()
    locals_[4].wait()
    arrive(3, y, h, whole, sib=True)
    project(0)
    arrive(1, down, h, part_q)
    send(8, down, h, part_q, dev_z)
    send(9, down, h, part_q, dev_sib)
    arrive(2, up, h, part_q)
    send(11, up, h, part_q, dev_z)
    send(12, up, h, part_q, dev_sib)
    arrive(0, y, n, part_p)
    send(13, y, n, part_p, dev_up)
    send(14, y, n, part_p, dev_down)
    send(7, down, h, q_a, dev_up)
    send(10, up, h, q_b, dev_down)
    send(15, y, n, part_p, dev_sib)
    merge(0)
    arrive(9, down, h, part_q, sib=True)
    project(2, part_q, keep=2)
    arrive(12, up, h, part_q, sib=True)
    project(3, part_q, keep=3)
    arrive(15, y, n, part_p, sib=True)
    project(1, part_p, keep=0)
    arrive(4, y, n, part_q)
    send(16, y, n, part_q, dev_sib)
    arrive(5, down, h, part_p)
    send(21, down, h, p_a, dev_up)
    send(22, down, h, part_p, dev_sib)
    arrive(6, up, h, part_p)
    send(23, up, h, p_b, dev_down)
    send(24, up, h, part_p, dev_sib)
    arrive(16, y, n, part_q, sib=True)
    project(1, part_q, add=0)
    arrive(22, down, h, part_p, sib=True)
    project(2, part_p, add=2)
    arrive(24, up, h, part_p, sib=True)
    project(3, part_p, add=3)
    merge(1)
    steps(y)
    bodies(y, conv_x)
    merge(2)
    merge(3)
    arrive(8, down, n, part_q)
    send(25, down, n, part_q, dev_sib)
    arrive(13, down, n, part_p)
    send(27, down, n, p_one, dev_up)
    send(37, down, n, rest_a, dev_up)
    send(28, down, n, part_p, dev_sib)
    arrive(14, up, n, part_p)
    send(29, up, n, p_two, dev_down)
    send(38, up, n, rest_b, dev_down)
    send(30, up, n, part_p, dev_sib)
    arrive(25, down, n, part_q, sib=True)
    arrive(28, down, n, part_p, sib=True)
    project(4)
    arrive(7, far, h, q_a)
    send(17, far, h, q_a, dev_z)
    send(18, far, h, q_a, dev_sib)
    arrive(10, far, h, q_b)
    send(19, far, h, q_b, dev_z)
    send(20, far, h, q_b, dev_sib)
    arrive(30, up, n, part_p, sib=True)
    project(5, part_p, keep=0)
    arrive(11, up, n, part_q)
    send(26, up, n, part_q, dev_sib)
    merge(4)
    arrive(18, far, h, q_a, sib=True)
    arrive(20, far, h, q_b, sib=True)
    project(6, part_q, keep=1)
    arrive(21, far, h, p_a)
    send(33, far, h, p_a, dev_sib)
    arrive(23, far, h, p_b)
    send(34, far, h, p_b, dev_sib)
    arrive(26, up, n, part_q, sib=True)
    project(5, part_q, add=0)
    steps(down)
    bodies(down, conv_x)
    merge(5)
    arrive(17, far, n, q_a)
    send(31, far, n, q_a, dev_sib)
    arrive(33, far, h, p_a, sib=True)
    arrive(34, far, h, p_b, sib=True)
    project(6, part_p, add=1)
    arrive(19, far, n, q_b)
    send(32, far, n, q_b, dev_sib)
    steps(up)
    bodies(up, conv_x)
    merge(6)
    arrive(31, far, n, q_a, sib=True)
    arrive(32, far, n, q_b, sib=True)
    project(7, part_q, keep=1)
    arrive(27, far, n, p_one)
    send(35, far, n, p_one, dev_sib)
    arrive(29, far, n, p_two)
    send(36, far, n, p_two, dev_sib)
    landed(mp.at[n, tap_own], z_s.at[8, 0], z_r.at[8, 0])
    for k in range(6):
        merged_there(k)
    for b in (y, up, down):
        bodies(b, lambda row, count: conv_map(0, row, count))
    arrive(37, far, n, rest_a)
    send(39, far, n, rest_a, dev_sib)
    arrive(38, far, n, rest_b)
    send(40, far, n, rest_b, dev_sib)
    arrive(35, far, n, p_one, sib=True)
    project(7, p_one, keep=1, add=1)
    arrive(36, far, n, p_two, sib=True)
    project(7, p_two, keep=1, add=1)
    arrive(39, far, n, rest_a, sib=True)
    arrive(40, far, n, rest_b, sib=True)

    project_small(7, p_rest, add=1)
    unit = pl.ds(unit_row(7), 2 * ROWS)
    push(bco.at[unit], bcs.at[unit], sib_s.at[7], sib_r.at[7], dev_sib)
    push(bco.at[unit], direct.at[0], z_s.at[7, 0], z_r.at[7, 0], dev_z)
    push(bco.at[unit], direct.at[1], z_s.at[7, 1], z_r.at[7, 1], dev_zsib)
    ending = pl.ds(SPAN - 16, 16)
    for k, (hh, cc) in enumerate(((h, c), (h, 1 - c), (n, c), (n, 1 - c))):
        push(bco.at[ending], halo_in.at[k], halo_s.at[1 + k], halo_r.at[1 + k], span(later, hh, cc))
    project_wide(7, 0, p_rest, add=1)
    last, first = pl.ds(SPAN, 16), pl.ds(0, 16)
    push(xp.at[last], xp.at[first], halo_s.at[0], halo_r.at[0], span(later, h, c))
    steps(far)
    decays[x] = a_x[0] + a_x[1] + a_x[2] + a_x[3]
    for d in (1, 2, 3):
        push(decays.at[x], decays.at[x], line_s.at[11 + d], line_r.at[11 + d], on_line[d - 1])
    bodies(far, conv_x)
    heads(conv_x, 1, 4)
    project_wide(7, 1, p_rest, add=1)
    for b in (y, up, down):
        bodies(b, lambda row, count: conv_map(1, row, count))
    merged_there(6)
    landed(bcs.at[unit], sib_s.at[7], sib_r.at[7])
    mp[h, pl.ds(pl.multiple_of(unit_row(7) + 16, 16), 2 * ROWS), :] = bco[unit, :] + bcs[unit, :]
    landed(direct.at[0], z_s.at[7, 0], z_r.at[7, 0])
    landed(direct.at[1], z_s.at[7, 1], z_r.at[7, 1])
    mp[n, pl.ds(pl.multiple_of(unit_row(7, flip=True) + 16, 16), 2 * ROWS), :] = direct[0] + direct[1]
    landed(xp.at[first], halo_s.at[0], halo_r.at[0])
    for k in range(4):
        landed(halo_in.at[k], halo_s.at[1 + k], halo_r.at[1 + k])
    begun = s > 0
    xp[first, :] = jnp.where(begun, xp[first, :].astype(F32), 0.0).astype(BF16)
    mp[h, first, :] = jnp.where(begun, halo_in[0].astype(F32) + halo_in[1].astype(F32), 0.0).astype(BF16)
    mp[n, first, :] = jnp.where(begun, halo_in[2].astype(F32) + halo_in[3].astype(F32), 0.0).astype(BF16)
    bodies(far, lambda row, count: conv_map(0, row, count))
    heads(conv_x, 0, 1)
    heads(lambda row, count: conv_map(0, row, count))

    state[...] = jnp.zeros_like(state)

    @pl.loop(0, 4)
    def _(b):
        rows = pl.ds(pl.multiple_of(b * BLOCK, BLOCK), BLOCK)
        turned = maps[0, rows, :].T
        b_t[:, rows] = turned
        entry[b] = state[...]
        state[...] = jnp.exp(-a_x[b][0:1]) * state[...] + jnp.dot(
            turned, xt[rows, :], preferred_element_type=F32
        )

    earlier = list(started)
    states[x] = state[...].astype(BF16)
    quarters = [pl.ds(128 * q, 128) for q in range(4)]
    for part, lanes in enumerate(quarters):
        for d in (1, 3, 2):
            ref = states.at[x, :, lanes]
            push(ref, ref, line_s.at[part * 3 + d - 1], line_r.at[part * 3 + d - 1], on_line[d - 1])

    bodies(far, lambda row, count: conv_map(1, row, count))
    heads(lambda row, count: conv_map(1, row, count))
    pair_lane = lax.broadcasted_iota(jnp.int32, (128, 128), 1)

    @pl.loop(0, 4)
    def _(b):
        start = pl.multiple_of(b * BLOCK, BLOCK)
        rows = pl.ds(start, BLOCK)
        aff[...] = jnp.dot(maps[1, rows, :], b_t[:, rows], preferred_element_type=F32)
        accum = rows_a[b]
        for t in (0, 1):
            reach = 128 * (t + 1)
            here = pl.ds(pl.multiple_of(start + 128 * t, 128), 128)
            near = pl.ds(start, reach)
            keep = (
                lax.broadcasted_iota(jnp.int32, (128, reach), 0) + 128 * t
                >= lax.broadcasted_iota(jnp.int32, (128, reach), 1)
            )
            column = cols[here, :]
            for j in range(4):
                lanes = slice(128 * j, 128 * j + 128)
                weights = [
                    jnp.where(
                        keep,
                        aff[128 * t : 128 * t + 128, 0:reach]
                        * jnp.exp(accum[i : i + 1, 0:reach] - column[:, i : i + 1]),
                        0.0,
                    ).astype(BF16)
                    for i in (2 * j, 2 * j + 1)
                ]
                both = jnp.dot(
                    jnp.concatenate(weights, axis=0), dtx[near, lanes], preferred_element_type=F32
                )
                yloc[here, lanes] = (
                    jnp.where(pair_lane < HEAD_DIM, both[0:128], both[128:256])
                    + skip_x[:, lanes] * xc[here, lanes].astype(F32)
                )

    for d in (1, 2, 3):
        index = (x + 4 - d) % 4
        landed(decays.at[index], line_s.at[11 + d], line_r.at[11 + d])
    for part, lanes in enumerate(quarters):
        for d in (1, 3, 2):
            landed(
                states.at[(x + 4 - d) % 4, :, lanes], line_s.at[part * 3 + d - 1], line_r.at[part * 3 + d - 1]
            )
        total = jnp.zeros((STATE, 128), F32)
        for j in range(4):
            total = jnp.exp(-decays[j, 0:1, lanes]) * total + states[j, :, lanes].astype(F32)
        t_out[:, lanes] = total.astype(BF16)
        push(t_out.at[:, lanes], t_in.at[:, lanes], t_s.at[part], t_r.at[part], across)
    sent(*earlier)
    for part, lanes in enumerate(quarters):
        total = jnp.zeros((STATE, 128), F32)
        passed = jnp.zeros((1, 128), F32)
        for j in range(4):
            taken = jnp.where(j < x, 1.0, 0.0)
            through = jnp.where(j < x, jnp.exp(-decays[j, 0:1, lanes]), 1.0)
            total = through * total + taken * states[j, :, lanes].astype(F32)
            passed = passed + taken * decays[j, 0:1, lanes]
        landed(t_in.at[:, lanes], t_s.at[part], t_r.at[part])
        state[:, lanes] = total + jnp.where(line == 1, jnp.exp(-passed), 0.0) * t_in[:, lanes].astype(F32)

    sent(*list(started))
    gain_r = gain[...].astype(F32).reshape(1, COLS)

    def gate(b, half):
        rows = pl.ds(pl.multiple_of(b * BLOCK + half * 128, 128), 128)
        ahead = sum(jnp.where(i < b, 1.0, 0.0) * a_x[i][0:1] for i in range(3))
        squares = jnp.zeros((128, 128), F32)
        column = cols[rows, :]
        for j in range(4):
            lanes = slice(128 * j, 128 * j + 128)
            entering = entry[b, :, lanes] + jnp.exp(-ahead[:, lanes]) * state[:, lanes]
            far_y = jnp.dot(maps[1, rows, :], entering.astype(BF16), preferred_element_type=F32)
            value = yloc[rows, lanes] + far_y * over_lanes(column, 3, j)
            value = value * silu(zs[rows, lanes].astype(F32))
            squares = squares + value * value
            g[rows, lanes] = (value * gain_r[:, lanes]).astype(BF16)
        buf[rows, pl.ds(D, 128)] = jnp.broadcast_to(
            jnp.sum(squares, axis=1, keepdims=True), (128, 128)
        ).astype(BF16)

    locals_[5].wait()
    reduce_stage(gate, g, w_o, out, buf, *reduce_refs)


def reduce_stage(
    gate, g, w_out, out, o, sib, zq, pa, pb, qa, qb, pf, qf, zp, sends, recvs
):
    s, y, h, c = place()
    up, down, far = (y + 1) % 4, (y + 3) % 4, (y + 2) % 4
    dev = lambda yy, hh, cc: (s, yy * 4 + hh * 2 + cc)
    dev_up, dev_down, dev_z, dev_sib = dev(up, h, c), dev(down, h, c), dev(y, 1 - h, c), dev(y, h, 1 - c)
    wide_q = WIDE - SPLIT
    part_p, part_q = (0, SPLIT), (SPLIT, wide_q)
    p_a, p_b = (0, HALF_P), (HALF_P, SPLIT - HALF_P)
    q_a, q_b = (SPLIT, HALF_Q), (SPLIT + HALF_Q, wide_q - HALF_Q)
    started = []

    def at(yy, hh, cc, cols):
        row = pl.multiple_of((yy * 4 + hh * 2 + cc) * ROWS, ROWS)
        return o.at[pl.ds(row, ROWS), pl.ds(cols[0], cols[1])]

    def copy_of(k, src, dst, to):
        return pltpu.make_async_remote_copy(
            src_ref=src, dst_ref=dst, send_sem=sends.at[k], recv_sem=recvs.at[k],
            device_id=to, device_id_type=MESH,
        )

    def send(k, src, dst, to):
        copy = copy_of(k, src, dst, to)
        copy.start()
        started.append(copy)
        return copy

    def arrive(k, ref):
        copy_of(k, ref, ref, dev_sib).wait_recv()

    def add(yy, hh, cols, ref):
        target = at(yy, hh, c, cols)

        @pl.loop(0, ROWS // 16)
        def _(i):
            rows = pl.ds(pl.multiple_of(i * 16, 16), 16)
            target[rows, :] = (target[rows, :].astype(F32) + ref[rows, :].astype(F32)).astype(BF16)

    def chip(yy, hh):
        return yy * 2 + hh

    def partial(yy, hh, k, cols=(0, WIDE)):
        row = pl.multiple_of((yy * 4 + hh * 2) * ROWS, 2 * ROWS)
        rows = pl.ds(row, 2 * ROWS)
        left = g[rows, :]
        low, high = cols[0], min(D, cols[0] + cols[1])
        pieces = -(-(high - low) // 1792)
        width = (high - low) // pieces
        for j in range(pieces):
            part = pl.ds(low + j * width, width)
            o[rows, part] = jnp.dot(left, w_out[:, part], preferred_element_type=F32).astype(BF16)
        send(k, at(yy, hh, 1 - c, cols), sib.at[chip(yy, hh), :, pl.ds(cols[0], cols[1])], dev_sib)

    def joined(yy, hh, k, cols=(0, WIDE)):
        ref = sib.at[chip(yy, hh), :, pl.ds(cols[0], cols[1])]
        arrive(k, ref)
        add(yy, hh, cols, ref)

    def in_q(cols):
        return pl.ds(cols[0] - SPLIT, cols[1])

    def in_p(cols):
        return pl.ds(cols[0], cols[1])

    n = 1 - h
    gate(far, n)
    partial(far, n, 0, p_a)
    partial(far, n, 32, p_b)
    partial(far, n, 31, part_q)
    gate(up, n)
    joined(far, n, 0, p_a)
    send(8, at(far, n, c, p_a), pa.at[n], dev_up)
    joined(far, n, 32, p_b)
    send(9, at(far, n, c, p_b), pb.at[n], dev_down)
    partial(up, n, 2)
    gate(down, n)
    joined(far, n, 31, part_q)
    send(10, at(far, n, c, part_q), zq.at[far], dev_z)
    partial(down, n, 3)
    joined(up, n, 2)
    send(11, at(up, n, c, p_b), pf.at[0, n, :, in_p(p_b)], dev_up)
    send(13, at(up, n, c, part_q), zq.at[up], dev_z)
    gate(far, h)
    partial(far, h, 1)
    joined(down, n, 3)
    send(12, at(down, n, c, p_a), pf.at[1, n, :, in_p(p_a)], dev_down)
    send(14, at(down, n, c, part_q), zq.at[down], dev_z)
    gate(up, h)
    partial(up, h, 4)
    joined(far, h, 1)
    arrive(8, pa.at[n])
    add(up, n, p_a, pa.at[n])
    send(15, at(up, n, c, p_a), pf.at[0, n, :, in_p(p_a)], dev_up)
    arrive(9, pb.at[n])
    add(down, n, p_b, pb.at[n])
    send(16, at(down, n, c, p_b), pf.at[1, n, :, in_p(p_b)], dev_down)
    send(17, at(far, h, c, p_a), pa.at[h], dev_up)
    send(18, at(far, h, c, p_b), pb.at[h], dev_down)
    gate(down, h)
    partial(down, h, 5)
    joined(up, h, 4)
    send(19, at(up, h, c, p_b), pf.at[0, h, :, in_p(p_b)], dev_up)
    gate(y, n)
    partial(y, n, 6)
    joined(down, h, 5)
    send(20, at(down, h, c, p_a), pf.at[1, h, :, in_p(p_a)], dev_down)
    gate(y, h)
    partial(y, h, 7)
    joined(y, n, 6)
    send(21, at(y, n, c, part_q), zq.at[y], dev_z)
    arrive(10, zq.at[far])
    add(far, h, part_q, zq.at[far])
    joined(y, h, 7)
    arrive(11, pf.at[0, n, :, in_p(p_b)])
    arrive(15, pf.at[0, n, :, in_p(p_a)])
    add(y, n, part_p, pf.at[0, n])
    arrive(12, pf.at[1, n, :, in_p(p_a)])
    arrive(16, pf.at[1, n, :, in_p(p_b)])
    add(y, n, part_p, pf.at[1, n])
    send(24, at(y, n, c, part_p), zp, dev_z)
    arrive(17, pa.at[h])
    add(up, h, p_a, pa.at[h])
    send(22, at(up, h, c, p_a), pf.at[0, h, :, in_p(p_a)], dev_up)
    arrive(18, pb.at[h])
    add(down, h, p_b, pb.at[h])
    send(23, at(down, h, c, p_b), pf.at[1, h, :, in_p(p_b)], dev_down)
    send(25, at(far, h, c, q_a), qa, dev_up)
    send(26, at(far, h, c, q_b), qb, dev_down)
    arrive(13, zq.at[up])
    add(up, h, part_q, zq.at[up])
    send(27, at(up, h, c, q_b), qf.at[0, :, in_q(q_b)], dev_up)
    arrive(14, zq.at[down])
    add(down, h, part_q, zq.at[down])
    send(28, at(down, h, c, q_a), qf.at[1, :, in_q(q_a)], dev_down)
    arrive(19, pf.at[0, h, :, in_p(p_b)])
    arrive(22, pf.at[0, h, :, in_p(p_a)])
    add(y, h, part_p, pf.at[0, h])
    arrive(20, pf.at[1, h, :, in_p(p_a)])
    arrive(23, pf.at[1, h, :, in_p(p_b)])
    add(y, h, part_p, pf.at[1, h])
    arrive(25, qa)
    add(up, h, q_a, qa)
    send(29, at(up, h, c, q_a), qf.at[0, :, in_q(q_a)], dev_up)
    arrive(26, qb)
    add(down, h, q_b, qb)
    send(30, at(down, h, c, q_b), qf.at[1, :, in_q(q_b)], dev_down)
    arrive(21, zq.at[y])
    add(y, h, part_q, zq.at[y])
    arrive(27, qf.at[0, :, in_q(q_b)])
    add(y, h, q_b, qf.at[0, :, in_q(q_b)])
    arrive(28, qf.at[1, :, in_q(q_a)])
    add(y, h, q_a, qf.at[1, :, in_q(q_a)])
    arrive(30, qf.at[1, :, in_q(q_b)])
    mine = at(y, h, c, (0, WIDE))
    squares = mine[:, D:WIDE].astype(F32) + qf[1, :, D - SPLIT : WIDE - SPLIT].astype(F32)
    scale = lax.rsqrt(squares / (COLS * 16) + 1e-05)

    def deliver(cols, other, begin):
        width = 256 if cols[1] % 512 else 512
        wide = jnp.concatenate([scale] * (width // 128), axis=1)

        @pl.loop(0, cols[1] // width)
        def _(j):
            here = pl.ds(pl.multiple_of(cols[0] + j * width, 128), width)
            total = mine[:, here].astype(F32)
            there = pl.ds(pl.multiple_of(cols[0] - begin + j * width, 128), width)
            total = total + other[:, there].astype(F32)
            out[:, here] = (total * wide).astype(BF16)

    deliver((q_b[0], D - q_b[0]), qf.at[1], SPLIT)
    arrive(29, qf.at[0, :, in_q(q_a)])
    deliver(q_a, qf.at[0], SPLIT)
    arrive(24, zp)
    deliver(part_p, zp, 0)
    for copy in started:
        copy.wait_send()


def mix(tokens, w_x, w_z, w_bc, w_dt, conv_x, conv_bc, dt_bias, decay_rate, skip, norm_gain, w_out):
    anywhere = pl.BlockSpec(memory_space=pl.ANY)
    vmem = pl.BlockSpec(memory_space=pltpu.VMEM)
    smem = pl.BlockSpec(memory_space=pltpu.SMEM)
    wide_q = WIDE - SPLIT
    dma = pltpu.SemaphoreType.DMA
    return pl.pallas_call(
        mixer_kernel,
        out_shape=jax.ShapeDtypeStruct((ROWS, D), BF16),
        in_specs=[anywhere] * 5 + [vmem, vmem, smem, smem, smem, vmem, anywhere],
        out_specs=vmem,
        scratch_shapes=[
            pltpu.VMEM((SPAN, WIDE), BF16),
            pltpu.VMEM((4, 2 * ROWS, 2 * COLS + 128), F32),
            pltpu.VMEM((D, 2 * COLS), BF16),
            pltpu.VMEM((D, 128), BF16),
            pltpu.VMEM((128, D), BF16),
            pltpu.VMEM((8, D), BF16),
            pltpu.VMEM((SPAN + 16, COLS), BF16),
            pltpu.VMEM((SPAN, COLS), BF16),
            pltpu.VMEM((SPAN, 128), F32),
            pltpu.VMEM((SPAN + 16, 128), BF16),
            pltpu.VMEM((SPAN + 16, 128), BF16),
            pltpu.VMEM((2, SPAN + 32, 128), BF16),
            pltpu.VMEM((2, 2 * ROWS, 128), BF16),
            pltpu.VMEM((4, 16, 128), BF16),
            pltpu.VMEM((2, SPAN, 128), BF16),
            pltpu.VMEM((STATE, SPAN), BF16),
            pltpu.VMEM((SPAN, COLS), BF16),
            pltpu.VMEM((SPAN, COLS), BF16),
            pltpu.VMEM((SPAN, COLS), BF16),
            pltpu.VMEM((SPAN, COLS), F32),
            pltpu.VMEM((SPAN, 128), F32),
            pltpu.VMEM((4, 8, BLOCK), F32),
            pltpu.VMEM((4, 8, COLS), F32),
            pltpu.VMEM((BLOCK, BLOCK), F32),
            pltpu.VMEM((4, STATE, COLS), F32),
            pltpu.VMEM((STATE, COLS), F32),
            pltpu.VMEM((4, STATE, COLS), BF16),
            pltpu.VMEM((4, 8, COLS), F32),
            pltpu.VMEM((STATE, COLS), BF16),
            pltpu.VMEM((STATE, COLS), BF16),
            dma((41,)), dma((41,)), dma((6,)), dma((9,)), dma((9,)), dma((9, 2)), dma((9, 2)),
            dma((5,)), dma((5,)), dma((15,)), dma((15,)), dma((4,)), dma((4,)),
            pltpu.VMEM((SPAN, COLS), BF16),
            pltpu.VMEM((COLS, D), BF16),
            pltpu.VMEM((8, ROWS, WIDE), BF16),
            pltpu.VMEM((4, ROWS, wide_q), BF16),
            pltpu.VMEM((2, ROWS, HALF_P), BF16),
            pltpu.VMEM((2, ROWS, SPLIT - HALF_P), BF16),
            pltpu.VMEM((ROWS, HALF_Q), BF16),
            pltpu.VMEM((ROWS, wide_q - HALF_Q), BF16),
            pltpu.VMEM((2, 2, ROWS, SPLIT), BF16),
            pltpu.VMEM((2, ROWS, wide_q), BF16),
            pltpu.VMEM((ROWS, SPLIT), BF16),
            pltpu.SemaphoreType.DMA((33,)),
            pltpu.SemaphoreType.DMA((33,)),
        ],
        compiler_params=pltpu.CompilerParams(
            collective_id=1, has_side_effects=True, vmem_limit_bytes=63 << 20
        ),
        name="mix",
    )(
        tokens, w_x, w_z, w_bc.T, w_dt.T, conv_x, conv_bc, dt_bias,
        decay_rate, skip, norm_gain, w_out,
    )


def on_device(
    tokens, w_x, w_z, w_bc, w_dt, conv_x, conv_bc, dt_bias, decay_rate, skip, norm_gain, w_out
):
    return mix(
        tokens, w_x, w_z, w_bc, w_dt, conv_x, conv_bc, dt_bias, decay_rate, skip, norm_gain, w_out
    )


def solution(mesh):
    placed = (
        P(("seq", "tp"), None),
        P(None, "tp"),
        P(None, "tp"),
        P(None, "tp"),
        P(None, "tp"),
        P(None, "tp"),
        P(None, "tp"),
        P("tp"),
        P("tp"),
        P("tp"),
        P("tp"),
        P("tp", None),
    )
    return jax.shard_map(
        on_device, mesh=mesh, in_specs=placed, out_specs=P(("seq", "tp"), None), check_vma=False
    )
```

```python
import jax
import jax.numpy as jnp
from jax import lax
from jax.experimental import pallas as pl
from jax.experimental.pallas import tpu as pltpu
from jax.sharding import PartitionSpec as P

HEAD_DIM = 64
STATE = 128
BLOCK = 256
MESH = pl.DeviceIdType.MESH
F32 = jnp.float32
BF16 = jnp.bfloat16

D = 6144
ROWS = 64
SPAN = 1024
COLS = 512
SPLIT = 3584
HALF_P = SPLIT // 2
HALF_Q = 1280
WIDE = D + 128
SPLIT_IN = 3584
HALF_P_IN = SPLIT_IN // 2
HALF_Q_IN = (D - SPLIT_IN) // 2


def place():
    tp = lax.axis_index("tp")
    return lax.axis_index("seq"), tp // 4, tp // 2 % 2, tp % 2


def greet(peers):
    barrier = pltpu.get_barrier_semaphore()
    for peer in peers:
        pl.semaphore_signal(barrier, inc=1, device_id=peer, device_id_type=MESH)
    pl.semaphore_wait(barrier, len(peers))


def silu(v):
    return v / (1.0 + jnp.exp(-v))


def mixer_kernel(
    tok, wx, wz, wbc, wdt, cx, cbc, bias, rate, skip, gain, w_out, out,
    buf, partials, w, w_small, st_w, st_dt, xp, zs, small, bco, bcs, mp, direct, halo_in, maps, b_t, xc, dtx, xt,
    yloc, cols, rows_a, a_x, aff, entry, state, states, decays, t_out, t_in,
    sends, recvs, locs, sib_s, sib_r, z_s, z_r, halo_s, halo_r, line_s, line_r, t_s, t_r,
    g, w_o, *reduce_refs,
):
    s, y, h, c = place()
    up, down, far = (y + 1) % 4, (y + 3) % 4, (y + 2) % 4
    n = 1 - h
    line, x = s // 4, s % 4
    dev = lambda yy, hh, cc: (s, yy * 4 + hh * 2 + cc)
    span = lambda ss, hh, cc: (ss, y * 4 + hh * 2 + cc)
    dev_up, dev_down, dev_z, dev_sib = dev(up, h, c), dev(down, h, c), dev(y, n, c), dev(y, h, 1 - c)
    dev_zsib = dev(y, n, 1 - c)
    later, before = (s + 1) % 8, (s + 7) % 8
    on_line = [span(line * 4 + (x + d) % 4, h, c) for d in (1, 2, 3)]
    across = span((1 - line) * 4 + x, h, c)
    part_p, part_q = (0, SPLIT_IN), (SPLIT_IN, D - SPLIT_IN)
    p_a, p_b = (0, HALF_P_IN), (HALF_P_IN, HALF_P_IN)
    q_a, q_b = (SPLIT_IN, HALF_Q_IN), (SPLIT_IN + HALF_Q_IN, HALF_Q_IN)
    whole = (0, D)
    p_one, p_two, p_rest = (0, 1280), (2304, 1280), (1280, 1024)
    rest_a, rest_b = (1280, 512), (1792, 512)

    def at(yy, hh, cc, cols_):
        row = pl.multiple_of((yy * 4 + hh * 2 + cc) * ROWS, ROWS)
        return buf.at[pl.ds(row, ROWS), pl.ds(cols_[0], cols_[1])]

    started = []

    def remote(src, dst, send_sem, recv_sem, to):
        return pltpu.make_async_remote_copy(
            src_ref=src, dst_ref=dst, send_sem=send_sem, recv_sem=recv_sem,
            device_id=to, device_id_type=MESH,
        )

    def push(src, dst, send_sem, recv_sem, to):
        copy = remote(src, dst, send_sem, recv_sem, to)
        copy.start()
        started.append(copy)
        return copy

    def sent(*copies):
        for copy in copies:
            copy.wait_send()
            started[:] = [other for other in started if other is not copy]

    def landed(ref, send_sem, recv_sem):
        remote(ref, ref, send_sem, recv_sem, dev_sib).wait_recv()

    def send(k, yy, hh, cols_, to, own=False):
        dst = at(yy, hh, c, cols_)
        src = tok.at[:, pl.ds(cols_[0], cols_[1])] if own else dst
        return push(src, dst, sends.at[k], recvs.at[k], to)

    def arrive(k, yy, hh, cols_, sib=False):
        landed(at(yy, hh, 1 - c if sib else c, cols_), sends.at[k], recvs.at[k])

    tall = pl.ds(pl.multiple_of(c * 64, 64), 64)
    locals_ = [
        pltpu.make_async_copy(tok, at(y, h, c, whole), locs.at[0]),
        pltpu.make_async_copy(wbc, st_w.at[tall], locs.at[1]),
        pltpu.make_async_copy(wdt, st_dt, locs.at[2]),
        pltpu.make_async_copy(wx, w.at[:, pl.ds(0, COLS)], locs.at[3]),
        pltpu.make_async_copy(wz, w.at[:, pl.ds(COLS, COLS)], locs.at[4]),
        pltpu.make_async_copy(w_out, w_o, locs.at[5]),
    ]
    st_w[...] = jnp.zeros_like(st_w)
    for copy in locals_:
        copy.start()
    greet(
        [dev_up, dev_down, dev_z, dev_sib, dev_zsib, across]
        + on_line
        + [span(later, hh, cc) for hh in (h, n) for cc in (c, 1 - c)]
        + [span(before, hh, cc) for hh in (h, n) for cc in (c, 1 - c)]
    )
    send(0, y, h, part_p, dev_z, own=True)
    send(1, y, h, part_q, dev_up, own=True)
    send(2, y, h, part_q, dev_down, own=True)
    send(3, y, h, whole, dev_sib, own=True)
    send(5, y, h, part_p, dev_up, own=True)
    send(6, y, h, part_p, dev_down, own=True)
    send(4, y, h, part_q, dev_z, own=True)

    units = [(y, h), (y, n), (down, h), (up, h), (down, n), (up, n), (far, h), (far, n)]

    def unit_row(k, flip=False):
        yy, hh = units[k]
        return pl.multiple_of((yy * 4 + (1 - hh if flip else hh) * 2) * ROWS, 2 * ROWS)

    def share(k, row, count):
        rows = pl.ds(row, count)
        push(bco.at[rows], bcs.at[rows], sib_s.at[k], sib_r.at[k], dev_sib)

    def merge(k):
        row = unit_row(k)
        rows = pl.ds(row, 2 * ROWS)
        landed(bcs.at[rows], sib_s.at[k], sib_r.at[k])
        mp[h, pl.ds(pl.multiple_of(row + 16, 16), 2 * ROWS), :] = bco[rows, :] + bcs[rows, :]
        half = pl.ds(pl.multiple_of(row + 16 + c * ROWS, 16), ROWS)
        push(mp.at[h, half], mp.at[h, half], z_s.at[k, 0], z_r.at[k, 0], dev_z)
        push(mp.at[h, half], mp.at[h, half], z_s.at[k, 1], z_r.at[k, 1], dev_zsib)

    def merged_there(k):
        row = unit_row(k, flip=True)
        for rel, core in ((0, c), (1, 1 - c)):
            ref = mp.at[n, pl.ds(pl.multiple_of(row + 16 + core * ROWS, 16), ROWS)]
            landed(ref, z_s.at[k, rel], z_r.at[k, rel])

    def project_small(k, cols_=(0, D), keep=None, add=None):
        row = unit_row(k)
        rows, inner = pl.ds(row, 2 * ROWS), pl.ds(cols_[0], cols_[1])
        part = jnp.dot(buf[rows, inner], w_small[inner, :], preferred_element_type=F32)
        if add is not None:
            part = part + partials[add, :, 2 * COLS : 2 * COLS + 128]
        if keep is not None:
            partials[keep, :, 2 * COLS : 2 * COLS + 128] = part
        else:
            small[rows, :] = part
            lane = lax.broadcasted_iota(jnp.int32, part.shape, 1)
            bco[rows, :] = jnp.where(lane // 64 == c, part, 0.0).astype(BF16)

    def project_wide(k, which, cols_=(0, D), keep=None, add=None):
        row = unit_row(k)
        rows, inner = pl.ds(row, 2 * ROWS), pl.ds(cols_[0], cols_[1])
        lanes = pl.ds(which * COLS, COLS)
        part = jnp.dot(buf[rows, inner], w[inner, lanes], preferred_element_type=F32)
        if add is not None:
            part = part + partials[add, :, lanes]
        if keep is not None:
            partials[keep, :, lanes] = part
        elif which == 0:
            xp[pl.ds(pl.multiple_of(row + 16, 16), 2 * ROWS), :] = part.astype(BF16)
        else:
            zs[rows, :] = part.astype(BF16)

    def project(k, cols_=(0, D), keep=None, add=None):
        project_small(k, cols_, keep, add)
        if keep is None:
            share(k, unit_row(k), 2 * ROWS)
        project_wide(k, 0, cols_, keep, add)
        project_wide(k, 1, cols_, keep, add)

    tap_rows = pl.ds(SPAN, 16)
    tap_own = pl.ds(SPAN + 16, 16)
    tap = jnp.concatenate([cbc[...].astype(F32), jnp.zeros((12, 64), F32)], axis=0)
    none = jnp.zeros_like(tap)
    bco[tap_rows, :] = jnp.where(
        c == 0, jnp.concatenate([tap, none], axis=1), jnp.concatenate([none, tap], axis=1)
    ).astype(BF16)
    share(8, SPAN, 16)

    head_lane = lax.broadcasted_iota(jnp.int32, (8, COLS), 1) // HEAD_DIM
    head_sub = lax.broadcasted_iota(jnp.int32, (8, COLS), 0)
    skip_x = sum(jnp.where(head_lane[0:1] == i, skip[i], 0.0) for i in range(8))
    sub256 = lax.broadcasted_iota(jnp.int32, (8, BLOCK), 0)
    bias_r = sum(jnp.where(sub256 == i, bias[i], 0.0) for i in range(8))
    rate_r = sum(jnp.where(sub256 == i, rate[i], 0.0) for i in range(8))

    deep = lax.broadcasted_iota(jnp.int32, (BLOCK, BLOCK), 0)
    summing = jnp.where(deep <= lax.broadcasted_iota(jnp.int32, (BLOCK, BLOCK), 1), 1.0, 0.0)

    def steps(b):
        rows = pl.ds(pl.multiple_of(b * BLOCK, BLOCK), BLOCK)
        turned = small[rows, :].T
        raw = jnp.where(c == 0, turned[64:72], turned[0:8]) + bias_r
        dt = jnp.maximum(raw, 0.0) + jnp.log1p(jnp.exp(-jnp.abs(raw)))
        accum = jnp.dot(
            dt * rate_r, summing, preferred_element_type=F32, precision=lax.Precision.HIGHEST
        )
        end = accum[:, BLOCK - 1 : BLOCK]
        stack = jnp.concatenate(
            [accum, dt, jnp.exp(accum - end) * dt, jnp.exp(-accum), jnp.zeros((96, BLOCK), F32)], axis=0
        )
        cols[rows, :] = stack.T
        rows_a[b] = accum
        total = jnp.sum(jnp.where(head_sub == head_lane, end, 0.0), axis=0, keepdims=True)
        a_x[b] = jnp.broadcast_to(total, (8, COLS))

    def convolve(src, row, lanes, taps, count):
        v = src[pl.ds(row, count + 16), lanes].astype(F32)
        acc = taps[0:1] * v[13 : 13 + count]
        for k in (1, 2, 3):
            acc = acc + taps[k : k + 1] * v[13 + k : 13 + k + count]
        return silu(acc).astype(BF16)

    def over_lanes(column, q, j):
        lane = lax.broadcasted_iota(jnp.int32, (column.shape[0], 128), 1)
        low = q * 8 + 2 * j
        return jnp.where(lane < HEAD_DIM, column[:, low : low + 1], column[:, low + 1 : low + 2])

    taps_x = cx[...].astype(F32)
    head_rows, body_rows = 16, 80

    def conv_x(row, count):
        rows = pl.ds(row, count)
        column = cols[rows, :]
        for j in range(4):
            lanes = slice(128 * j, 128 * j + 128)
            done = convolve(xp, row, lanes, taps_x[:, lanes], count)
            xc[rows, lanes] = done
            value = done.astype(F32)
            dtx[rows, lanes] = (value * over_lanes(column, 1, j)).astype(BF16)
            xt[rows, lanes] = (value * over_lanes(column, 2, j)).astype(BF16)

    def conv_map(index, row, count):
        taps = mp[index, tap_own, :][0:4].astype(F32)
        maps[index, pl.ds(row, count), :] = convolve(mp.at[index], row, slice(0, 128), taps, count)

    def bodies(b, one):
        @pl.loop(0, 3)
        def _(i):
            one(pl.multiple_of(b * BLOCK + 16 + i * body_rows, 16), body_rows)

    def heads(one, low=0, high=4):
        @pl.loop(low, high)
        def _(b):
            one(pl.multiple_of(b * BLOCK, BLOCK), head_rows)

    locals_[1].wait()
    locals_[2].wait()
    st_w[pl.ds(pl.multiple_of((1 - c) * 64, 64), 16), :] = (
        jnp.concatenate([st_dt[...].astype(F32), jnp.zeros((8, D), F32)], axis=0).astype(BF16)
    )

    @pl.loop(0, D // 128)
    def _(j):
        part = pl.ds(pl.multiple_of(j * 128, 128), 128)
        w_small[part, :] = st_w[:, part].T

    landed(bcs.at[tap_rows], sib_s.at[8], sib_r.at[8])
    mp[h, tap_own, :] = bco[tap_rows, :] + bcs[tap_rows, :]
    push(mp.at[h, tap_own], mp.at[h, tap_own], z_s.at[8, 0], z_r.at[8, 0], dev_z)
    locals_[0].wait()
    locals_[3].wait()
    locals_[4].wait()
    arrive(3, y, h, whole, sib=True)
    project(0)
    arrive(1, down, h, part_q)
    send(8, down, h, part_q, dev_z)
    send(9, down, h, part_q, dev_sib)
    arrive(2, up, h, part_q)
    send(11, up, h, part_q, dev_z)
    send(12, up, h, part_q, dev_sib)
    arrive(0, y, n, part_p)
    send(13, y, n, part_p, dev_up)
    send(14, y, n, part_p, dev_down)
    send(7, down, h, q_a, dev_up)
    send(10, up, h, q_b, dev_down)
    send(15, y, n, part_p, dev_sib)
    merge(0)
    arrive(9, down, h, part_q, sib=True)
    project(2, part_q, keep=2)
    arrive(12, up, h, part_q, sib=True)
    project(3, part_q, keep=3)
    arrive(15, y, n, part_p, sib=True)
    project(1, part_p, keep=0)
    arrive(4, y, n, part_q)
    send(16, y, n, part_q, dev_sib)
    arrive(5, down, h, part_p)
    send(21, down, h, p_a, dev_up)
    send(22, down, h, part_p, dev_sib)
    arrive(6, up, h, part_p)
    send(23, up, h, p_b, dev_down)
    send(24, up, h, part_p, dev_sib)
    arrive(16, y, n, part_q, sib=True)
    project(1, part_q, add=0)
    arrive(22, down, h, part_p, sib=True)
    project(2, part_p, add=2)
    arrive(24, up, h, part_p, sib=True)
    project(3, part_p, add=3)
    merge(1)
    steps(y)
    bodies(y, conv_x)
    merge(2)
    merge(3)
    arrive(8, down, n, part_q)
    send(25, down, n, part_q, dev_sib)
    arrive(13, down, n, part_p)
    send(27, down, n, p_one, dev_up)
    send(37, down, n, rest_a, dev_up)
    send(28, down, n, part_p, dev_sib)
    arrive(14, up, n, part_p)
    send(29, up, n, p_two, dev_down)
    send(38, up, n, rest_b, dev_down)
    send(30, up, n, part_p, dev_sib)
    arrive(25, down, n, part_q, sib=True)
    arrive(28, down, n, part_p, sib=True)
    project(4)
    arrive(7, far, h, q_a)
    send(17, far, h, q_a, dev_z)
    send(18, far, h, q_a, dev_sib)
    arrive(10, far, h, q_b)
    send(19, far, h, q_b, dev_z)
    send(20, far, h, q_b, dev_sib)
    arrive(30, up, n, part_p, sib=True)
    project(5, part_p, keep=0)
    arrive(11, up, n, part_q)
    send(26, up, n, part_q, dev_sib)
    merge(4)
    arrive(18, far, h, q_a, sib=True)
    arrive(20, far, h, q_b, sib=True)
    project(6, part_q, keep=1)
    arrive(21, far, h, p_a)
    send(33, far, h, p_a, dev_sib)
    arrive(23, far, h, p_b)
    send(34, far, h, p_b, dev_sib)
    arrive(26, up, n, part_q, sib=True)
    project(5, part_q, add=0)
    steps(down)
    bodies(down, conv_x)
    merge(5)
    arrive(17, far, n, q_a)
    send(31, far, n, q_a, dev_sib)
    arrive(33, far, h, p_a, sib=True)
    arrive(34, far, h, p_b, sib=True)
    project(6, part_p, add=1)
    arrive(19, far, n, q_b)
    send(32, far, n, q_b, dev_sib)
    steps(up)
    bodies(up, conv_x)
    merge(6)
    arrive(31, far, n, q_a, sib=True)
    arrive(32, far, n, q_b, sib=True)
    project(7, part_q, keep=1)
    arrive(27, far, n, p_one)
    send(35, far, n, p_one, dev_sib)
    arrive(29, far, n, p_two)
    send(36, far, n, p_two, dev_sib)
    landed(mp.at[n, tap_own], z_s.at[8, 0], z_r.at[8, 0])
    for k in range(6):
        merged_there(k)
    for b in (y, up, down):
        bodies(b, lambda row, count: conv_map(0, row, count))
    arrive(37, far, n, rest_a)
    send(39, far, n, rest_a, dev_sib)
    arrive(38, far, n, rest_b)
    send(40, far, n, rest_b, dev_sib)
    arrive(35, far, n, p_one, sib=True)
    project(7, p_one, keep=1, add=1)
    arrive(36, far, n, p_two, sib=True)
    project(7, p_two, keep=1, add=1)
    arrive(39, far, n, rest_a, sib=True)
    arrive(40, far, n, rest_b, sib=True)

    project_small(7, p_rest, add=1)
    unit = pl.ds(unit_row(7), 2 * ROWS)
    push(bco.at[unit], bcs.at[unit], sib_s.at[7], sib_r.at[7], dev_sib)
    push(bco.at[unit], direct.at[0], z_s.at[7, 0], z_r.at[7, 0], dev_z)
    push(bco.at[unit], direct.at[1], z_s.at[7, 1], z_r.at[7, 1], dev_zsib)
    ending = pl.ds(SPAN - 16, 16)
    for k, (hh, cc) in enumerate(((h, c), (h, 1 - c), (n, c), (n, 1 - c))):
        push(bco.at[ending], halo_in.at[k], halo_s.at[1 + k], halo_r.at[1 + k], span(later, hh, cc))
    project_wide(7, 0, p_rest, add=1)
    last, first = pl.ds(SPAN, 16), pl.ds(0, 16)
    push(xp.at[last], xp.at[first], halo_s.at[0], halo_r.at[0], span(later, h, c))
    steps(far)
    decays[x] = a_x[0] + a_x[1] + a_x[2] + a_x[3]
    for d in (1, 2, 3):
        push(decays.at[x], decays.at[x], line_s.at[11 + d], line_r.at[11 + d], on_line[d - 1])
    bodies(far, conv_x)
    heads(conv_x, 1, 4)
    project_wide(7, 1, p_rest, add=1)
    for b in (y, up, down):
        bodies(b, lambda row, count: conv_map(1, row, count))
    merged_there(6)
    landed(bcs.at[unit], sib_s.at[7], sib_r.at[7])
    mp[h, pl.ds(pl.multiple_of(unit_row(7) + 16, 16), 2 * ROWS), :] = bco[unit, :] + bcs[unit, :]
    landed(direct.at[0], z_s.at[7, 0], z_r.at[7, 0])
    landed(direct.at[1], z_s.at[7, 1], z_r.at[7, 1])
    mp[n, pl.ds(pl.multiple_of(unit_row(7, flip=True) + 16, 16), 2 * ROWS), :] = direct[0] + direct[1]
    landed(xp.at[first], halo_s.at[0], halo_r.at[0])
    for k in range(4):
        landed(halo_in.at[k], halo_s.at[1 + k], halo_r.at[1 + k])
    begun = s > 0
    xp[first, :] = jnp.where(begun, xp[first, :].astype(F32), 0.0).astype(BF16)
    mp[h, first, :] = jnp.where(begun, halo_in[0].astype(F32) + halo_in[1].astype(F32), 0.0).astype(BF16)
    mp[n, first, :] = jnp.where(begun, halo_in[2].astype(F32) + halo_in[3].astype(F32), 0.0).astype(BF16)
    bodies(far, lambda row, count: conv_map(0, row, count))
    heads(conv_x, 0, 1)
    heads(lambda row, count: conv_map(0, row, count))

    state[...] = jnp.zeros_like(state)

    @pl.loop(0, 4)
    def _(b):
        rows = pl.ds(pl.multiple_of(b * BLOCK, BLOCK), BLOCK)
        turned = maps[0, rows, :].T
        b_t[:, rows] = turned
        entry[b] = state[...]
        state[...] = jnp.exp(-a_x[b][0:1]) * state[...] + jnp.dot(
            turned, xt[rows, :], preferred_element_type=F32
        )

    earlier = list(started)
    states[x] = state[...].astype(BF16)
    quarters = [pl.ds(128 * q, 128) for q in range(4)]
    for part, lanes in enumerate(quarters):
        for d in (1, 3, 2):
            ref = states.at[x, :, lanes]
            push(ref, ref, line_s.at[part * 3 + d - 1], line_r.at[part * 3 + d - 1], on_line[d - 1])

    bodies(far, lambda row, count: conv_map(1, row, count))
    heads(lambda row, count: conv_map(1, row, count))
    pair_lane = lax.broadcasted_iota(jnp.int32, (128, 128), 1)

    @pl.loop(0, 4)
    def _(b):
        start = pl.multiple_of(b * BLOCK, BLOCK)
        rows = pl.ds(start, BLOCK)
        aff[...] = jnp.dot(maps[1, rows, :], b_t[:, rows], preferred_element_type=F32)
        accum = rows_a[b]
        for t in (0, 1):
            reach = 128 * (t + 1)
            here = pl.ds(pl.multiple_of(start + 128 * t, 128), 128)
            near = pl.ds(start, reach)
            keep = (
                lax.broadcasted_iota(jnp.int32, (128, reach), 0) + 128 * t
                >= lax.broadcasted_iota(jnp.int32, (128, reach), 1)
            )
            column = cols[here, :]
            for j in range(4):
                lanes = slice(128 * j, 128 * j + 128)
                weights = [
                    jnp.where(
                        keep,
                        aff[128 * t : 128 * t + 128, 0:reach]
                        * jnp.exp(accum[i : i + 1, 0:reach] - column[:, i : i + 1]),
                        0.0,
                    ).astype(BF16)
                    for i in (2 * j, 2 * j + 1)
                ]
                both = jnp.dot(
                    jnp.concatenate(weights, axis=0), dtx[near, lanes], preferred_element_type=F32
                )
                yloc[here, lanes] = (
                    jnp.where(pair_lane < HEAD_DIM, both[0:128], both[128:256])
                    + skip_x[:, lanes] * xc[here, lanes].astype(F32)
                )

    for d in (1, 2, 3):
        index = (x + 4 - d) % 4
        landed(decays.at[index], line_s.at[11 + d], line_r.at[11 + d])
    for part, lanes in enumerate(quarters):
        for d in (1, 3, 2):
            landed(
                states.at[(x + 4 - d) % 4, :, lanes], line_s.at[part * 3 + d - 1], line_r.at[part * 3 + d - 1]
            )
        total = jnp.zeros((STATE, 128), F32)
        for j in range(4):
            total = jnp.exp(-decays[j, 0:1, lanes]) * total + states[j, :, lanes].astype(F32)
        t_out[:, lanes] = total.astype(BF16)
        push(t_out.at[:, lanes], t_in.at[:, lanes], t_s.at[part], t_r.at[part], across)
    sent(*earlier)
    for part, lanes in enumerate(quarters):
        total = jnp.zeros((STATE, 128), F32)
        passed = jnp.zeros((1, 128), F32)
        for j in range(4):
            taken = jnp.where(j < x, 1.0, 0.0)
            through = jnp.where(j < x, jnp.exp(-decays[j, 0:1, lanes]), 1.0)
            total = through * total + taken * states[j, :, lanes].astype(F32)
            passed = passed + taken * decays[j, 0:1, lanes]
        landed(t_in.at[:, lanes], t_s.at[part], t_r.at[part])
        state[:, lanes] = total + jnp.where(line == 1, jnp.exp(-passed), 0.0) * t_in[:, lanes].astype(F32)

    sent(*list(started))
    gain_r = gain[...].astype(F32).reshape(1, COLS)

    def gate(b, half):
        rows = pl.ds(pl.multiple_of(b * BLOCK + half * 128, 128), 128)
        ahead = sum(jnp.where(i < b, 1.0, 0.0) * a_x[i][0:1] for i in range(3))
        squares = jnp.zeros((128, 128), F32)
        column = cols[rows, :]
        for j in range(4):
            lanes = slice(128 * j, 128 * j + 128)
            entering = entry[b, :, lanes] + jnp.exp(-ahead[:, lanes]) * state[:, lanes]
            far_y = jnp.dot(maps[1, rows, :], entering.astype(BF16), preferred_element_type=F32)
            value = yloc[rows, lanes] + far_y * over_lanes(column, 3, j)
            value = value * silu(zs[rows, lanes].astype(F32))
            squares = squares + value * value
            g[rows, lanes] = (value * gain_r[:, lanes]).astype(BF16)
        buf[rows, pl.ds(D, 128)] = jnp.broadcast_to(
            jnp.sum(squares, axis=1, keepdims=True), (128, 128)
        ).astype(BF16)

    locals_[5].wait()
    reduce_stage(gate, g, w_o, out, buf, *reduce_refs)


def reduce_stage(
    gate, g, w_out, out, o, sib, zq, pa, pb, qa, qb, pf, qf, zp, sends, recvs
):
    s, y, h, c = place()
    up, down, far = (y + 1) % 4, (y + 3) % 4, (y + 2) % 4
    dev = lambda yy, hh, cc: (s, yy * 4 + hh * 2 + cc)
    dev_up, dev_down, dev_z, dev_sib = dev(up, h, c), dev(down, h, c), dev(y, 1 - h, c), dev(y, h, 1 - c)
    wide_q = WIDE - SPLIT
    part_p, part_q = (0, SPLIT), (SPLIT, wide_q)
    p_a, p_b = (0, HALF_P), (HALF_P, SPLIT - HALF_P)
    q_a, q_b = (SPLIT, HALF_Q), (SPLIT + HALF_Q, wide_q - HALF_Q)
    started = []

    def at(yy, hh, cc, cols):
        row = pl.multiple_of((yy * 4 + hh * 2 + cc) * ROWS, ROWS)
        return o.at[pl.ds(row, ROWS), pl.ds(cols[0], cols[1])]

    def copy_of(k, src, dst, to):
        return pltpu.make_async_remote_copy(
            src_ref=src, dst_ref=dst, send_sem=sends.at[k], recv_sem=recvs.at[k],
            device_id=to, device_id_type=MESH,
        )

    def send(k, src, dst, to):
        copy = copy_of(k, src, dst, to)
        copy.start()
        started.append(copy)
        return copy

    def arrive(k, ref):
        copy_of(k, ref, ref, dev_sib).wait_recv()

    def add(yy, hh, cols, ref):
        target = at(yy, hh, c, cols)

        @pl.loop(0, ROWS // 16)
        def _(i):
            rows = pl.ds(pl.multiple_of(i * 16, 16), 16)
            target[rows, :] = (target[rows, :].astype(F32) + ref[rows, :].astype(F32)).astype(BF16)

    def chip(yy, hh):
        return yy * 2 + hh

    def partial(yy, hh, k, cols=(0, WIDE)):
        row = pl.multiple_of((yy * 4 + hh * 2) * ROWS, 2 * ROWS)
        rows = pl.ds(row, 2 * ROWS)
        left = g[rows, :]
        low, high = cols[0], min(D, cols[0] + cols[1])
        pieces = -(-(high - low) // 1792)
        width = (high - low) // pieces
        for j in range(pieces):
            part = pl.ds(low + j * width, width)
            o[rows, part] = jnp.dot(left, w_out[:, part], preferred_element_type=F32).astype(BF16)
        send(k, at(yy, hh, 1 - c, cols), sib.at[chip(yy, hh), :, pl.ds(cols[0], cols[1])], dev_sib)

    def joined(yy, hh, k, cols=(0, WIDE)):
        ref = sib.at[chip(yy, hh), :, pl.ds(cols[0], cols[1])]
        arrive(k, ref)
        add(yy, hh, cols, ref)

    def in_q(cols):
        return pl.ds(cols[0] - SPLIT, cols[1])

    def in_p(cols):
        return pl.ds(cols[0], cols[1])

    n = 1 - h
    gate(far, n)
    partial(far, n, 0, p_a)
    partial(far, n, 32, p_b)
    partial(far, n, 31, part_q)
    gate(up, n)
    joined(far, n, 0, p_a)
    send(8, at(far, n, c, p_a), pa.at[n], dev_up)
    joined(far, n, 32, p_b)
    send(9, at(far, n, c, p_b), pb.at[n], dev_down)
    partial(up, n, 2)
    gate(down, n)
    joined(far, n, 31, part_q)
    send(10, at(far, n, c, part_q), zq.at[far], dev_z)
    partial(down, n, 3)
    joined(up, n, 2)
    send(11, at(up, n, c, p_b), pf.at[0, n, :, in_p(p_b)], dev_up)
    send(13, at(up, n, c, part_q), zq.at[up], dev_z)
    gate(far, h)
    partial(far, h, 1)
    joined(down, n, 3)
    send(12, at(down, n, c, p_a), pf.at[1, n, :, in_p(p_a)], dev_down)
    send(14, at(down, n, c, part_q), zq.at[down], dev_z)
    gate(up, h)
    partial(up, h, 4)
    joined(far, h, 1)
    arrive(8, pa.at[n])
    add(up, n, p_a, pa.at[n])
    send(15, at(up, n, c, p_a), pf.at[0, n, :, in_p(p_a)], dev_up)
    arrive(9, pb.at[n])
    add(down, n, p_b, pb.at[n])
    send(16, at(down, n, c, p_b), pf.at[1, n, :, in_p(p_b)], dev_down)
    send(17, at(far, h, c, p_a), pa.at[h], dev_up)
    send(18, at(far, h, c, p_b), pb.at[h], dev_down)
    gate(down, h)
    partial(down, h, 5)
    joined(up, h, 4)
    send(19, at(up, h, c, p_b), pf.at[0, h, :, in_p(p_b)], dev_up)
    gate(y, n)
    partial(y, n, 6)
    joined(down, h, 5)
    send(20, at(down, h, c, p_a), pf.at[1, h, :, in_p(p_a)], dev_down)
    gate(y, h)
    partial(y, h, 7)
    joined(y, n, 6)
    send(21, at(y, n, c, part_q), zq.at[y], dev_z)
    arrive(10, zq.at[far])
    add(far, h, part_q, zq.at[far])
    joined(y, h, 7)
    arrive(11, pf.at[0, n, :, in_p(p_b)])
    arrive(15, pf.at[0, n, :, in_p(p_a)])
    add(y, n, part_p, pf.at[0, n])
    arrive(12, pf.at[1, n, :, in_p(p_a)])
    arrive(16, pf.at[1, n, :, in_p(p_b)])
    add(y, n, part_p, pf.at[1, n])
    send(24, at(y, n, c, part_p), zp, dev_z)
    arrive(17, pa.at[h])
    add(up, h, p_a, pa.at[h])
    send(22, at(up, h, c, p_a), pf.at[0, h, :, in_p(p_a)], dev_up)
    arrive(18, pb.at[h])
    add(down, h, p_b, pb.at[h])
    send(23, at(down, h, c, p_b), pf.at[1, h, :, in_p(p_b)], dev_down)
    send(25, at(far, h, c, q_a), qa, dev_up)
    send(26, at(far, h, c, q_b), qb, dev_down)
    arrive(13, zq.at[up])
    add(up, h, part_q, zq.at[up])
    send(27, at(up, h, c, q_b), qf.at[0, :, in_q(q_b)], dev_up)
    arrive(14, zq.at[down])
    add(down, h, part_q, zq.at[down])
    send(28, at(down, h, c, q_a), qf.at[1, :, in_q(q_a)], dev_down)
    arrive(19, pf.at[0, h, :, in_p(p_b)])
    arrive(22, pf.at[0, h, :, in_p(p_a)])
    add(y, h, part_p, pf.at[0, h])
    arrive(20, pf.at[1, h, :, in_p(p_a)])
    arrive(23, pf.at[1, h, :, in_p(p_b)])
    add(y, h, part_p, pf.at[1, h])
    arrive(25, qa)
    add(up, h, q_a, qa)
    send(29, at(up, h, c, q_a), qf.at[0, :, in_q(q_a)], dev_up)
    arrive(26, qb)
    add(down, h, q_b, qb)
    send(30, at(down, h, c, q_b), qf.at[1, :, in_q(q_b)], dev_down)
    arrive(21, zq.at[y])
    add(y, h, part_q, zq.at[y])
    arrive(27, qf.at[0, :, in_q(q_b)])
    add(y, h, q_b, qf.at[0, :, in_q(q_b)])
    arrive(28, qf.at[1, :, in_q(q_a)])
    add(y, h, q_a, qf.at[1, :, in_q(q_a)])
    arrive(30, qf.at[1, :, in_q(q_b)])
    mine = at(y, h, c, (0, WIDE))
    squares = mine[:, D:WIDE].astype(F32) + qf[1, :, D - SPLIT : WIDE - SPLIT].astype(F32)
    scale = lax.rsqrt(squares / (COLS * 16) + 1e-05)

    def deliver(cols, other, begin):
        width = 256 if cols[1] % 512 else 512
        wide = jnp.concatenate([scale] * (width // 128), axis=1)

        @pl.loop(0, cols[1] // width)
        def _(j):
            here = pl.ds(pl.multiple_of(cols[0] + j * width, 128), width)
            total = mine[:, here].astype(F32)
            there = pl.ds(pl.multiple_of(cols[0] - begin + j * width, 128), width)
            total = total + other[:, there].astype(F32)
            out[:, here] = (total * wide).astype(BF16)

    deliver((q_b[0], D - q_b[0]), qf.at[1], SPLIT)
    arrive(29, qf.at[0, :, in_q(q_a)])
    deliver(q_a, qf.at[0], SPLIT)
    arrive(24, zp)
    deliver(part_p, zp, 0)
    for copy in started:
        copy.wait_send()


def mix(tokens, w_x, w_z, w_bc, w_dt, conv_x, conv_bc, dt_bias, decay_rate, skip, norm_gain, w_out):
    anywhere = pl.BlockSpec(memory_space=pl.ANY)
    vmem = pl.BlockSpec(memory_space=pltpu.VMEM)
    smem = pl.BlockSpec(memory_space=pltpu.SMEM)
    wide_q = WIDE - SPLIT
    dma = pltpu.SemaphoreType.DMA
    return pl.pallas_call(
        mixer_kernel,
        out_shape=jax.ShapeDtypeStruct((ROWS, D), BF16),
        in_specs=[anywhere] * 5 + [vmem, vmem, smem, smem, smem, vmem, anywhere],
        out_specs=vmem,
        scratch_shapes=[
            pltpu.VMEM((SPAN, WIDE), BF16),
            pltpu.VMEM((4, 2 * ROWS, 2 * COLS + 128), F32),
            pltpu.VMEM((D, 2 * COLS), BF16),
            pltpu.VMEM((D, 128), BF16),
            pltpu.VMEM((128, D), BF16),
            pltpu.VMEM((8, D), BF16),
            pltpu.VMEM((SPAN + 16, COLS), BF16),
            pltpu.VMEM((SPAN, COLS), BF16),
            pltpu.VMEM((SPAN, 128), F32),
            pltpu.VMEM((SPAN + 16, 128), BF16),
            pltpu.VMEM((SPAN + 16, 128), BF16),
            pltpu.VMEM((2, SPAN + 32, 128), BF16),
            pltpu.VMEM((2, 2 * ROWS, 128), BF16),
            pltpu.VMEM((4, 16, 128), BF16),
            pltpu.VMEM((2, SPAN, 128), BF16),
            pltpu.VMEM((STATE, SPAN), BF16),
            pltpu.VMEM((SPAN, COLS), BF16),
            pltpu.VMEM((SPAN, COLS), BF16),
            pltpu.VMEM((SPAN, COLS), BF16),
            pltpu.VMEM((SPAN, COLS), F32),
            pltpu.VMEM((SPAN, 128), F32),
            pltpu.VMEM((4, 8, BLOCK), F32),
            pltpu.VMEM((4, 8, COLS), F32),
            pltpu.VMEM((BLOCK, BLOCK), F32),
            pltpu.VMEM((4, STATE, COLS), F32),
            pltpu.VMEM((STATE, COLS), F32),
            pltpu.VMEM((4, STATE, COLS), BF16),
            pltpu.VMEM((4, 8, COLS), F32),
            pltpu.VMEM((STATE, COLS), BF16),
            pltpu.VMEM((STATE, COLS), BF16),
            dma((41,)), dma((41,)), dma((6,)), dma((9,)), dma((9,)), dma((9, 2)), dma((9, 2)),
            dma((5,)), dma((5,)), dma((15,)), dma((15,)), dma((4,)), dma((4,)),
            pltpu.VMEM((SPAN, COLS), BF16),
            pltpu.VMEM((COLS, D), BF16),
            pltpu.VMEM((8, ROWS, WIDE), BF16),
            pltpu.VMEM((4, ROWS, wide_q), BF16),
            pltpu.VMEM((2, ROWS, HALF_P), BF16),
            pltpu.VMEM((2, ROWS, SPLIT - HALF_P), BF16),
            pltpu.VMEM((ROWS, HALF_Q), BF16),
            pltpu.VMEM((ROWS, wide_q - HALF_Q), BF16),
            pltpu.VMEM((2, 2, ROWS, SPLIT), BF16),
            pltpu.VMEM((2, ROWS, wide_q), BF16),
            pltpu.VMEM((ROWS, SPLIT), BF16),
            pltpu.SemaphoreType.DMA((33,)),
            pltpu.SemaphoreType.DMA((33,)),
        ],
        compiler_params=pltpu.CompilerParams(
            collective_id=1, has_side_effects=True, vmem_limit_bytes=63 << 20
        ),
        name="mix",
    )(
        tokens, w_x, w_z, w_bc.T, w_dt.T, conv_x, conv_bc, dt_bias,
        decay_rate, skip, norm_gain, w_out,
    )


def on_device(
    tokens, w_x, w_z, w_bc, w_dt, conv_x, conv_bc, dt_bias, decay_rate, skip, norm_gain, w_out
):
    return mix(
        tokens, w_x, w_z, w_bc, w_dt, conv_x, conv_bc, dt_bias, decay_rate, skip, norm_gain, w_out
    )


def solution(mesh):
    placed = (
        P(("seq", "tp"), None),
        P(None, "tp"),
        P(None, "tp"),
        P(None, "tp"),
        P(None, "tp"),
        P(None, "tp"),
        P(None, "tp"),
        P("tp"),
        P("tp"),
        P("tp"),
        P("tp"),
        P("tp", None),
    )
    return jax.shard_map(
        on_device, mesh=mesh, in_specs=placed, out_specs=P(("seq", "tp"), None), check_vma=False
    )
```
